32 devices in a mesh: seq: 8 (over z, y), head: 4 (over x, core).
Axes of the slice: x: 2, y: 2, z: 4, core: 2. Of those that a mesh axis runs over, the one named last changes fastest.
Arguments:
- x_quant: bfloat16 [1024, 8192], P('seq', 'head'), may hold values from -6 to 6
- scale_exp: int32 [64, 1024], P('head', 'seq'), may hold values from -2 to 1
- dt_raw: bfloat16 [128, 1024], P('head', 'seq'), may hold values from -5 to 5
- dt_bias: float32 [128], P('head'), may hold values from -3 to -1
- a_log: float32 [128], P('head')
- skip_weight: float32 [128], P('head'), may hold values from 0.5 to 1.5
- b_proj: bfloat16 [1024, 128], P('seq'), may hold values from -4 to 4
- c_proj: bfloat16 [1024, 128], P('seq'), may hold values from -0.5 to 0.5
- doc_starts: int32 [8, 2], P('seq'), may hold values from 0 to 128, as said below
- grad_out: bfloat16 [1024, 8192], P('seq', 'head'), may hold values from -6 to 6
Outputs:
- grad_x: bfloat16 [1024, 8192], P('seq', 'head')
- grad_dt: float32 [128, 1024], P('head', 'seq')
- grad_bc: float32 [2, 1024, 128], P(None, 'seq')
- head_grads: float32 [2, 128], P(None, 'head')
The draws below stay inside these ranges and needn't reach their ends.
Inputs may be any that keep to these rules, and one draw needn't show every extreme that they name: `doc_starts`: each entry is the offset within its slab of 128 tokens of a token that begins a document, or 128 for an unused entry; a slab's entries are in no order and may repeat.
All inputs are finite; a program needn't handle non-finite values.
Results may differ from the reference program's by a relative error of at most 0.0024.
Values sent between devices are 32-bit elements; how exact they have to be, the bound alone decides.
A program may use at most 128 MiB of HBM per device.

```python
import math
import jax
import jax.numpy as jnp
from jax import lax

HEADS = 128
HEAD_DIM = 64
STATE = 128
SPAN = 256
SLOTS = 2
TOK_DEV = 128
SLABS = 8
TOKENS = 1024


def draw_a_log(key, part):
    key = jax.random.fold_in(key, 11)
    key_kind, key_pos = jax.random.split(key)
    slow_heads = jax.random.uniform(key_kind, (HEADS,)) < 0.5
    spread = jax.random.uniform(key_pos, (HEADS,), jnp.float32)
    slow_low = math.log(1.0 / (8.0 * TOKENS))
    slow_high = math.log(2.0 / TOKENS)
    fast_high = math.log(1.0 / 30.0)
    log_rate = jnp.where(slow_heads, slow_low + spread * (slow_high - slow_low), slow_high + spread * (fast_high - slow_high))
    return (log_rate - math.log(0.17)).astype(jnp.float32)


def draw_doc_starts(key, part):
    key = jax.random.fold_in(key, 23)
    key_off, key_keep, key_pick = jax.random.split(key, 3)
    offsets = jax.random.randint(key_off, (SLABS, SLOTS), 0, TOK_DEV)
    keeping = jax.random.randint(key_keep, (SLABS, SLOTS), 0, 16) == 0
    picked = jax.random.randint(key_pick, (), 0, SLABS)
    row_ids = jnp.arange(SLABS, dtype=jnp.int32)[:, None]
    col_ids = jnp.arange(SLOTS, dtype=jnp.int32)[None, :]
    values = jnp.where(keeping, offsets, TOK_DEV)
    values = jnp.where((row_ids == picked) & (col_ids == 0), 0, values)
    values = jnp.where((row_ids == (picked + 1) % SLABS) & (col_ids == SLOTS - 1), TOK_DEV, values)
    return values.astype(jnp.int32)


def plant(drawn, stream_key, low, largest):
    place = [jax.random.randint(jax.random.fold_in(stream_key, axis), (), 0, length) for axis, length in enumerate(drawn.shape)]
    main_axis = drawn.shape.index(max(drawn.shape))
    next_to = place[:main_axis] + [(place[main_axis] + 1) % drawn.shape[main_axis]] + place[main_axis + 1:]
    return drawn.at[tuple(place)].set(low).at[tuple(next_to)].set(largest)


def levels(key, extent, cuts, low, top_value):
    factor_of = 1.0
    for dim, shards_of in cuts:
        steps = jax.random.uniform(jax.random.fold_in(jax.random.fold_in(key, 6), dim), (shards_of,), jnp.float32, low / len(cuts), top_value / len(cuts))
        factor_of = factor_of * jnp.repeat(jnp.exp(steps), extent[dim] // shards_of).reshape((-1,) + (1,) * (len(extent) - 1 - dim))
    return factor_of


def normal_values(key, extent, width, reach, shards=(), held_as=jnp.bfloat16):
    factor_of = levels(key, extent, shards, -0.22, 0.18) if shards else 1.0
    values = jax.random.normal(key, extent, jnp.float32) * width * factor_of
    return jnp.minimum(jnp.maximum(values, -reach), reach).astype(held_as)


def setup_inputs(seed: int = 0) -> dict:
    seeds = jax.random.split(jax.random.key(seed), 11)
    x_quant = normal_values(seeds[0], (TOKENS, HEADS * HEAD_DIM), 1.0, 6.0, ((0, 8), (1, 4)))
    scale_exp = plant(jax.random.randint(seeds[1], (HEADS * HEAD_DIM // 128, TOKENS), -2, 2), jax.random.fold_in(seeds[1], 1), -2, 1).astype(jnp.int32)
    dt_raw = normal_values(seeds[2], (HEADS, TOKENS), 1.0, 5.0, ((0, 4), (1, 8)))
    dt_bias = jnp.clip(-3.0 + 2.0 * jax.random.uniform(seeds[3], (HEADS,), jnp.float32) ** levels(seeds[3], (HEADS,), ((0, 4),), -0.2, 0.2), -3.0, -1.0)
    a_log = draw_a_log(jax.random.fold_in(seeds[10], 71), 0)
    skip_weight = jnp.clip(0.5 + 1.0 * jax.random.uniform(seeds[5], (HEADS,), jnp.float32) ** levels(seeds[5], (HEADS,), ((0, 4),), -0.2, 0.2), 0.5, 1.5)
    b_proj = normal_values(seeds[6], (TOKENS, STATE), 0.25, 4.0, ((0, 8),))
    c_proj = normal_values(seeds[7], (TOKENS, STATE), STATE ** -0.5, 0.5, ((0, 8),))
    doc_starts = draw_doc_starts(jax.random.fold_in(seeds[10], 71), 0)
    grad_out = normal_values(seeds[9], (TOKENS, HEADS * HEAD_DIM), 1.0, 6.0, ((0, 8), (1, 4)))
    return dict(x_quant=x_quant, scale_exp=scale_exp, dt_raw=dt_raw, dt_bias=dt_bias, a_log=a_log, skip_weight=skip_weight, b_proj=b_proj, c_proj=c_proj, doc_starts=doc_starts, grad_out=grad_out)


def block_step(carry, inputs, skip_vec, block_len):
    carried, running = carry
    x_block, step_block, decay_block, b_block, c_block, reset_block, grad_block = inputs
    cumulative = jnp.cumsum(decay_block, axis=1)
    segment = jnp.cumsum(reset_block)
    index_row = jnp.arange(block_len, dtype=jnp.int32)
    same_doc = (index_row[:, None] >= index_row[None, :]) & (segment[:, None] == segment[None, :])
    log_gap = cumulative[:, :, None] - cumulative[:, None, :]
    decay_mat = jnp.exp(jnp.where(same_doc[None], log_gap, -1e+30))
    kernel = jnp.dot(c_block, b_block.T, precision=lax.Precision.HIGHEST)
    scaled_input = x_block * step_block[:, :, None]
    first_doc = (segment == 0.0).astype(cumulative.dtype)
    last_doc = (segment == segment[-1]).astype(cumulative.dtype)
    enter_decay = jnp.exp(cumulative) * first_doc
    within = jnp.einsum('hts,hsp->htp', decay_mat * kernel[None], scaled_input, precision=lax.Precision.HIGHEST)
    state_read = jnp.einsum('hpn,tn->htp', carried, c_block, precision=lax.Precision.HIGHEST)
    mixer = within + enter_decay[:, :, None] * state_read + skip_vec[:, None, None] * x_block
    running = running + jnp.sum(grad_block * mixer)
    exit_decay = jnp.exp(cumulative[:, -1:] - cumulative) * last_doc
    slab_decay = jnp.exp(cumulative[:, -1]) * first_doc[-1]
    carried = slab_decay[:, None, None] * carried + jnp.einsum('hsp,sn->hpn', exit_decay[:, :, None] * scaled_input, b_block, precision=lax.Precision.HIGHEST)
    return ((carried, running), None)

def partial_step(skip_vec, block_len):

    def stepper(carry, inputs):
        return block_step(carry, inputs, skip_vec, block_len)
    return stepper

def reference(x_quant, scale_exp, dt_raw, dt_bias, a_log, skip_weight, b_proj, c_proj, doc_starts, grad_out):
    channels = HEADS * HEAD_DIM
    factor = jnp.left_shift(jnp.int32(1), scale_exp + 8).astype(jnp.float32) / 256.0
    x_vals = (x_quant.astype(jnp.float32).reshape(TOKENS, channels // 128, 128) * factor.T[:, :, None]).reshape(TOKENS, channels).astype(jnp.bfloat16)
    position = jnp.arange(TOKENS, dtype=jnp.int32)
    offsets = position % TOK_DEV
    slab_rows = doc_starts[position // TOK_DEV]
    resets = jnp.any(slab_rows == offsets[:, None], axis=1).astype(jnp.float32)
    block_len = min(SPAN, TOK_DEV)
    pieces = TOKENS // block_len
    grad_blocks = grad_out.astype(jnp.float32).reshape(pieces, block_len, HEADS, HEAD_DIM).transpose(0, 2, 1, 3)
    reset_blocks = resets.reshape(pieces, block_len)

    def loss_of(x_float, raw, b_float, c_float, log_rate, skip_vec):
        step_size = jax.nn.softplus(raw + dt_bias[:, None])
        decay_log = -jnp.exp(log_rate)[:, None] * step_size
        x_blocks = x_float.reshape(pieces, block_len, HEADS, HEAD_DIM).transpose(0, 2, 1, 3)
        step_blocks = step_size.reshape(HEADS, pieces, block_len).transpose(1, 0, 2)
        decay_blocks = decay_log.reshape(HEADS, pieces, block_len).transpose(1, 0, 2)
        b_blocks = b_float.reshape(pieces, block_len, STATE)
        c_blocks = c_float.reshape(pieces, block_len, STATE)
        stepper = jax.checkpoint(partial_step(skip_vec, block_len))
        initial = (jnp.zeros((HEADS, HEAD_DIM, STATE), jnp.float32), jnp.zeros((), jnp.float32))
        (ending, running), unused = lax.scan(stepper, initial, (x_blocks, step_blocks, decay_blocks, b_blocks, c_blocks, reset_blocks, grad_blocks))
        return running
    gradients = jax.grad(loss_of, argnums=(0, 1, 2, 3, 4, 5))(x_vals.astype(jnp.float32), dt_raw.astype(jnp.float32), b_proj.astype(jnp.float32), c_proj.astype(jnp.float32), a_log, skip_weight)
    grad_x = gradients[0].astype(jnp.bfloat16)
    grad_dt = gradients[1]
    grad_bc = jnp.stack([gradients[2], gradients[3]])
    head_grads = jnp.stack([gradients[4], gradients[5]]) / math.sqrt(TOKENS * HEAD_DIM)
    return (grad_x, grad_dt, grad_bc, head_grads)
```

```python
import functools
import math

import jax
import jax.numpy as jnp
from jax import lax
from jax.experimental import pallas as pl
from jax.experimental.pallas import tpu as pltpu
from jax.sharding import PartitionSpec as P

HEAD_DIM = 64
MESH = pl.DeviceIdType.MESH
F32 = jnp.float32
BF16 = jnp.bfloat16
HIGHEST = lax.Precision.HIGHEST

ROWS = ((1,), (1,))
COLS = ((0,), (0,))
PLAIN = ((1,), (0,))


def mm(a, b, dims):
    return lax.dot_general(a, b, (dims, ((), ())), preferred_element_type=F32)


def split(a):
    high = a.astype(BF16)
    return high, (a - high.astype(F32)).astype(BF16)


def mm2(a, b, dims):
    high, low = split(a)
    return mm(high, b, dims) + mm(low, b, dims)


def mm2r(a, b, dims):
    high, low = split(b)
    return mm(a, high, dims) + mm(a, low, dims)


def mm3(a, b, dims):
    a_high, a_low = split(a)
    b_high, b_low = split(b)
    return mm(a_high, b_high, dims) + (mm(a_high, b_low, dims) + mm(a_low, b_high, dims))


def kernel(
    nseq, nhead, norm,
    x_ref, sc_ref, dt_ref, bias_ref, alog_ref, skip_ref, b_ref, c_ref, doc_ref, g_ref,
    gx_out, dt_out, bc_out, hg_out,
    fac, steps, cums, rates, sigm, skips, meta, msend, bcf, xgs, xg, kern, same, first, last,
    xs_s, ge_s, exit_s, loc, es, rs_, er, rr, gxa, gxr, kg, cx, skp, ct, sg, sgr, bcp, red, gat, hgp,
    meta_sems, bc_sems, xg_send, xg_recv, e_send, e_recv, r_send, r_recv, gx_send, gx_recv,
    sg_sems, red_send, red_recv, gat_send, gat_recv, hg_send, hg_recv,
):
    me, hd = lax.axis_index("seq"), lax.axis_index("head")
    par, z = lax.rem(me, 2), lax.div(me, 2)
    zs = nseq // 2
    oth = 1 - par
    partner = me + 1 - 2 * par
    tok = x_ref.shape[0]
    heads = dt_ref.shape[0]
    half = heads // 2
    npair = half // 2

    barrier = pltpu.get_barrier_semaphore()
    for j in range(1, nseq):
        pl.semaphore_signal(barrier, inc=1, device_id=(lax.rem(me + j, nseq), hd), device_id_type=MESH)
    for j in range(1, nhead):
        there = lax.rem(hd + j, nhead)
        pl.semaphore_signal(barrier, inc=1, device_id=(me, there), device_id_type=MESH)
        pl.semaphore_signal(barrier, inc=1, device_id=(partner, there), device_id_type=MESH)

    def remote(src, dst, send, recv, device):
        return pltpu.make_async_remote_copy(
            src_ref=src, dst_ref=dst, send_sem=send, recv_sem=recv,
            device_id=device, device_id_type=MESH,
        )

    across = (partner, hd)

    def bc_copy(slab):
        return remote(bcf.at[slab], bcf.at[slab], bc_sems.at[0], bc_sems.at[1], across)

    def meta_copy(slab):
        return remote(msend, meta.at[slab], meta_sems.at[0], meta_sems.at[1], across)

    def xg_copy(slab, k):
        return remote(xgs.at[k], xg.at[slab, k], xg_send.at[k], xg_recv.at[k], across)

    def e_copy(k):
        return remote(es.at[k], er.at[k], e_send.at[k], e_recv.at[k], (lax.rem(me + 2, nseq), hd))

    def r_copy(k):
        return remote(rs_.at[k], rr.at[k], r_send.at[k], r_recv.at[k], (lax.rem(me + nseq - 2, nseq), hd))

    def gx_copy(k):
        return remote(gxa.at[oth, k], gxr.at[k], gx_send.at[k], gx_recv.at[k], across)

    bcf[par, 0] = b_ref[...].astype(F32)
    bcf[par, 1] = c_ref[...].astype(F32)
    fac[...] = jnp.left_shift(jnp.int32(1), sc_ref[...] + 8).astype(F32) / 256.0

    sub = lax.broadcasted_iota(jnp.int32, (heads, heads), 0)
    lane = lax.broadcasted_iota(jnp.int32, (heads, heads), 1)

    def column(ref):
        return jnp.sum(jnp.where(sub == lane, ref[...], 0.0), axis=1, keepdims=True)

    t_sub = lax.broadcasted_iota(jnp.int32, (tok, tok), 0)
    t_lane = lax.broadcasted_iota(jnp.int32, (tok, tok), 1)
    pre = dt_ref[...].astype(F32) + column(bias_ref)
    step_all = jnp.maximum(pre, 0.0) + jnp.log1p(jnp.exp(-jnp.abs(pre)))
    rate = jnp.exp(column(alog_ref))
    upper = (t_sub <= t_lane).astype(F32)
    steps[...] = step_all
    cums[...] = lax.dot_general(
        -rate * step_all, upper, (PLAIN, ((), ())), precision=HIGHEST, preferred_element_type=F32
    )
    rates[...] = jnp.broadcast_to(rate, (heads, tok))
    sigm[...] = 1.0 / (1.0 + jnp.exp(-pre))
    skips[...] = jnp.broadcast_to(column(skip_ref), (heads, tok))
    row_id = lax.broadcasted_iota(jnp.int32, (8, tok), 1)
    count = jnp.zeros((8, tok), F32)
    for j in range(doc_ref.shape[1]):
        count = count + (row_id >= doc_ref[0, j]).astype(F32)
    mine = pl.ds(pl.multiple_of(par * half, half), half)
    theirs = pl.ds(pl.multiple_of(oth * half, half), half)
    meta[par, 0:half] = steps[mine]
    meta[par, half:2 * half] = cums[mine]
    meta[par, 2 * half:2 * half + 8] = count
    msend[0:half] = steps[theirs]
    msend[half:2 * half] = cums[theirs]
    msend[2 * half:2 * half + 8] = count

    pl.semaphore_wait(barrier, nseq - 1 + 2 * (nhead - 1))
    bc_copy(par).start()
    meta_copy(par).start()

    def scaled(j):
        lanes = pl.ds(pl.multiple_of(j * tok, tok), tok)
        factor = jnp.broadcast_to(fac[pl.ds(j, 1), :], (tok, tok)).T
        return x_ref[:, lanes].astype(F32) * factor, g_ref[:, lanes].astype(F32)

    def send_pair(k, carry):
        x_val, g_val = scaled(oth * npair + k)
        xgs[k, 0] = x_val
        xgs[k, 1] = g_val
        xg_copy(par, k).start()
        return carry

    lax.fori_loop(0, npair, send_pair, 0)

    def own_pair(k, carry):
        x_val, g_val = scaled(par * npair + k)
        xg[par, k, 0] = x_val
        xg[par, k, 1] = g_val
        return carry

    lax.fori_loop(0, npair, own_pair, 0)
    kg[...] = jnp.zeros_like(kg)
    cx[...] = jnp.zeros_like(cx)

    @pl.when(z == 0)
    def _():
        er[...] = jnp.zeros_like(er)

    @pl.when(z == zs - 1)
    def _():
        rr[...] = jnp.zeros_like(rr)

    bc_copy(oth).wait_recv()
    meta_copy(oth).wait_recv()

    def pair_of(q, row):
        return meta[q, pl.ds(row, 1), :]

    for q in range(2):
        seg_row = jnp.broadcast_to(meta[q, 2 * half:2 * half + 1, :], (tok, tok))
        seg_col = seg_row.T
        end = meta[q, 2 * half:2 * half + 1, tok - 1:tok]
        same[q] = ((t_sub >= t_lane) & (seg_row == seg_col)).astype(F32)
        first[q] = (seg_col == 0.0).astype(F32)
        last[q] = (seg_col == end).astype(F32)
        kern[q] = mm(bcf[q, 1].astype(BF16), bcf[q, 0].astype(BF16), ROWS)

    def lanes_of(a, b):
        return jnp.concatenate(
            [jnp.broadcast_to(a, (HEAD_DIM, tok)), jnp.broadcast_to(b, (HEAD_DIM, tok))], axis=0
        ).T

    def slab_decay(q, k):
        whole = 1.0 - jnp.minimum(meta[q, 2 * half:2 * half + 1, tok - 1:tok], 1.0)
        ends = [
            jnp.broadcast_to(
                jnp.exp(pair_of(q, half + 2 * k + s)[:, tok - 1:tok]) * whole, (HEAD_DIM, tok)
            )
            for s in range(2)
        ]
        return jnp.concatenate(ends, axis=0)

    def local_part(k):
        xg_copy(oth, k).wait_recv()
        states, grads = [], []
        for q in range(2):
            cum = lanes_of(pair_of(q, half + 2 * k), pair_of(q, half + 2 * k + 1))
            step = lanes_of(pair_of(q, 2 * k), pair_of(q, 2 * k + 1))
            enter_w = jnp.exp(cum) * first[q]
            exit_w = jnp.exp(cum[tok - 1:tok, :] - cum) * last[q]
            xs = exit_w * (step * xg[q, k, 0])
            ge = enter_w * xg[q, k, 1]
            xs_s[k, q] = xs
            ge_s[k, q] = ge
            exit_s[k, q] = exit_w
            states.append(mm2(xs, bcf[q, 0].astype(BF16), COLS))
            grads.append(mm2(ge, bcf[q, 1].astype(BF16), COLS))
        d0, d1 = slab_decay(0, k), slab_decay(1, k)
        loc[k, 0] = d1 * states[0] + states[1]
        loc[k, 1] = d0 * grads[1] + grads[0]
        loc[k, 2] = states[0]
        loc[k, 3] = grads[1]

    def forward_part(k):
        @pl.when(z > 0)
        def _():
            e_copy(k).wait_recv()

        @pl.when(z < zs - 1)
        def _():
            es[k] = slab_decay(0, k) * slab_decay(1, k) * er[k] + loc[k, 0]
            e_copy(k).start()

    def backward_part(k):
        @pl.when(z < zs - 1)
        def _():
            r_copy(k).wait_recv()

        @pl.when(z > 0)
        def _():
            rs_[k] = slab_decay(0, k) * slab_decay(1, k) * rr[k] + loc[k, 1]
            r_copy(k).start()

    lane_a = t_lane < HEAD_DIM

    def final_part(k):
        entry0, exit1 = er[k], rr[k]
        decays = [slab_decay(0, k), slab_decay(1, k)]
        entries = [entry0, decays[0] * entry0 + loc[k, 2]]
        exits = [decays[1] * exit1 + loc[k, 3], exit1]
        skip_rows = [skips[pl.ds(par * half + 2 * k + s, 1), :] for s in range(2)]
        skip_lanes = jnp.where(lane_a[0:1], skip_rows[0], skip_rows[1])
        skip_sum = jnp.zeros((1, tok), F32)
        for q in range(2):
            x_val, g_val = xg[q, k, 0], xg[q, k, 1]
            bq, cq = bcf[q, 0].astype(BF16), bcf[q, 1].astype(BF16)
            xs, ge, exit_w = xs_s[k, q], ge_s[k, q], exit_s[k, q]
            entry, leave = entries[q], exits[q]
            read = mm2r(cq, entry, ROWS)
            back = mm2r(bq, leave, ROWS)
            cx[q, 1] += mm3(ge, entry, PLAIN)
            cx[q, 0] += mm3(xs, leave, PLAIN)
            exit_terms = xs * back
            g_two = jnp.concatenate(
                [jnp.where(lane_a, g_val, 0.0), jnp.where(lane_a, 0.0, g_val)], axis=0
            ).astype(BF16)
            scores = mm(g_two, x_val.astype(BF16), ROWS)
            weights, flows = [], []
            kern_q, mask = kern[q], same[q] > 0.5
            total = jnp.zeros((tok, tok), F32)
            for s in range(2):
                step_row = pair_of(q, 2 * k + s)
                row = jnp.broadcast_to(pair_of(q, half + 2 * k + s), (tok, tok))
                decay = jnp.exp(jnp.where(mask, row.T - row, -1e30))
                part = decay * (scores[s * tok:(s + 1) * tok] * step_row)
                total = total + part
                weights.append(decay * kern_q)
                flows.append(part * kern_q)
            kg[q] += total
            inner = mm2(jnp.concatenate(weights, axis=0), g_two, COLS)
            input_total = inner + exit_w * back
            sums = (ge * read - exit_terms).T
            moved = (input_total * x_val).T
            exit_sum = jnp.sum(exit_terms, axis=0, keepdims=True)
            both = leave * entry * decays[q]
            at_end = t_lane[0:1] == tok - 1
            for s in range(2):
                span = slice(s * HEAD_DIM, (s + 1) * HEAD_DIM)
                ending = jnp.sum(exit_sum[:, span], keepdims=True) + jnp.sum(both[span], keepdims=True)
                cumul = (
                    jnp.sum(flows[s].T - flows[s], axis=0, keepdims=True)
                    + jnp.sum(sums[span], axis=0, keepdims=True)
                    + jnp.where(at_end, ending, 0.0)
                )
                ct[q, pl.ds(2 * k + s, 1), :] = cumul
                sg[q, pl.ds(2 * k + s, 1), :] = jnp.sum(moved[span], axis=0, keepdims=True)
            skip_sum = skip_sum + jnp.sum(g_val * x_val, axis=0, keepdims=True)
            step = lanes_of(pair_of(q, 2 * k), pair_of(q, 2 * k + 1))
            gxa[q, k] = input_total * step + skip_lanes * g_val
        skp[pl.ds(k, 1), :] = skip_sum
        gx_copy(k).start()
        own_lanes = pl.ds(pl.multiple_of((par * npair + k) * tok, tok), tok)
        gx_out[:, own_lanes] = gxa[par, k].astype(BF16)

    def lap(i, carry):
        @pl.when(i < npair)
        def _():
            local_part(i)

        ahead = i - z

        @pl.when((ahead >= 0) & (ahead < npair))
        def _():
            forward_part(ahead)

        behind = i - (zs - 1 - z)

        @pl.when((behind >= 0) & (behind < npair))
        def _():
            backward_part(behind)

        @pl.when(i >= zs - 1)
        def _():
            final_part(i - (zs - 1))

        return carry

    lax.fori_loop(0, npair + zs - 1, lap, 0)

    for q in range(2):
        bcp[q, 0:tok] = mm2(kg[q], bcf[q, 1].astype(BF16), COLS) + cx[q, 0]
        bcp[q, tok:2 * tok] = mm2(kg[q], bcf[q, 0].astype(BF16), PLAIN) + cx[q, 1]
    piece = 2 * tok // nhead
    here = par * nhead + hd
    base = me - par

    def red_copy(to, slot):
        rows = pl.ds(pl.multiple_of(lax.rem(to, nhead) * piece, piece), piece)
        return remote(
            bcp.at[lax.div(to, nhead), rows], red.at[slot], red_send.at[to], red_recv.at[slot],
            (base + lax.div(to, nhead), lax.rem(to, nhead)),
        )

    for j in range(1, 2 * nhead):
        red_copy(lax.rem(here + j, 2 * nhead), here).start()

    lower = (t_sub >= t_lane).astype(F32)
    rate_own = rates[mine]
    alog_sum = jnp.zeros((half, 1), F32)
    for q in range(2):
        decay_grad = lax.dot_general(
            ct[q], lower, (PLAIN, ((), ())), precision=HIGHEST, preferred_element_type=F32
        )
        sg[q] = sg[q] - rate_own * decay_grad
        alog_sum = alog_sum - jnp.sum(decay_grad * meta[q, 0:half] * rate_own, axis=1, keepdims=True)
    sg_copy = remote(sg.at[oth], sgr, sg_sems.at[0], sg_sems.at[1], across)
    sg_copy.start()
    h_sub = lax.broadcasted_iota(jnp.int32, (half, tok), 0)
    h_lane = lax.broadcasted_iota(jnp.int32, (half, tok), 1) - par * half
    alog_row = jnp.sum(jnp.where(h_sub == h_lane, alog_sum, 0.0), axis=0, keepdims=True)
    skip_all = skp[...]
    skip_a = jnp.sum(skip_all[:, 0:HEAD_DIM], axis=1, keepdims=True)
    skip_b = jnp.sum(skip_all[:, HEAD_DIM:], axis=1, keepdims=True)
    k_sub, k_lane = 2 * h_sub[0:npair], h_lane[0:npair]
    skip_row = jnp.sum(
        jnp.where(k_sub == k_lane, skip_a, 0.0) + jnp.where(k_sub + 1 == k_lane, skip_b, 0.0),
        axis=0, keepdims=True,
    )
    r_sub = lax.broadcasted_iota(jnp.int32, (8, tok), 0)
    hgp[me] = jnp.where(r_sub == 0, alog_row, jnp.where(r_sub == 1, skip_row, 0.0))

    def hg_copy(to, slot):
        return remote(hgp.at[slot], hgp.at[slot], hg_send.at[to], hg_recv.at[slot], (to, hd))

    for j in range(1, nseq):
        hg_copy(lax.rem(me + j, nseq), me).start()

    red[here] = bcp[par, pl.ds(pl.multiple_of(hd * piece, piece), piece), :]
    for j in range(1, 2 * nhead):
        other = lax.rem(here + j, 2 * nhead)
        red_copy(other, other).wait_recv()
    gat[hd] = jnp.sum(red[...], axis=0)

    def gat_copy(to, slot):
        return remote(gat.at[slot], gat.at[slot], gat_send.at[to], gat_recv.at[slot], (me, to))

    for j in range(1, nhead):
        gat_copy(lax.rem(hd + j, nhead), hd).start()

    def take_pair(k, carry):
        gx_copy(k).wait_recv()
        lanes = pl.ds(pl.multiple_of((oth * npair + k) * tok, tok), tok)
        gx_out[:, lanes] = gxr[k].astype(BF16)
        return carry

    lax.fori_loop(0, npair, take_pair, 0)
    dt_out[mine] = sg[par] * sigm[mine]
    sg_copy.wait_recv()
    dt_out[theirs] = sgr[...] * sigm[theirs]
    for j in range(1, nseq):
        other = lax.rem(me + j, nseq)
        hg_copy(other, other).wait_recv()
    hg_out[...] = jnp.sum(hgp[...], axis=0)[0:2, 0:heads] * norm
    for j in range(1, nhead):
        other = lax.rem(hd + j, nhead)
        gat_copy(other, other).wait_recv()
    bc_out[...] = gat[...].reshape(2, tok, b_ref.shape[1])

    bc_copy(par).wait_send()
    meta_copy(par).wait_send()
    sg_copy.wait_send()

    def drain(k, carry):
        xg_copy(par, k).wait_send()
        gx_copy(k).wait_send()

        @pl.when(z < zs - 1)
        def _():
            e_copy(k).wait_send()

        @pl.when(z > 0)
        def _():
            r_copy(k).wait_send()

        return carry

    lax.fori_loop(0, npair, drain, 0)
    for j in range(1, 2 * nhead):
        red_copy(lax.rem(here + j, 2 * nhead), here).wait_send()
    for j in range(1, nhead):
        gat_copy(lax.rem(hd + j, nhead), hd).wait_send()
    for j in range(1, nseq):
        hg_copy(lax.rem(me + j, nseq), me).wait_send()


def local(
    x_quant, scale_exp, dt_raw, dt_bias, a_log, skip_weight, b_proj, c_proj, doc_starts, grad_out
):
    nseq, nhead = lax.axis_size("seq"), lax.axis_size("head")
    tok, channels = x_quant.shape
    heads = dt_raw.shape[0]
    state = b_proj.shape[1]
    half, npair = heads // 2, heads // 4
    norm = 1.0 / math.sqrt(tok * nseq * HEAD_DIM)
    vmem = lambda *shape: pltpu.VMEM(shape, F32)
    dma = lambda n: pltpu.SemaphoreType.DMA((n,))
    sq = (tok, state)
    scratch = [
        vmem(scale_exp.shape[0], tok),
        vmem(heads, tok), vmem(heads, tok), vmem(heads, tok), vmem(heads, tok), vmem(heads, tok),
        vmem(2, 2 * half + 8, tok), vmem(2 * half + 8, tok),
        vmem(2, 2, *sq),
        vmem(npair, 2, *sq), vmem(2, npair, 2, *sq),
        vmem(2, *sq), vmem(2, *sq), vmem(2, *sq), vmem(2, *sq),
        vmem(npair, 2, *sq), vmem(npair, 2, *sq), vmem(npair, 2, *sq),
        vmem(npair, 4, *sq),
        vmem(npair, *sq), vmem(npair, *sq), vmem(npair, *sq), vmem(npair, *sq),
        vmem(2, npair, *sq), vmem(npair, *sq),
        vmem(2, *sq), vmem(2, 2, *sq),
        vmem(npair, tok),
        vmem(2, half, tok), vmem(2, half, tok), vmem(half, tok),
        vmem(2, 2 * tok, state),
        vmem(2 * nhead, 2 * tok // nhead, state),
        vmem(nhead, 2 * tok // nhead, state),
        vmem(nseq, 8, tok),
        dma(2), dma(2), dma(npair), dma(npair), dma(npair), dma(npair), dma(npair), dma(npair),
        dma(npair), dma(npair), dma(2), dma(2 * nhead), dma(2 * nhead), dma(nhead), dma(nhead),
        dma(nseq), dma(nseq),
    ]
    whole = pl.BlockSpec(memory_space=pltpu.VMEM)
    return tuple(pl.pallas_call(
        functools.partial(kernel, nseq, nhead, norm),
        out_shape=(
            jax.ShapeDtypeStruct((tok, channels), BF16),
            jax.ShapeDtypeStruct((heads, tok), F32),
            jax.ShapeDtypeStruct((2, tok, state), F32),
            jax.ShapeDtypeStruct((2, heads), F32),
        ),
        in_specs=[whole] * 8 + [pl.BlockSpec(memory_space=pltpu.SMEM), whole],
        out_specs=(whole,) * 4,
        scratch_shapes=scratch,
        compiler_params=pltpu.CompilerParams(
            collective_id=0, has_side_effects=True, vmem_limit_bytes=48 << 20
        ),
    )(
        x_quant, scale_exp, dt_raw, dt_bias.reshape(1, heads), a_log.reshape(1, heads),
        skip_weight.reshape(1, heads), b_proj, c_proj, doc_starts, grad_out,
    ))


def solution(mesh):
    in_specs = (
        P("seq", "head"),
        P("head", "seq"),
        P("head", "seq"),
        P("head"),
        P("head"),
        P("head"),
        P("seq", None),
        P("seq", None),
        P("seq", None),
        P("seq", "head"),
    )
    out_specs = (P("seq", "head"), P("head", "seq"), P(None, "seq", None), P(None, "head"))
    return jax.shard_map(local, mesh=mesh, in_specs=in_specs, out_specs=out_specs, check_vma=False)
```

```python
import functools
import math

import jax
import jax.numpy as jnp
from jax import lax
from jax.experimental import pallas as pl
from jax.experimental.pallas import tpu as pltpu
from jax.sharding import PartitionSpec as P

HEAD_DIM = 64
MESH = pl.DeviceIdType.MESH
F32 = jnp.float32
BF16 = jnp.bfloat16
HIGHEST = lax.Precision.HIGHEST

ROWS = ((1,), (1,))
COLS = ((0,), (0,))
PLAIN = ((1,), (0,))


def mm(a, b, dims):
    return lax.dot_general(a, b, (dims, ((), ())), preferred_element_type=F32)


def split(a):
    high = a.astype(BF16)
    return high, (a - high.astype(F32)).astype(BF16)


def mm2(a, b, dims):
    high, low = split(a)
    return mm(high, b, dims) + mm(low, b, dims)


def mm2r(a, b, dims):
    high, low = split(b)
    return mm(a, high, dims) + mm(a, low, dims)


def kernel(
    nseq, nhead, norm,
    x_hbm, sc_hbm, dt_hbm, b_hbm, c_hbm, g_hbm, bias_ref, alog_ref, skip_ref, doc_ref,
    gx_out, dt_out, bc_out, hg_out,
    x_ref, sc_ref, dt_ref, b_ref, c_ref, g_ref,
    fac, steps, cums, rates, sigm, skips, meta, msend, bcf, xgs, xg, kern, same, first, last, cols,
    twice, turned, step_s, enter_s, exit_s, ds_s, w_s, xs_s, ge_s, loc, es, rs_, er, rr, gxa, gxr,
    kg, cx, ends, skp, ct, sg, sgr, ctc, sgc, bcp, red, gat, hgp, in_sems,
    meta_sems, bc_sems, xg_send, xg_recv, e_send, e_recv, r_send, r_recv, gx_send, gx_recv,
    sg_sems, red_send, red_recv, gat_send, gat_recv, hg_send, hg_recv,
):
    me, hd = lax.axis_index("seq"), lax.axis_index("head")
    par, z = lax.rem(me, 2), lax.div(me, 2)
    zs = nseq // 2
    oth = 1 - par
    partner = me + 1 - 2 * par
    tok = x_ref.shape[0]
    heads = dt_ref.shape[0]
    half = heads // 2
    npair = half // 2

    fetches = [
        pltpu.make_async_copy(src, dst, in_sems.at[i])
        for i, (src, dst) in enumerate((
            (sc_hbm, sc_ref), (b_hbm, b_ref), (c_hbm, c_ref), (dt_hbm, dt_ref), (x_hbm, x_ref), (g_hbm, g_ref),
        ))
    ]
    for fetch in fetches:
        fetch.start()
    barrier = pltpu.get_barrier_semaphore()
    for j in range(1, nseq):
        pl.semaphore_signal(barrier, inc=1, device_id=(lax.rem(me + j, nseq), hd), device_id_type=MESH)
    for j in range(1, nhead):
        there = lax.rem(hd + j, nhead)
        pl.semaphore_signal(barrier, inc=1, device_id=(me, there), device_id_type=MESH)
        pl.semaphore_signal(barrier, inc=1, device_id=(partner, there), device_id_type=MESH)

    def remote(src, dst, send, recv, device):
        return pltpu.make_async_remote_copy(
            src_ref=src, dst_ref=dst, send_sem=send, recv_sem=recv,
            device_id=device, device_id_type=MESH,
        )

    across = (partner, hd)

    def bc_copy(slab):
        return remote(bcf.at[slab], bcf.at[slab], bc_sems.at[0], bc_sems.at[1], across)

    def meta_copy(slab):
        return remote(msend, meta.at[slab], meta_sems.at[0], meta_sems.at[1], across)

    def xg_copy(slab, k):
        return remote(xgs.at[k], xg.at[slab, k], xg_send.at[k], xg_recv.at[k], across)

    def e_copy(k):
        return remote(es.at[k], er.at[k], e_send.at[k], e_recv.at[k], (lax.rem(me + 2, nseq), hd))

    def r_copy(k):
        return remote(rs_.at[k], rr.at[k], r_send.at[k], r_recv.at[k], (lax.rem(me + nseq - 2, nseq), hd))

    def gx_copy(k):
        return remote(gxa.at[oth, k], gxr.at[k], gx_send.at[k], gx_recv.at[k], across)

    for fetch in fetches[:4]:
        fetch.wait()
    bcf[par, 0] = b_ref[...].astype(F32)
    bcf[par, 1] = c_ref[...].astype(F32)
    fac[...] = jnp.left_shift(jnp.int32(1), sc_ref[...] + 8).astype(F32) / 256.0

    sub = lax.broadcasted_iota(jnp.int32, (heads, heads), 0)
    lane = lax.broadcasted_iota(jnp.int32, (heads, heads), 1)

    def column(ref):
        return jnp.sum(jnp.where(sub == lane, ref[...], 0.0), axis=1, keepdims=True)

    t_sub = lax.broadcasted_iota(jnp.int32, (tok, tok), 0)
    t_lane = lax.broadcasted_iota(jnp.int32, (tok, tok), 1)
    pre = dt_ref[...].astype(F32) + column(bias_ref)
    step_all = jnp.maximum(pre, 0.0) + jnp.log1p(jnp.exp(-jnp.abs(pre)))
    rate = jnp.exp(column(alog_ref))
    upper = (t_sub <= t_lane).astype(F32)
    steps[...] = step_all
    cums[...] = lax.dot_general(
        -rate * step_all, upper, (PLAIN, ((), ())), precision=HIGHEST, preferred_element_type=F32
    )
    rates[...] = jnp.broadcast_to(rate, (heads, tok))
    sigm[...] = 1.0 / (1.0 + jnp.exp(-pre))
    skips[...] = jnp.broadcast_to(column(skip_ref), (heads, tok))
    row_id = lax.broadcasted_iota(jnp.int32, (8, tok), 1)
    count = jnp.zeros((8, tok), F32)
    for j in range(doc_ref.shape[1]):
        count = count + (row_id >= doc_ref[0, j]).astype(F32)
    mine = pl.ds(pl.multiple_of(par * half, half), half)
    theirs = pl.ds(pl.multiple_of(oth * half, half), half)
    for fetch in fetches[4:]:
        fetch.wait()
    meta[par, 0:half] = steps[mine]
    meta[par, half:2 * half] = cums[mine]
    meta[par, 2 * half:2 * half + 8] = count
    msend[0:half] = steps[theirs]
    msend[half:2 * half] = cums[theirs]
    msend[2 * half:2 * half + 8] = count

    pl.semaphore_wait(barrier, nseq - 1 + 2 * (nhead - 1))
    bc_copy(par).start()
    meta_copy(par).start()

    def scaled(j):
        lanes = pl.ds(pl.multiple_of(j * tok, tok), tok)
        factor = jnp.broadcast_to(fac[pl.ds(j, 1), :], (tok, tok)).T
        return x_ref[:, lanes].astype(F32) * factor, g_ref[:, lanes].astype(F32)

    def send_pair(k, carry):
        x_val, g_val = scaled(oth * npair + k)
        xgs[k, 0] = x_val
        xgs[k, 1] = g_val
        xg_copy(par, k).start()
        return carry

    lax.fori_loop(0, npair, send_pair, 0)

    def own_pair(k, carry):
        x_val, g_val = scaled(par * npair + k)
        xg[par, k, 0] = x_val
        xg[par, k, 1] = g_val
        return carry

    lax.fori_loop(0, npair, own_pair, 0)
    kg[...] = jnp.zeros_like(kg)
    cx[...] = jnp.zeros_like(cx)
    ctc[...] = jnp.zeros_like(ctc)
    sgc[...] = jnp.zeros_like(sgc)

    @pl.when(z == 0)
    def _():
        er[...] = jnp.zeros_like(er)

    @pl.when(z == zs - 1)
    def _():
        rr[...] = jnp.zeros_like(rr)

    lane_a = t_lane < HEAD_DIM

    def row_of(q, row):
        return meta[q, pl.ds(row, 1), :]

    def prepare(q):
        seg_row = jnp.broadcast_to(meta[q, 2 * half:2 * half + 1, :], (tok, tok))
        padded = jnp.concatenate([meta[q], jnp.zeros((tok - 2 * half - 8, tok), F32)], axis=0).T
        cols[...] = padded
        seg_col = jnp.broadcast_to(padded[:, 2 * half:2 * half + 1], (tok, tok))
        end = meta[q, 2 * half:2 * half + 1, tok - 1:tok]
        same[...] = ((t_sub <= t_lane) & (seg_row == seg_col)).astype(F32)
        first[...] = (seg_col == 0.0).astype(F32)
        last[...] = (seg_col == end).astype(F32)
        for i in range(2):
            whole = bcf[q, i].astype(BF16)
            flat = bcf[q, i].T.astype(BF16)
            twice[q, i] = jnp.concatenate([whole, whole], axis=1)
            turned[q, i] = jnp.concatenate([flat, flat], axis=1)
        kern[q] = mm(bcf[q, 0].astype(BF16), bcf[q, 1].astype(BF16), ROWS)

        def pair(k, carry):
            rolled = pltpu.roll(cols[...], lax.rem(tok - 2 * k, tok), 1)
            step_cols = [jnp.broadcast_to(rolled[:, i:i + 1], (tok, tok)) for i in range(2)]
            cum_cols = [jnp.broadcast_to(rolled[:, half + i:half + i + 1], (tok, tok)) for i in range(2)]
            cum = jnp.where(lane_a, cum_cols[0], cum_cols[1])
            step_s[k, q] = jnp.where(lane_a, step_cols[0], step_cols[1])
            enter_s[k, q] = jnp.exp(cum) * first[...]
            exit_s[k, q] = jnp.exp(cum[tok - 1:tok, :] - cum) * last[...]
            mask = same[...] > 0.5
            for i in range(2):
                gap = row_of(q, half + 2 * k + i) - cum_cols[i]
                decay = jnp.exp(jnp.where(mask, gap, -1e30))
                ds_s[k, q, i] = decay * step_cols[i]
                high, low = split(decay * kern[q])
                w_s[k, q, :, i * tok:(i + 1) * tok] = high
                w_s[k, q, :, (2 + i) * tok:(3 + i) * tok] = low
            return carry

        lax.fori_loop(0, npair, pair, 0)

    prepare(par)
    bc_copy(oth).wait_recv()
    meta_copy(oth).wait_recv()
    prepare(oth)

    def decay_of(q, k):
        return enter_s[k, q, tok - 1:tok, :]

    def local_part(k):
        xg_copy(oth, k).wait_recv()
        states, grads = [], []
        for q in range(2):
            xs = exit_s[k, q] * (step_s[k, q] * xg[q, k, 0])
            ge = enter_s[k, q] * xg[q, k, 1]
            xs_two = jnp.concatenate(split(xs), axis=0)
            ge_two = jnp.concatenate(split(ge), axis=0)
            xs_s[k, q] = xs_two
            ge_s[k, q] = ge_two
            states.append(mm(turned[q, 0], xs_two, PLAIN))
            grads.append(mm(turned[q, 1], ge_two, PLAIN))
        loc[k, 0] = decay_of(1, k) * states[0] + states[1]
        loc[k, 1] = decay_of(0, k) * grads[1] + grads[0]
        loc[k, 2] = states[0]
        loc[k, 3] = grads[1]

    def forward_part(k):
        @pl.when(z > 0)
        def _():
            e_copy(k).wait_recv()

        @pl.when(z < zs - 1)
        def _():
            es[k] = (decay_of(0, k) * decay_of(1, k)) * er[k] + loc[k, 0]
            e_copy(k).start()

    def backward_part(k):
        @pl.when(z < zs - 1)
        def _():
            r_copy(k).wait_recv()

        @pl.when(z > 0)
        def _():
            rs_[k] = (decay_of(0, k) * decay_of(1, k)) * rr[k] + loc[k, 1]
            r_copy(k).start()

    def wide(a):
        return jnp.concatenate([a[0:tok], a[tok:2 * tok]], axis=1)

    def corner(high, low):
        return jnp.concatenate(
            [jnp.concatenate([high, high], axis=1), jnp.concatenate([low, low], axis=1)], axis=0
        )

    def final_part(k):
        entry0, exit1 = er[k], rr[k]
        entries = [entry0, decay_of(0, k) * entry0 + loc[k, 2]]
        exits = [decay_of(1, k) * exit1 + loc[k, 3], exit1]
        skip_rows = [skips[pl.ds(par * half + 2 * k + i, 1), :] for i in range(2)]
        skip_lanes = jnp.where(lane_a[0:1], skip_rows[0], skip_rows[1])
        skip_sum = jnp.zeros((1, tok), F32)
        for q in range(2):
            x_val, g_val = xg[q, k, 0], xg[q, k, 1]
            exit_w, step = exit_s[k, q], step_s[k, q]
            entry, leave = entries[q], exits[q]
            e_high, e_low = split(entry)
            l_high, l_low = split(leave)
            read = mm(twice[q, 1], jnp.concatenate([e_high, e_low], axis=0), PLAIN)
            back = mm(twice[q, 0], jnp.concatenate([l_high, l_low], axis=0), PLAIN)
            cx[q, 1] += mm(wide(ge_s[k, q]), corner(e_high, e_low), ROWS)
            cx[q, 0] += mm(wide(xs_s[k, q]), corner(l_high, l_low), ROWS)
            g_two = jnp.concatenate(
                [jnp.where(lane_a, g_val, 0.0), jnp.where(lane_a, 0.0, g_val)], axis=0
            ).astype(BF16)
            scores = mm(x_val.astype(BF16), g_two, ROWS)
            inner = mm(w_s[k, q], jnp.concatenate([g_two, g_two], axis=0), PLAIN)
            kern_q = kern[q]
            parts = [scores[:, i * tok:(i + 1) * tok] * ds_s[k, q, i] for i in range(2)]
            kg[q] += parts[0] + parts[1]
            flows = [part * kern_q for part in parts]
            back_w = exit_w * back
            input_total = inner + back_w
            exit_terms = (step * x_val) * back_w
            through = (enter_s[k, q] * g_val) * read - exit_terms
            moved = input_total * x_val
            ends[q, pl.ds(k, 1), :] = jnp.sum(
                exit_terms + leave * entry * decay_of(q, k), axis=0, keepdims=True
            )
            ct_cols, sg_cols = ctc[q], sgc[q]
            for i in range(2):
                mine_only = lane_a if i == 0 else ~lane_a
                ct_col = jnp.sum(jnp.where(mine_only, through, 0.0) - flows[i], axis=1, keepdims=True)
                sg_col = jnp.sum(jnp.where(mine_only, moved, 0.0), axis=1, keepdims=True)
                spot = t_lane == 2 * k + i
                ct_cols = jnp.where(spot, ct_col, ct_cols)
                sg_cols = jnp.where(spot, sg_col, sg_cols)
                ct[q, pl.ds(2 * k + i, 1), :] = jnp.sum(flows[i], axis=0, keepdims=True)
            ctc[q] = ct_cols
            sgc[q] = sg_cols
            skip_sum = skip_sum + jnp.sum(g_val * x_val, axis=0, keepdims=True)
            gxa[q, k] = input_total * step + skip_lanes * g_val
        skp[pl.ds(k, 1), :] = skip_sum
        gx_copy(k).start()
        own_lanes = pl.ds(pl.multiple_of((par * npair + k) * tok, tok), tok)
        gx_out[:, own_lanes] = gxa[par, k].astype(BF16)

    def lap(i, carry):
        @pl.when(i < npair)
        def _():
            local_part(i)

        ahead = i - z

        @pl.when((ahead >= 0) & (ahead < npair))
        def _():
            forward_part(ahead)

        behind = i - (zs - 1 - z)

        @pl.when((behind >= 0) & (behind < npair))
        def _():
            backward_part(behind)

        @pl.when(i >= zs - 1)
        def _():
            final_part(i - (zs - 1))

        return carry

    lax.fori_loop(0, npair + zs - 1, lap, 0)

    for q in range(2):
        b_sum, c_sum = cx[q, 0], cx[q, 1]
        b_sum, c_sum = b_sum[:, 0:tok] + b_sum[:, tok:], c_sum[:, 0:tok] + c_sum[:, tok:]
        bcp[q, 0:tok] = mm2(kg[q], bcf[q, 1].astype(BF16), PLAIN) + b_sum
        bcp[q, tok:2 * tok] = mm2(kg[q], bcf[q, 0].astype(BF16), COLS) + c_sum
    piece = 2 * tok // nhead
    here = par * nhead + hd
    base = me - par

    def red_copy(to, slot):
        rows = pl.ds(pl.multiple_of(lax.rem(to, nhead) * piece, piece), piece)
        return remote(
            bcp.at[lax.div(to, nhead), rows], red.at[slot], red_send.at[to], red_recv.at[slot],
            (base + lax.div(to, nhead), lax.rem(to, nhead)),
        )

    for j in range(1, 2 * nhead):
        red_copy(lax.rem(here + j, 2 * nhead), here).start()

    lower = (t_sub >= t_lane).astype(F32)
    rate_own = rates[mine]
    alog_sum = jnp.zeros((half, 1), F32)
    h_sub = lax.broadcasted_iota(jnp.int32, (half, tok), 0)
    h_lane = lax.broadcasted_iota(jnp.int32, (half, tok), 1)
    pick = lax.div(h_lane, HEAD_DIM) == lax.rem(h_sub, 2)
    for q in range(2):
        per_pair = ends[q]
        ending = jnp.sum(
            jnp.where(pick, jnp.broadcast_to(per_pair[:, None, :], (npair, 2, tok)).reshape(half, tok), 0.0),
            axis=1, keepdims=True,
        )
        total = ct[q] + ctc[q].T[0:half] + jnp.where(h_lane == tok - 1, ending, 0.0)
        sg[q] = sgc[q].T[0:half]
        decay_grad = lax.dot_general(
            total, lower, (PLAIN, ((), ())), precision=HIGHEST, preferred_element_type=F32
        )
        sg[q] = sg[q] - rate_own * decay_grad
        alog_sum = alog_sum - jnp.sum(decay_grad * meta[q, 0:half] * rate_own, axis=1, keepdims=True)
    sg_copy = remote(sg.at[oth], sgr, sg_sems.at[0], sg_sems.at[1], across)
    sg_copy.start()
    h_lane = h_lane - par * half
    alog_row = jnp.sum(jnp.where(h_sub == h_lane, alog_sum, 0.0), axis=0, keepdims=True)
    skip_all = skp[...]
    skip_a = jnp.sum(skip_all[:, 0:HEAD_DIM], axis=1, keepdims=True)
    skip_b = jnp.sum(skip_all[:, HEAD_DIM:], axis=1, keepdims=True)
    k_sub, k_lane = 2 * h_sub[0:npair], h_lane[0:npair]
    skip_row = jnp.sum(
        jnp.where(k_sub == k_lane, skip_a, 0.0) + jnp.where(k_sub + 1 == k_lane, skip_b, 0.0),
        axis=0, keepdims=True,
    )
    r_sub = lax.broadcasted_iota(jnp.int32, (8, tok), 0)
    hgp[me] = jnp.where(r_sub == 0, alog_row, jnp.where(r_sub == 1, skip_row, 0.0))

    def hg_copy(to, slot):
        return remote(hgp.at[slot], hgp.at[slot], hg_send.at[to], hg_recv.at[slot], (to, hd))

    for j in range(1, nseq):
        hg_copy(lax.rem(me + j, nseq), me).start()

    red[here] = bcp[par, pl.ds(pl.multiple_of(hd * piece, piece), piece), :]
    for j in range(1, 2 * nhead):
        other = lax.rem(here + j, 2 * nhead)
        red_copy(other, other).wait_recv()
    gat[hd] = jnp.sum(red[...], axis=0)

    def gat_copy(to, slot):
        return remote(gat.at[slot], gat.at[slot], gat_send.at[to], gat_recv.at[slot], (me, to))

    for j in range(1, nhead):
        gat_copy(lax.rem(hd + j, nhead), hd).start()

    def take_pair(k, carry):
        gx_copy(k).wait_recv()
        lanes = pl.ds(pl.multiple_of((oth * npair + k) * tok, tok), tok)
        gx_out[:, lanes] = gxr[k].astype(BF16)
        return carry

    lax.fori_loop(0, npair, take_pair, 0)
    dt_out[mine] = sg[par] * sigm[mine]
    sg_copy.wait_recv()
    dt_out[theirs] = sgr[...] * sigm[theirs]
    for j in range(1, nseq):
        other = lax.rem(me + j, nseq)
        hg_copy(other, other).wait_recv()
    hg_out[...] = jnp.sum(hgp[...], axis=0)[0:2, 0:heads] * norm
    for j in range(1, nhead):
        other = lax.rem(hd + j, nhead)
        gat_copy(other, other).wait_recv()
    bc_out[...] = gat[...].reshape(2, tok, b_ref.shape[1])

    bc_copy(par).wait_send()
    meta_copy(par).wait_send()
    sg_copy.wait_send()

    def drain(k, carry):
        xg_copy(par, k).wait_send()
        gx_copy(k).wait_send()

        @pl.when(z < zs - 1)
        def _():
            e_copy(k).wait_send()

        @pl.when(z > 0)
        def _():
            r_copy(k).wait_send()

        return carry

    lax.fori_loop(0, npair, drain, 0)
    for j in range(1, 2 * nhead):
        red_copy(lax.rem(here + j, 2 * nhead), here).wait_send()
    for j in range(1, nhead):
        gat_copy(lax.rem(hd + j, nhead), hd).wait_send()
    for j in range(1, nseq):
        hg_copy(lax.rem(me + j, nseq), me).wait_send()


def local(
    x_quant, scale_exp, dt_raw, dt_bias, a_log, skip_weight, b_proj, c_proj, doc_starts, grad_out
):
    nseq, nhead = lax.axis_size("seq"), lax.axis_size("head")
    tok, channels = x_quant.shape
    heads = dt_raw.shape[0]
    state = b_proj.shape[1]
    half, npair = heads // 2, heads // 4
    norm = 1.0 / math.sqrt(tok * nseq * HEAD_DIM)
    vmem = lambda *shape: pltpu.VMEM(shape, F32)
    dma = lambda n: pltpu.SemaphoreType.DMA((n,))
    sq = (tok, state)
    half16 = lambda *shape: pltpu.VMEM(shape, BF16)
    scratch = [
        half16(tok, channels), pltpu.VMEM(scale_exp.shape, jnp.int32), half16(heads, tok),
        half16(*sq), half16(*sq), half16(tok, channels),
        vmem(scale_exp.shape[0], tok),
        vmem(heads, tok), vmem(heads, tok), vmem(heads, tok), vmem(heads, tok), vmem(heads, tok),
        vmem(2, 2 * half + 8, tok), vmem(2 * half + 8, tok),
        vmem(2, 2, *sq),
        vmem(npair, 2, *sq), vmem(2, npair, 2, *sq),
        vmem(2, *sq), vmem(*sq), vmem(*sq), vmem(*sq), vmem(*sq),
        half16(2, 2, tok, 2 * state), half16(2, 2, state, 2 * tok),
        vmem(npair, 2, *sq), vmem(npair, 2, *sq), vmem(npair, 2, *sq),
        vmem(npair, 2, 2, *sq), half16(npair, 2, tok, 4 * tok),
        half16(npair, 2, 2 * tok, state), half16(npair, 2, 2 * tok, state),
        vmem(npair, 4, *sq),
        vmem(npair, *sq), vmem(npair, *sq), vmem(npair, *sq), vmem(npair, *sq),
        vmem(2, npair, *sq), vmem(npair, *sq),
        vmem(2, *sq), vmem(2, 2, tok, 2 * state),
        vmem(2, npair, tok), vmem(npair, tok),
        vmem(2, half, tok), vmem(2, half, tok), vmem(half, tok),
        vmem(2, *sq), vmem(2, *sq),
        vmem(2, 2 * tok, state),
        vmem(2 * nhead, 2 * tok // nhead, state),
        vmem(nhead, 2 * tok // nhead, state),
        vmem(nseq, 8, tok),
        dma(6),
        dma(2), dma(2), dma(npair), dma(npair), dma(npair), dma(npair), dma(npair), dma(npair),
        dma(npair), dma(npair), dma(2), dma(2 * nhead), dma(2 * nhead), dma(nhead), dma(nhead),
        dma(nseq), dma(nseq),
    ]
    whole = pl.BlockSpec(memory_space=pltpu.VMEM)
    return tuple(pl.pallas_call(
        functools.partial(kernel, nseq, nhead, norm),
        out_shape=(
            jax.ShapeDtypeStruct((tok, channels), BF16),
            jax.ShapeDtypeStruct((heads, tok), F32),
            jax.ShapeDtypeStruct((2, tok, state), F32),
            jax.ShapeDtypeStruct((2, heads), F32),
        ),
        in_specs=[pl.BlockSpec(memory_space=pl.ANY)] * 6 + [whole] * 3 + [pl.BlockSpec(memory_space=pltpu.SMEM)],
        out_specs=(whole,) * 4,
        scratch_shapes=scratch,
        compiler_params=pltpu.CompilerParams(
            collective_id=0, has_side_effects=True, vmem_limit_bytes=48 << 20
        ),
    )(
        x_quant, scale_exp, dt_raw, b_proj, c_proj, grad_out, dt_bias.reshape(1, heads),
        a_log.reshape(1, heads), skip_weight.reshape(1, heads), doc_starts,
    ))


def solution(mesh):
    in_specs = (
        P("seq", "head"),
        P("head", "seq"),
        P("head", "seq"),
        P("head"),
        P("head"),
        P("head"),
        P("seq", None),
        P("seq", None),
        P("seq", None),
        P("seq", "head"),
    )
    out_specs = (P("seq", "head"), P("head", "seq"), P(None, "seq", None), P(None, "head"))
    return jax.shard_map(local, mesh=mesh, in_specs=in_specs, out_specs=out_specs, check_vma=False)
```

```python
import functools
import math

import jax
import jax.numpy as jnp
from jax import lax
from jax.experimental import pallas as pl
from jax.experimental.pallas import tpu as pltpu
from jax.sharding import PartitionSpec as P

HEAD_DIM = 64
MESH = pl.DeviceIdType.MESH
F32 = jnp.float32
BF16 = jnp.bfloat16
HIGHEST = lax.Precision.HIGHEST

ROWS = ((1,), (1,))
COLS = ((0,), (0,))
PLAIN = ((1,), (0,))


def mm(a, b, dims):
    return lax.dot_general(a, b, (dims, ((), ())), preferred_element_type=F32)


def split(a):
    high = a.astype(BF16)
    return high, (a - high.astype(F32)).astype(BF16)


def mm2(a, b, dims):
    high, low = split(a)
    return mm(high, b, dims) + mm(low, b, dims)


def mm2r(a, b, dims):
    high, low = split(b)
    return mm(a, high, dims) + mm(a, low, dims)


def kernel(
    nseq, nhead, norm,
    x_hbm, sc_hbm, dt_hbm, b_hbm, c_hbm, g_hbm, bias_ref, alog_ref, skip_ref, doc_ref,
    gx_out, dt_out, bc_out, hg_out,
    x_ref, sc_ref, dt_ref, b_ref, c_ref, g_ref,
    fac, steps, rates, skips, meta, cf, gg, xv, kern, same, first, last, cols,
    twice, turned, step_s, enter_s, exit_s, ds_s, w_s, xs_s, ge_s, loc, es, rs_, er, rr,
    kg, bx, cx, ends, skp, ct, ctc, sgc, far, near, own_out, oth_out, red_own, red_oth, gat, hgp,
    in_sems, c_sems, meta_sems, g_send, g_recv, e_send, e_recv, r_send, r_recv, far_sems,
    own_send, own_recv, oth_send, oth_recv, gat_send, gat_recv, hg_send, hg_recv,
):
    me, hd = lax.axis_index("seq"), lax.axis_index("head")
    par, z = lax.rem(me, 2), lax.div(me, 2)
    zs = nseq // 2
    oth = 1 - par
    partner = me + 1 - 2 * par
    tok = x_ref.shape[0]
    heads = dt_ref.shape[0]
    npair = heads // 2
    step_at = heads + 8

    fetches = [
        pltpu.make_async_copy(src, dst, in_sems.at[i])
        for i, (src, dst) in enumerate((
            (c_hbm, c_ref), (dt_hbm, dt_ref), (g_hbm, g_ref), (sc_hbm, sc_ref), (b_hbm, b_ref), (x_hbm, x_ref),
        ))
    ]
    for fetch in fetches:
        fetch.start()
    barrier = pltpu.get_barrier_semaphore()
    for j in range(1, nseq):
        pl.semaphore_signal(barrier, inc=1, device_id=(lax.rem(me + j, nseq), hd), device_id_type=MESH)
    for j in range(1, nhead):
        there = lax.rem(hd + j, nhead)
        pl.semaphore_signal(barrier, inc=1, device_id=(me, there), device_id_type=MESH)
        pl.semaphore_signal(barrier, inc=1, device_id=(partner, there), device_id_type=MESH)

    def remote(src, dst, send, recv, device):
        return pltpu.make_async_remote_copy(
            src_ref=src, dst_ref=dst, send_sem=send, recv_sem=recv,
            device_id=device, device_id_type=MESH,
        )

    across = (partner, hd)

    def c_copy(slab):
        return remote(cf.at[slab], cf.at[slab], c_sems.at[0], c_sems.at[1], across)

    def meta_copy(slab):
        return remote(meta.at[slab], meta.at[slab], meta_sems.at[0], meta_sems.at[1], across)

    def g_copy(slab, k):
        return remote(gg.at[slab, k], gg.at[slab, k], g_send.at[k], g_recv.at[k], across)

    def e_copy(k):
        return remote(es.at[k], er.at[k], e_send.at[k], e_recv.at[k], (lax.rem(me + 2, nseq), hd))

    def r_copy(k):
        return remote(rs_.at[k], rr.at[k], r_send.at[k], r_recv.at[k], (lax.rem(me + nseq - 2, nseq), hd))

    sub = lax.broadcasted_iota(jnp.int32, (heads, heads), 0)
    lane = lax.broadcasted_iota(jnp.int32, (heads, heads), 1)

    def column(ref):
        return jnp.sum(jnp.where(sub == lane, ref[...], 0.0), axis=1, keepdims=True)

    t_sub = lax.broadcasted_iota(jnp.int32, (tok, tok), 0)
    t_lane = lax.broadcasted_iota(jnp.int32, (tok, tok), 1)
    lane_a = t_lane < HEAD_DIM
    rate = jnp.exp(column(alog_ref))
    rates[...] = jnp.broadcast_to(rate, (heads, tok))
    skips[...] = jnp.broadcast_to(column(skip_ref), (heads, tok))
    row_id = lax.broadcasted_iota(jnp.int32, (8, tok), 1)
    count = jnp.zeros((8, tok), F32)
    for j in range(doc_ref.shape[1]):
        count = count + (row_id >= doc_ref[0, j]).astype(F32)
    bias = column(bias_ref)
    fetches[0].wait()
    cf[par] = c_ref[...].astype(F32)
    fetches[1].wait()
    pre = dt_ref[...].astype(F32) + bias
    step_all = jnp.maximum(pre, 0.0) + jnp.log1p(jnp.exp(-jnp.abs(pre)))
    steps[...] = step_all
    upper = (t_sub <= t_lane).astype(F32)
    meta[par, 0:heads] = lax.dot_general(
        -rate * step_all, upper, (PLAIN, ((), ())), precision=HIGHEST, preferred_element_type=F32
    )
    meta[par, heads:heads + 8] = count
    fetches[2].wait()

    pl.semaphore_wait(barrier, nseq - 1 + 2 * (nhead - 1))
    meta_copy(par).start()
    c_copy(par).start()

    def lanes_at(k):
        return pl.ds(pl.multiple_of(k * tok, tok), tok)

    def send_pair(k, carry):
        gg[par, k] = g_ref[:, lanes_at(k)].astype(F32)
        g_copy(par, k).start()
        return carry

    lax.fori_loop(0, npair, send_pair, 0)
    for fetch in fetches[3:]:
        fetch.wait()
    fac[...] = jnp.left_shift(jnp.int32(1), sc_ref[...] + 8).astype(F32) / 256.0
    kg[...] = jnp.zeros_like(kg)
    bx[...] = jnp.zeros_like(bx)
    cx[...] = jnp.zeros_like(cx)
    ctc[...] = jnp.zeros_like(ctc)
    sgc[...] = jnp.zeros_like(sgc)

    @pl.when(z == 0)
    def _():
        er[...] = jnp.zeros_like(er)

    @pl.when(z == zs - 1)
    def _():
        rr[...] = jnp.zeros_like(rr)

    def row_of(q, row):
        return meta[q, pl.ds(row, 1), :]

    def prepare(q, rest):
        rows = jnp.concatenate([meta[q], rest], axis=0)
        flat = rows.T
        cols[q] = flat
        seg_col = jnp.broadcast_to(flat[:, heads:heads + 1], (tok, tok))
        first[q] = (seg_col == 0.0).astype(F32)
        whole = cf[q].astype(BF16)
        c_flat = cf[q].T.astype(BF16)
        twice[q] = jnp.concatenate([whole, whole], axis=1)
        turned[q] = jnp.concatenate([c_flat, c_flat], axis=1)
        return seg_col

    def enter_of(q, k):
        rolled = pltpu.roll(cols[q], lax.rem(tok - 2 * k, tok), 1)
        cum_cols = [jnp.broadcast_to(rolled[:, i:i + 1], (tok, tok)) for i in range(2)]
        cum = jnp.where(lane_a, cum_cols[0], cum_cols[1])
        enter_s[q, k] = jnp.exp(cum) * first[q]
        return rolled, cum_cols, cum

    seg_own = prepare(par, jnp.concatenate([steps[...], jnp.zeros((tok - 2 * heads - 8, tok), F32)], axis=0))
    seg_row = jnp.broadcast_to(meta[par, heads:heads + 1, :], (tok, tok))
    same[...] = ((t_sub <= t_lane) & (seg_row == seg_own)).astype(F32)
    last[...] = (seg_own == meta[par, heads:heads + 1, tok - 1:tok]).astype(F32)
    b_own = b_ref[...]
    b_flat = b_own.astype(F32).T.astype(BF16)
    twice[2] = jnp.concatenate([b_own, b_own], axis=1)
    turned[2] = jnp.concatenate([b_flat, b_flat], axis=1)
    kern[...] = mm(b_own, c_ref[...], ROWS)

    def own_pair(k, carry):
        factor = jnp.broadcast_to(fac[pl.ds(k, 1), :], (tok, tok)).T
        x_val = x_ref[:, lanes_at(k)].astype(F32) * factor
        xv[k] = x_val
        rolled, cum_cols, cum = enter_of(par, k)
        step_cols = [jnp.broadcast_to(rolled[:, step_at + i:step_at + i + 1], (tok, tok)) for i in range(2)]
        step = jnp.where(lane_a, step_cols[0], step_cols[1])
        exit_w = jnp.exp(cum[tok - 1:tok, :] - cum) * last[...]
        step_s[k] = step
        exit_s[k] = exit_w
        mask = same[...] > 0.5
        for i in range(2):
            gap = row_of(par, 2 * k + i) - cum_cols[i]
            decay = jnp.exp(jnp.where(mask, gap, -1e30))
            ds_s[k, i] = decay * step_cols[i]
            high, low = split(decay * kern[...])
            w_s[k, :, i * tok:(i + 1) * tok] = high
            w_s[k, :, (2 + i) * tok:(3 + i) * tok] = low
        xs_two = jnp.concatenate(split(exit_w * (step * x_val)), axis=0)
        xs_s[k] = xs_two
        loc[k, 2] = mm(turned[2], xs_two, PLAIN)
        ge_s[par, k] = jnp.concatenate(split(enter_s[par, k] * gg[par, k]), axis=0)
        return carry

    lax.fori_loop(0, npair, own_pair, 0)
    meta_copy(oth).wait_recv()
    c_copy(oth).wait_recv()
    prepare(oth, jnp.zeros((tok - heads - 8, tok), F32))

    def decay_of(q, k):
        return enter_s[q, k, tok - 1:tok, :]

    def local_part(k):
        enter_of(oth, k)
        g_copy(oth, k).wait_recv()
        ge_s[oth, k] = jnp.concatenate(split(enter_s[oth, k] * gg[oth, k]), axis=0)
        grads = [mm(turned[q], ge_s[q, k], PLAIN) for q in range(2)]
        onward = jnp.where(par == 0, decay_of(1, k), 1.0)
        loc[k, 0] = onward * loc[k, 2]
        loc[k, 1] = decay_of(0, k) * grads[1] + grads[0]
        loc[k, 3] = grads[1]

    def forward_part(k):
        @pl.when(z > 0)
        def _():
            e_copy(k).wait_recv()

        @pl.when(z < zs - 1)
        def _():
            es[k] = (decay_of(0, k) * decay_of(1, k)) * er[k] + loc[k, 0]
            e_copy(k).start()

    def backward_part(k):
        @pl.when(z < zs - 1)
        def _():
            r_copy(k).wait_recv()

        @pl.when(z > 0)
        def _():
            rs_[k] = (decay_of(0, k) * decay_of(1, k)) * rr[k] + loc[k, 1]
            r_copy(k).start()

    def wide(a):
        return jnp.concatenate([a[0:tok], a[tok:2 * tok]], axis=1)

    def corner(high, low):
        return jnp.concatenate(
            [jnp.concatenate([high, high], axis=1), jnp.concatenate([low, low], axis=1)], axis=0
        )

    def final_part(k):
        entry0, exit1 = er[k], rr[k]
        entry1 = decay_of(0, k) * entry0 + jnp.where(par == 0, loc[k, 2], 0.0)
        exit0 = decay_of(1, k) * exit1 + loc[k, 3]
        early = par == 0
        entry_own, entry_oth = jnp.where(early, entry0, entry1), jnp.where(early, entry1, entry0)
        leave_own, leave_oth = jnp.where(early, exit0, exit1), jnp.where(early, exit1, exit0)

        def entering(q, entry):
            high, low = split(entry)
            read = mm(twice[q], jnp.concatenate([high, low], axis=0), PLAIN)
            cx[q] += mm(wide(ge_s[q, k]), corner(high, low), ROWS)
            return (enter_s[q, k] * gg[q, k]) * read

        def place(cols_ref, q, full, minus):
            kept = cols_ref[q]
            for i in range(2):
                part = jnp.where(lane_a if i == 0 else ~lane_a, full, 0.0)
                if minus is not None:
                    part = part - minus[i]
                kept = jnp.where(t_lane == 2 * k + i, jnp.sum(part, axis=1, keepdims=True), kept)
            cols_ref[q] = kept

        through = entering(oth, entry_oth)
        place(ctc, oth, through, None)
        ends[oth, pl.ds(k, 1), :] = jnp.sum(leave_oth * entry_oth, axis=0, keepdims=True) * decay_of(oth, k)

        x_val, g_val = xv[k], gg[par, k]
        exit_w, step = exit_s[k], step_s[k]
        l_high, l_low = split(leave_own)
        back = mm(twice[2], jnp.concatenate([l_high, l_low], axis=0), PLAIN)
        bx[...] += mm(wide(xs_s[k]), corner(l_high, l_low), ROWS)
        g_two = jnp.concatenate(
            [jnp.where(lane_a, g_val, 0.0), jnp.where(lane_a, 0.0, g_val)], axis=0
        ).astype(BF16)
        scores = mm(x_val.astype(BF16), g_two, ROWS)
        inner = mm(w_s[k], jnp.concatenate([g_two, g_two], axis=0), PLAIN)
        kern_own = kern[...]
        parts = [scores[:, i * tok:(i + 1) * tok] * ds_s[k, i] for i in range(2)]
        kg[...] += parts[0] + parts[1]
        flows = [part * kern_own for part in parts]
        back_w = exit_w * back
        input_total = inner + back_w
        exit_terms = (step * x_val) * back_w
        place(ctc, par, entering(par, entry_own) - exit_terms, flows)
        place(sgc, 0, input_total * x_val, None)
        ends[par, pl.ds(k, 1), :] = (
            jnp.sum(exit_terms, axis=0, keepdims=True)
            + jnp.sum(leave_own * entry_own, axis=0, keepdims=True) * decay_of(par, k)
        )
        for i in range(2):
            ct[pl.ds(2 * k + i, 1), :] = jnp.sum(flows[i], axis=0, keepdims=True)
        skp[pl.ds(k, 1), :] = jnp.sum(g_val * x_val, axis=0, keepdims=True)
        skip_rows = [skips[pl.ds(2 * k + i, 1), :] for i in range(2)]
        skip_lanes = jnp.where(lane_a[0:1], skip_rows[0], skip_rows[1])
        gx_out[:, lanes_at(k)] = (input_total * step + skip_lanes * g_val).astype(BF16)

    def lap(i, carry):
        @pl.when(i < npair)
        def _():
            local_part(i)

        ahead = i - z

        @pl.when((ahead >= 0) & (ahead < npair))
        def _():
            forward_part(ahead)

        behind = i - (zs - 1 - z)

        @pl.when((behind >= 0) & (behind < npair))
        def _():
            backward_part(behind)

        @pl.when(i >= zs - 1)
        def _():
            final_part(i - (zs - 1))

        return carry

    lax.fori_loop(0, npair + zs - 1, lap, 0)

    def folded(a):
        return a[:, 0:tok] + a[:, tok:]

    piece = tok // nhead
    state = b_ref.shape[1]
    oth_out[...] = folded(cx[oth]).reshape(nhead, piece, state)

    def oth_copy(to, slot):
        return remote(oth_out.at[to], red_oth.at[slot], oth_send.at[to], oth_recv.at[slot], (partner, to))

    def own_copy(to, slot):
        return remote(own_out.at[to], red_own.at[slot], own_send.at[to], own_recv.at[slot], (me, to))

    for j in range(nhead):
        oth_copy(lax.rem(hd + j, nhead), hd).start()

    h_sub = lax.broadcasted_iota(jnp.int32, (heads, tok), 0)
    h_lane = lax.broadcasted_iota(jnp.int32, (heads, tok), 1)
    pick = lax.div(h_lane, HEAD_DIM) == lax.rem(h_sub, 2)

    def cumul_of(q):
        per_head = jnp.broadcast_to(ends[q][:, None, :], (npair, 2, tok)).reshape(heads, tok)
        ending = jnp.sum(jnp.where(pick, per_head, 0.0), axis=1, keepdims=True)
        return ctc[q].T[0:heads] + jnp.where(h_lane == tok - 1, ending, 0.0)

    far[...] = cumul_of(oth)
    far_copy = remote(far, near, far_sems.at[0], far_sems.at[1], across)
    far_copy.start()

    own_out[:, 0] = (mm2(kg[...], c_ref[...], PLAIN) + folded(bx[...])).reshape(nhead, piece, state)
    own_out[:, 1] = (mm2(kg[...], b_ref[...], COLS) + folded(cx[par])).reshape(nhead, piece, state)
    for j in range(1, nhead):
        own_copy(lax.rem(hd + j, nhead), hd).start()

    mine = ct[...] + cumul_of(par)
    lower = (t_sub >= t_lane).astype(F32)
    far_copy.wait_recv()
    decay_grad = lax.dot_general(
        mine + near[...], lower, (PLAIN, ((), ())), precision=HIGHEST, preferred_element_type=F32
    )
    step_all = steps[...]
    alog_sum = -jnp.sum(decay_grad * step_all * rates[...], axis=1, keepdims=True)
    alog_row = jnp.sum(jnp.where(h_sub == h_lane, alog_sum, 0.0), axis=0, keepdims=True)
    skip_all = skp[...]
    skip_a = jnp.sum(skip_all[:, 0:HEAD_DIM], axis=1, keepdims=True)
    skip_b = jnp.sum(skip_all[:, HEAD_DIM:], axis=1, keepdims=True)
    k_sub, k_lane = 2 * h_sub[0:npair], h_lane[0:npair]
    skip_row = jnp.sum(
        jnp.where(k_sub == k_lane, skip_a, 0.0) + jnp.where(k_sub + 1 == k_lane, skip_b, 0.0),
        axis=0, keepdims=True,
    )
    r_sub = lax.broadcasted_iota(jnp.int32, (8, tok), 0)
    hgp[me] = jnp.where(r_sub == 0, alog_row, jnp.where(r_sub == 1, skip_row, 0.0))

    def hg_copy(to, slot):
        return remote(hgp.at[slot], hgp.at[slot], hg_send.at[to], hg_recv.at[slot], (to, hd))

    for j in range(1, nseq):
        hg_copy(lax.rem(me + j, nseq), me).start()

    red_own[hd] = own_out[hd]
    for j in range(nhead):
        other = lax.rem(hd + j, nhead)
        oth_copy(other, other).wait_recv()
    for j in range(1, nhead):
        other = lax.rem(hd + j, nhead)
        own_copy(other, other).wait_recv()
    b_c = jnp.sum(red_own[...], axis=0)
    gat[hd, 0] = b_c[0]
    gat[hd, 1] = b_c[1] + jnp.sum(red_oth[...], axis=0)

    def gat_copy(to, slot):
        return remote(gat.at[slot], gat.at[slot], gat_send.at[to], gat_recv.at[slot], (me, to))

    for j in range(1, nhead):
        gat_copy(lax.rem(hd + j, nhead), hd).start()

    sigmoid = 1.0 / (1.0 + jnp.exp(-(dt_ref[...].astype(F32) + bias)))
    dt_out[...] = (sgc[0].T[0:heads] - rates[...] * decay_grad) * sigmoid
    for j in range(1, nseq):
        other = lax.rem(me + j, nseq)
        hg_copy(other, other).wait_recv()
    hg_out[...] = jnp.sum(hgp[...], axis=0)[0:2, 0:heads] * norm
    for j in range(1, nhead):
        other = lax.rem(hd + j, nhead)
        gat_copy(other, other).wait_recv()
    for i in range(2):
        bc_out[i] = gat[:, i].reshape(tok, state)

    meta_copy(par).wait_send()
    c_copy(par).wait_send()
    far_copy.wait_send()

    def drain(k, carry):
        g_copy(par, k).wait_send()

        @pl.when(z < zs - 1)
        def _():
            e_copy(k).wait_send()

        @pl.when(z > 0)
        def _():
            r_copy(k).wait_send()

        return carry

    lax.fori_loop(0, npair, drain, 0)
    for j in range(nhead):
        oth_copy(lax.rem(hd + j, nhead), hd).wait_send()
    for j in range(1, nhead):
        own_copy(lax.rem(hd + j, nhead), hd).wait_send()
        gat_copy(lax.rem(hd + j, nhead), hd).wait_send()
    for j in range(1, nseq):
        hg_copy(lax.rem(me + j, nseq), me).wait_send()


def local(
    x_quant, scale_exp, dt_raw, dt_bias, a_log, skip_weight, b_proj, c_proj, doc_starts, grad_out
):
    nseq, nhead = lax.axis_size("seq"), lax.axis_size("head")
    tok, channels = x_quant.shape
    heads = dt_raw.shape[0]
    state = b_proj.shape[1]
    npair, piece = heads // 2, tok // nhead
    norm = 1.0 / math.sqrt(tok * nseq * HEAD_DIM)
    vmem = lambda *shape: pltpu.VMEM(shape, F32)
    half16 = lambda *shape: pltpu.VMEM(shape, BF16)
    dma = lambda n: pltpu.SemaphoreType.DMA((n,))
    sq = (tok, state)
    scratch = [
        half16(tok, channels), pltpu.VMEM(scale_exp.shape, jnp.int32), half16(heads, tok),
        half16(*sq), half16(*sq), half16(tok, channels),
        vmem(scale_exp.shape[0], tok),
        vmem(heads, tok), vmem(heads, tok), vmem(heads, tok),
        vmem(2, heads + 8, tok), vmem(2, *sq),
        vmem(2, npair, *sq), vmem(npair, *sq),
        vmem(*sq), vmem(*sq), vmem(2, *sq), vmem(*sq), vmem(2, *sq),
        half16(3, tok, 2 * state), half16(3, state, 2 * tok),
        vmem(npair, *sq), vmem(2, npair, *sq), vmem(npair, *sq),
        vmem(npair, 2, *sq), half16(npair, tok, 4 * tok),
        half16(npair, 2 * tok, state), half16(2, npair, 2 * tok, state),
        vmem(npair, 4, *sq),
        vmem(npair, *sq), vmem(npair, *sq), vmem(npair, *sq), vmem(npair, *sq),
        vmem(*sq), vmem(tok, 2 * state), vmem(2, tok, 2 * state),
        vmem(2, npair, tok), vmem(npair, tok), vmem(heads, tok),
        vmem(2, *sq), vmem(1, *sq), vmem(heads, tok), vmem(heads, tok),
        vmem(nhead, 2, piece, state), vmem(nhead, piece, state),
        vmem(nhead, 2, piece, state), vmem(nhead, piece, state),
        vmem(nhead, 2, piece, state), vmem(nseq, 8, tok),
        dma(6), dma(2), dma(2), dma(npair), dma(npair), dma(npair), dma(npair), dma(npair), dma(npair),
        dma(2), dma(nhead), dma(nhead), dma(nhead), dma(nhead), dma(nhead), dma(nhead),
        dma(nseq), dma(nseq),
    ]
    whole = pl.BlockSpec(memory_space=pltpu.VMEM)
    return tuple(pl.pallas_call(
        functools.partial(kernel, nseq, nhead, norm),
        out_shape=(
            jax.ShapeDtypeStruct((tok, channels), BF16),
            jax.ShapeDtypeStruct((heads, tok), F32),
            jax.ShapeDtypeStruct((2, tok, state), F32),
            jax.ShapeDtypeStruct((2, heads), F32),
        ),
        in_specs=[pl.BlockSpec(memory_space=pl.ANY)] * 6 + [whole] * 3 + [pl.BlockSpec(memory_space=pltpu.SMEM)],
        out_specs=(whole,) * 4,
        scratch_shapes=scratch,
        compiler_params=pltpu.CompilerParams(
            collective_id=0, has_side_effects=True, vmem_limit_bytes=60 << 20
        ),
    )(
        x_quant, scale_exp, dt_raw, b_proj, c_proj, grad_out, dt_bias.reshape(1, heads),
        a_log.reshape(1, heads), skip_weight.reshape(1, heads), doc_starts,
    ))


def solution(mesh):
    in_specs = (
        P("seq", "head"),
        P("head", "seq"),
        P("head", "seq"),
        P("head"),
        P("head"),
        P("head"),
        P("seq", None),
        P("seq", None),
        P("seq", None),
        P("seq", "head"),
    )
    out_specs = (P("seq", "head"), P("head", "seq"), P(None, "seq", None), P(None, "head"))
    return jax.shard_map(local, mesh=mesh, in_specs=in_specs, out_specs=out_specs, check_vma=False)
```

```python
import functools
import math

import jax
import jax.numpy as jnp
from jax import lax
from jax.experimental import pallas as pl
from jax.experimental.pallas import tpu as pltpu
from jax.sharding import PartitionSpec as P

HEAD_DIM = 64
LAG = 2
MESH = pl.DeviceIdType.MESH
F32 = jnp.float32
BF16 = jnp.bfloat16
HIGHEST = lax.Precision.HIGHEST

ROWS = ((1,), (1,))
COLS = ((0,), (0,))
PLAIN = ((1,), (0,))


def mm(a, b, dims):
    return lax.dot_general(a, b, (dims, ((), ())), preferred_element_type=F32)


def split(a):
    high = a.astype(BF16)
    return high, (a - high.astype(F32)).astype(BF16)


def mm2(a, b, dims):
    high, low = split(a)
    return mm(high, b, dims) + mm(low, b, dims)


def mm2r(a, b, dims):
    high, low = split(b)
    return mm(a, high, dims) + mm(a, low, dims)


def kernel(
    nseq, nhead, norm,
    x_hbm, sc_hbm, dt_hbm, b_hbm, c_hbm, g_hbm, bias_ref, alog_ref, skip_ref, doc_ref,
    gx_out, dt_out, bc_out, hg_out,
    x_ref, sc_ref, dt_ref, b_ref, c_ref, g_ref,
    fac, steps, rates, skips, meta, cf, gg, xv, kern, same, first, last, cols,
    twice, turned, step_s, enter_s, exit_s, inner_s, xs_s, ge_s, loc, es, rs_, er, rr,
    kg, bx, cx, ends, skp, ct, ctc, sgc, far, near, own_out, oth_out, red_own, red_oth, gat, hgp,
    in_sems, c_sems, meta_sems, g_send, g_recv, e_send, e_recv, r_send, r_recv, far_sems,
    own_send, own_recv, oth_send, oth_recv, gat_send, gat_recv, hg_send, hg_recv,
):
    me, hd = lax.axis_index("seq"), lax.axis_index("head")
    par, z = lax.rem(me, 2), lax.div(me, 2)
    zs = nseq // 2
    oth = 1 - par
    partner = me + 1 - 2 * par
    tok = x_ref.shape[0]
    heads = dt_ref.shape[0]
    npair = heads // 2
    step_at = heads + 8

    fetches = [
        pltpu.make_async_copy(src, dst, in_sems.at[i])
        for i, (src, dst) in enumerate((
            (c_hbm, c_ref), (dt_hbm, dt_ref), (g_hbm, g_ref), (sc_hbm, sc_ref), (b_hbm, b_ref), (x_hbm, x_ref),
        ))
    ]
    for fetch in fetches:
        fetch.start()
    barrier = pltpu.get_barrier_semaphore()
    for j in range(1, nseq):
        pl.semaphore_signal(barrier, inc=1, device_id=(lax.rem(me + j, nseq), hd), device_id_type=MESH)
    for j in range(1, nhead):
        there = lax.rem(hd + j, nhead)
        pl.semaphore_signal(barrier, inc=1, device_id=(me, there), device_id_type=MESH)
        pl.semaphore_signal(barrier, inc=1, device_id=(partner, there), device_id_type=MESH)

    def remote(src, dst, send, recv, device):
        return pltpu.make_async_remote_copy(
            src_ref=src, dst_ref=dst, send_sem=send, recv_sem=recv,
            device_id=device, device_id_type=MESH,
        )

    across = (partner, hd)

    def c_copy(slab):
        return remote(cf.at[slab], cf.at[slab], c_sems.at[0], c_sems.at[1], across)

    def meta_copy(slab):
        return remote(meta.at[slab], meta.at[slab], meta_sems.at[0], meta_sems.at[1], across)

    def g_copy(slab, k):
        return remote(gg.at[slab, k], gg.at[slab, k], g_send.at[k], g_recv.at[k], across)

    def e_copy(k):
        return remote(es.at[k], er.at[k], e_send.at[k], e_recv.at[k], (lax.rem(me + 2, nseq), hd))

    def r_copy(k):
        return remote(rs_.at[k], rr.at[k], r_send.at[k], r_recv.at[k], (lax.rem(me + nseq - 2, nseq), hd))

    sub = lax.broadcasted_iota(jnp.int32, (heads, heads), 0)
    lane = lax.broadcasted_iota(jnp.int32, (heads, heads), 1)

    def column(ref):
        return jnp.sum(jnp.where(sub == lane, ref[...], 0.0), axis=1, keepdims=True)

    t_sub = lax.broadcasted_iota(jnp.int32, (tok, tok), 0)
    t_lane = lax.broadcasted_iota(jnp.int32, (tok, tok), 1)
    lane_a = t_lane < HEAD_DIM
    rate = jnp.exp(column(alog_ref))
    rates[...] = jnp.broadcast_to(rate, (heads, tok))
    skips[...] = jnp.broadcast_to(column(skip_ref), (heads, tok))
    row_id = lax.broadcasted_iota(jnp.int32, (8, tok), 1)
    count = jnp.zeros((8, tok), F32)
    for j in range(doc_ref.shape[1]):
        count = count + (row_id >= doc_ref[0, j]).astype(F32)
    bias = column(bias_ref)
    fetches[0].wait()
    cf[par] = c_ref[...].astype(F32)
    fetches[1].wait()
    pre = dt_ref[...].astype(F32) + bias
    step_all = jnp.maximum(pre, 0.0) + jnp.log1p(jnp.exp(-jnp.abs(pre)))
    steps[...] = step_all
    upper = (t_sub <= t_lane).astype(F32)
    meta[par, 0:heads] = lax.dot_general(
        -rate * step_all, upper, (PLAIN, ((), ())), precision=HIGHEST, preferred_element_type=F32
    )
    meta[par, heads:heads + 8] = count
    fetches[2].wait()

    pl.semaphore_wait(barrier, nseq - 1 + 2 * (nhead - 1))
    meta_copy(par).start()
    c_copy(par).start()

    def lanes_at(k):
        return pl.ds(pl.multiple_of(k * tok, tok), tok)

    def send_pair(k, carry):
        gg[par, k] = g_ref[:, lanes_at(k)].astype(F32)
        g_copy(par, k).start()
        return carry

    lax.fori_loop(0, npair, send_pair, 0)
    for fetch in fetches[3:]:
        fetch.wait()
    fac[...] = jnp.left_shift(jnp.int32(1), sc_ref[...] + 8).astype(F32) / 256.0
    kg[...] = jnp.zeros_like(kg)
    bx[...] = jnp.zeros_like(bx)
    cx[...] = jnp.zeros_like(cx)
    ctc[...] = jnp.zeros_like(ctc)
    sgc[...] = jnp.zeros_like(sgc)

    @pl.when(z == 0)
    def _():
        er[...] = jnp.zeros_like(er)

    @pl.when(z == zs - 1)
    def _():
        rr[...] = jnp.zeros_like(rr)

    def row_of(q, row):
        return meta[q, pl.ds(row, 1), :]

    def prepare(q, rest):
        rows = jnp.concatenate([meta[q], rest], axis=0)
        flat = rows.T
        cols[q] = flat
        seg_col = jnp.broadcast_to(flat[:, heads:heads + 1], (tok, tok))
        first[q] = (seg_col == 0.0).astype(F32)
        whole = cf[q].astype(BF16)
        c_flat = cf[q].T.astype(BF16)
        twice[q] = jnp.concatenate([whole, whole], axis=1)
        turned[q] = jnp.concatenate([c_flat, c_flat], axis=1)
        return seg_col

    def enter_of(q, k):
        rolled = pltpu.roll(cols[q], lax.rem(tok - 2 * k, tok), 1)
        cum_cols = [jnp.broadcast_to(rolled[:, i:i + 1], (tok, tok)) for i in range(2)]
        cum = jnp.where(lane_a, cum_cols[0], cum_cols[1])
        enter_s[q, k] = jnp.exp(cum) * first[q]
        return rolled, cum_cols, cum

    seg_own = prepare(par, jnp.concatenate([steps[...], jnp.zeros((tok - 2 * heads - 8, tok), F32)], axis=0))
    seg_row = jnp.broadcast_to(meta[par, heads:heads + 1, :], (tok, tok))
    same[...] = ((t_sub <= t_lane) & (seg_row == seg_own)).astype(F32)
    last[...] = (seg_own == meta[par, heads:heads + 1, tok - 1:tok]).astype(F32)
    b_own = b_ref[...]
    b_flat = b_own.astype(F32).T.astype(BF16)
    twice[2] = jnp.concatenate([b_own, b_own], axis=1)
    turned[2] = jnp.concatenate([b_flat, b_flat], axis=1)
    kern[...] = mm(b_own, c_ref[...], ROWS)

    meta_copy(oth).wait_recv()
    c_copy(oth).wait_recv()
    prepare(oth, jnp.zeros((tok - heads - 8, tok), F32))

    def decay_of(q, k):
        return enter_s[q, k, tok - 1:tok, :]

    def own_part(k):
        factor = jnp.broadcast_to(fac[pl.ds(k, 1), :], (tok, tok)).T
        x_val = x_ref[:, lanes_at(k)].astype(F32) * factor
        xv[k] = x_val
        rolled, cum_cols, cum = enter_of(par, k)
        step_cols = [jnp.broadcast_to(rolled[:, step_at + i:step_at + i + 1], (tok, tok)) for i in range(2)]
        step = jnp.where(lane_a, step_cols[0], step_cols[1])
        exit_w = jnp.exp(cum[tok - 1:tok, :] - cum) * last[...]
        step_s[k] = step
        exit_s[k] = exit_w
        xs_two = jnp.concatenate(split(exit_w * (step * x_val)), axis=0)
        xs_s[k] = xs_two
        own_state = mm(turned[2], xs_two, PLAIN)
        loc[k, 2] = own_state
        g_val = gg[par, k]
        ge_s[par, k] = jnp.concatenate(split(enter_s[par, k] * g_val), axis=0)
        g_two = jnp.concatenate(
            [jnp.where(lane_a, g_val, 0.0), jnp.where(lane_a, 0.0, g_val)], axis=0
        ).astype(BF16)
        scores = mm(x_val.astype(BF16), g_two, ROWS)
        mask = same[...] > 0.5
        kern_own = kern[...]
        total, highs, lows, flows = None, [], [], []
        for i in range(2):
            gap = row_of(par, 2 * k + i) - cum_cols[i]
            decay = jnp.exp(jnp.where(mask, gap, -1e30))
            part = scores[:, i * tok:(i + 1) * tok] * (decay * step_cols[i])
            high, low = split(decay * kern_own)
            highs.append(high)
            lows.append(low)
            flow = part * kern_own
            flows.append(flow)
            total = part if total is None else total + part
            ct[pl.ds(2 * k + i, 1), :] = jnp.sum(flow, axis=0, keepdims=True)
        kg[...] += total
        kept = ctc[par]
        for i in range(2):
            kept = jnp.where(t_lane == 2 * k + i, -jnp.sum(flows[i], axis=1, keepdims=True), kept)
        ctc[par] = kept
        inner_s[k] = mm(
            jnp.concatenate(highs + lows, axis=1), jnp.concatenate([g_two, g_two], axis=0), PLAIN
        )
        skp[pl.ds(k, 1), :] = jnp.sum(g_val * x_val, axis=0, keepdims=True)

    def local_part(k):
        enter_of(oth, k)
        loc[k, 0] = jnp.where(par == 0, decay_of(1, k), 1.0) * loc[k, 2]
        g_copy(oth, k).wait_recv()
        ge_s[oth, k] = jnp.concatenate(split(enter_s[oth, k] * gg[oth, k]), axis=0)
        grads = [mm(turned[q], ge_s[q, k], PLAIN) for q in range(2)]
        loc[k, 1] = decay_of(0, k) * grads[1] + grads[0]
        loc[k, 3] = grads[1]

    def forward_part(k):
        @pl.when(z > 0)
        def _():
            e_copy(k).wait_recv()

        @pl.when(z < zs - 1)
        def _():
            es[k] = (decay_of(0, k) * decay_of(1, k)) * er[k] + loc[k, 0]
            e_copy(k).start()

    def backward_part(k):
        @pl.when(z < zs - 1)
        def _():
            r_copy(k).wait_recv()

        @pl.when(z > 0)
        def _():
            rs_[k] = (decay_of(0, k) * decay_of(1, k)) * rr[k] + loc[k, 1]
            r_copy(k).start()

    def wide(a):
        return jnp.concatenate([a[0:tok], a[tok:2 * tok]], axis=1)

    def corner(high, low):
        return jnp.concatenate(
            [jnp.concatenate([high, high], axis=1), jnp.concatenate([low, low], axis=1)], axis=0
        )

    def final_part(k):
        entry0, exit1 = er[k], rr[k]
        entry1 = decay_of(0, k) * entry0 + jnp.where(par == 0, loc[k, 2], 0.0)
        exit0 = decay_of(1, k) * exit1 + loc[k, 3]
        early = par == 0
        entry_own, entry_oth = jnp.where(early, entry0, entry1), jnp.where(early, entry1, entry0)
        leave_own, leave_oth = jnp.where(early, exit0, exit1), jnp.where(early, exit1, exit0)

        def entering(q, entry):
            high, low = split(entry)
            read = mm(twice[q], jnp.concatenate([high, low], axis=0), PLAIN)
            cx[q] += mm(wide(ge_s[q, k]), corner(high, low), ROWS)
            return (enter_s[q, k] * gg[q, k]) * read

        def place(cols_ref, q, full):
            kept = cols_ref[q]
            for i in range(2):
                part = jnp.where(lane_a if i == 0 else ~lane_a, full, 0.0)
                part_sum = jnp.sum(part, axis=1, keepdims=True)
                kept = kept + jnp.where(t_lane == 2 * k + i, part_sum, 0.0)
            cols_ref[q] = kept

        through = entering(oth, entry_oth)
        place(ctc, oth, through)
        ends[oth, pl.ds(k, 1), :] = jnp.sum(leave_oth * entry_oth, axis=0, keepdims=True) * decay_of(oth, k)

        x_val, g_val = xv[k], gg[par, k]
        exit_w, step = exit_s[k], step_s[k]
        l_high, l_low = split(leave_own)
        back = mm(twice[2], jnp.concatenate([l_high, l_low], axis=0), PLAIN)
        bx[...] += mm(wide(xs_s[k]), corner(l_high, l_low), ROWS)
        back_w = exit_w * back
        input_total = inner_s[k] + back_w
        exit_terms = (step * x_val) * back_w
        place(ctc, par, entering(par, entry_own) - exit_terms)
        place(sgc, 0, input_total * x_val)
        ends[par, pl.ds(k, 1), :] = (
            jnp.sum(exit_terms, axis=0, keepdims=True)
            + jnp.sum(leave_own * entry_own, axis=0, keepdims=True) * decay_of(par, k)
        )
        skip_rows = [skips[pl.ds(2 * k + i, 1), :] for i in range(2)]
        skip_lanes = jnp.where(lane_a[0:1], skip_rows[0], skip_rows[1])
        gx_out[:, lanes_at(k)] = (input_total * step + skip_lanes * g_val).astype(BF16)

    def lap(i, carry):
        @pl.when(i < npair)
        def _():
            own_part(i)
            local_part(i)

        ahead = i - LAG * z

        @pl.when((ahead >= 0) & (ahead < npair))
        def _():
            forward_part(ahead)

        behind = i - LAG * (zs - 1 - z)

        @pl.when((behind >= 0) & (behind < npair))
        def _():
            backward_part(behind)

        @pl.when(i >= LAG * (zs - 1))
        def _():
            final_part(i - LAG * (zs - 1))

        return carry

    lax.fori_loop(0, npair + LAG * (zs - 1), lap, 0)

    def folded(a):
        return a[:, 0:tok] + a[:, tok:]

    piece = tok // nhead
    state = b_ref.shape[1]
    oth_out[...] = folded(cx[oth]).reshape(nhead, piece, state)

    def oth_copy(to, slot):
        return remote(oth_out.at[to], red_oth.at[slot], oth_send.at[to], oth_recv.at[slot], (partner, to))

    def own_copy(to, slot):
        return remote(own_out.at[to], red_own.at[slot], own_send.at[to], own_recv.at[slot], (me, to))

    for j in range(nhead):
        oth_copy(lax.rem(hd + j, nhead), hd).start()

    h_sub = lax.broadcasted_iota(jnp.int32, (heads, tok), 0)
    h_lane = lax.broadcasted_iota(jnp.int32, (heads, tok), 1)
    pick = lax.div(h_lane, HEAD_DIM) == lax.rem(h_sub, 2)

    def cumul_of(q):
        per_head = jnp.broadcast_to(ends[q][:, None, :], (npair, 2, tok)).reshape(heads, tok)
        ending = jnp.sum(jnp.where(pick, per_head, 0.0), axis=1, keepdims=True)
        return ctc[q].T[0:heads] + jnp.where(h_lane == tok - 1, ending, 0.0)

    far[...] = cumul_of(oth)
    far_copy = remote(far, near, far_sems.at[0], far_sems.at[1], across)
    far_copy.start()

    own_out[:, 0] = (mm2(kg[...], c_ref[...], PLAIN) + folded(bx[...])).reshape(nhead, piece, state)
    own_out[:, 1] = (mm2(kg[...], b_ref[...], COLS) + folded(cx[par])).reshape(nhead, piece, state)
    for j in range(1, nhead):
        own_copy(lax.rem(hd + j, nhead), hd).start()

    mine = ct[...] + cumul_of(par)
    lower = (t_sub >= t_lane).astype(F32)
    far_copy.wait_recv()
    decay_grad = lax.dot_general(
        mine + near[...], lower, (PLAIN, ((), ())), precision=HIGHEST, preferred_element_type=F32
    )
    step_all = steps[...]
    alog_sum = -jnp.sum(decay_grad * step_all * rates[...], axis=1, keepdims=True)
    alog_row = jnp.sum(jnp.where(h_sub == h_lane, alog_sum, 0.0), axis=0, keepdims=True)
    skip_all = skp[...]
    skip_a = jnp.sum(skip_all[:, 0:HEAD_DIM], axis=1, keepdims=True)
    skip_b = jnp.sum(skip_all[:, HEAD_DIM:], axis=1, keepdims=True)
    k_sub, k_lane = 2 * h_sub[0:npair], h_lane[0:npair]
    skip_row = jnp.sum(
        jnp.where(k_sub == k_lane, skip_a, 0.0) + jnp.where(k_sub + 1 == k_lane, skip_b, 0.0),
        axis=0, keepdims=True,
    )
    r_sub = lax.broadcasted_iota(jnp.int32, (8, tok), 0)
    hgp[me] = jnp.where(r_sub == 0, alog_row, jnp.where(r_sub == 1, skip_row, 0.0))

    def hg_copy(to, slot):
        return remote(hgp.at[slot], hgp.at[slot], hg_send.at[to], hg_recv.at[slot], (to, hd))

    for j in range(1, nseq):
        hg_copy(lax.rem(me + j, nseq), me).start()

    red_own[hd] = own_out[hd]
    for j in range(nhead):
        other = lax.rem(hd + j, nhead)
        oth_copy(other, other).wait_recv()
    for j in range(1, nhead):
        other = lax.rem(hd + j, nhead)
        own_copy(other, other).wait_recv()
    b_c = jnp.sum(red_own[...], axis=0)
    gat[hd, 0] = b_c[0]
    gat[hd, 1] = b_c[1] + jnp.sum(red_oth[...], axis=0)

    def gat_copy(to, slot):
        return remote(gat.at[slot], gat.at[slot], gat_send.at[to], gat_recv.at[slot], (me, to))

    for j in range(1, nhead):
        gat_copy(lax.rem(hd + j, nhead), hd).start()

    sigmoid = 1.0 / (1.0 + jnp.exp(-(dt_ref[...].astype(F32) + bias)))
    dt_out[...] = (sgc[0].T[0:heads] - rates[...] * decay_grad) * sigmoid
    for j in range(1, nseq):
        other = lax.rem(me + j, nseq)
        hg_copy(other, other).wait_recv()
    hg_out[...] = jnp.sum(hgp[...], axis=0)[0:2, 0:heads] * norm
    for j in range(1, nhead):
        other = lax.rem(hd + j, nhead)
        gat_copy(other, other).wait_recv()
    for i in range(2):
        bc_out[i] = gat[:, i].reshape(tok, state)

    meta_copy(par).wait_send()
    c_copy(par).wait_send()
    far_copy.wait_send()

    def drain(k, carry):
        g_copy(par, k).wait_send()

        @pl.when(z < zs - 1)
        def _():
            e_copy(k).wait_send()

        @pl.when(z > 0)
        def _():
            r_copy(k).wait_send()

        return carry

    lax.fori_loop(0, npair, drain, 0)
    for j in range(nhead):
        oth_copy(lax.rem(hd + j, nhead), hd).wait_send()
    for j in range(1, nhead):
        own_copy(lax.rem(hd + j, nhead), hd).wait_send()
        gat_copy(lax.rem(hd + j, nhead), hd).wait_send()
    for j in range(1, nseq):
        hg_copy(lax.rem(me + j, nseq), me).wait_send()


def local(
    x_quant, scale_exp, dt_raw, dt_bias, a_log, skip_weight, b_proj, c_proj, doc_starts, grad_out
):
    nseq, nhead = lax.axis_size("seq"), lax.axis_size("head")
    tok, channels = x_quant.shape
    heads = dt_raw.shape[0]
    state = b_proj.shape[1]
    npair, piece = heads // 2, tok // nhead
    norm = 1.0 / math.sqrt(tok * nseq * HEAD_DIM)
    vmem = lambda *shape: pltpu.VMEM(shape, F32)
    half16 = lambda *shape: pltpu.VMEM(shape, BF16)
    dma = lambda n: pltpu.SemaphoreType.DMA((n,))
    sq = (tok, state)
    scratch = [
        half16(tok, channels), pltpu.VMEM(scale_exp.shape, jnp.int32), half16(heads, tok),
        half16(*sq), half16(*sq), half16(tok, channels),
        vmem(scale_exp.shape[0], tok),
        vmem(heads, tok), vmem(heads, tok), vmem(heads, tok),
        vmem(2, heads + 8, tok), vmem(2, *sq),
        vmem(2, npair, *sq), vmem(npair, *sq),
        vmem(*sq), vmem(*sq), vmem(2, *sq), vmem(*sq), vmem(2, *sq),
        half16(3, tok, 2 * state), half16(3, state, 2 * tok),
        vmem(npair, *sq), vmem(2, npair, *sq), vmem(npair, *sq),
        vmem(npair, *sq),
        half16(npair, 2 * tok, state), half16(2, npair, 2 * tok, state),
        vmem(npair, 4, *sq),
        vmem(npair, *sq), vmem(npair, *sq), vmem(npair, *sq), vmem(npair, *sq),
        vmem(*sq), vmem(tok, 2 * state), vmem(2, tok, 2 * state),
        vmem(2, npair, tok), vmem(npair, tok), vmem(heads, tok),
        vmem(2, *sq), vmem(1, *sq), vmem(heads, tok), vmem(heads, tok),
        vmem(nhead, 2, piece, state), vmem(nhead, piece, state),
        vmem(nhead, 2, piece, state), vmem(nhead, piece, state),
        vmem(nhead, 2, piece, state), vmem(nseq, 8, tok),
        dma(6), dma(2), dma(2), dma(npair), dma(npair), dma(npair), dma(npair), dma(npair), dma(npair),
        dma(2), dma(nhead), dma(nhead), dma(nhead), dma(nhead), dma(nhead), dma(nhead),
        dma(nseq), dma(nseq),
    ]
    whole = pl.BlockSpec(memory_space=pltpu.VMEM)
    return tuple(pl.pallas_call(
        functools.partial(kernel, nseq, nhead, norm),
        out_shape=(
            jax.ShapeDtypeStruct((tok, channels), BF16),
            jax.ShapeDtypeStruct((heads, tok), F32),
            jax.ShapeDtypeStruct((2, tok, state), F32),
            jax.ShapeDtypeStruct((2, heads), F32),
        ),
        in_specs=[pl.BlockSpec(memory_space=pl.ANY)] * 6 + [whole] * 3 + [pl.BlockSpec(memory_space=pltpu.SMEM)],
        out_specs=(whole,) * 4,
        scratch_shapes=scratch,
        compiler_params=pltpu.CompilerParams(
            collective_id=0, has_side_effects=True, vmem_limit_bytes=60 << 20
        ),
    )(
        x_quant, scale_exp, dt_raw, b_proj, c_proj, grad_out, dt_bias.reshape(1, heads),
        a_log.reshape(1, heads), skip_weight.reshape(1, heads), doc_starts,
    ))


def solution(mesh):
    in_specs = (
        P("seq", "head"),
        P("head", "seq"),
        P("head", "seq"),
        P("head"),
        P("head"),
        P("head"),
        P("seq", None),
        P("seq", None),
        P("seq", None),
        P("seq", "head"),
    )
    out_specs = (P("seq", "head"), P("head", "seq"), P(None, "seq", None), P(None, "head"))
    return jax.shard_map(local, mesh=mesh, in_specs=in_specs, out_specs=out_specs, check_vma=False)
```

```python
import functools
import math

import jax
import jax.numpy as jnp
from jax import lax
from jax.experimental import pallas as pl
from jax.experimental.pallas import tpu as pltpu
from jax.sharding import PartitionSpec as P

HEAD_DIM = 64
LAG = 3
MESH = pl.DeviceIdType.MESH
F32 = jnp.float32
BF16 = jnp.bfloat16
HIGHEST = lax.Precision.HIGHEST

ROWS = ((1,), (1,))
COLS = ((0,), (0,))
PLAIN = ((1,), (0,))


def mm(a, b, dims):
    return lax.dot_general(a, b, (dims, ((), ())), preferred_element_type=F32)


def split(a):
    high = a.astype(BF16)
    return high, (a - high.astype(F32)).astype(BF16)


def mm2(a, b, dims):
    high, low = split(a)
    return mm(high, b, dims) + mm(low, b, dims)


def mm2r(a, b, dims):
    high, low = split(b)
    return mm(a, high, dims) + mm(a, low, dims)


def kernel(
    nseq, nhead, norm,
    x_hbm, sc_hbm, dt_hbm, b_hbm, c_hbm, g_hbm, bias_ref, alog_ref, skip_ref, doc_ref,
    gx_out, dt_out, bc_out, hg_out,
    x_ref, sc_ref, dt_ref, b_ref, c_ref, g_ref,
    fac, steps, rates, skips, meta, cf, gg, xv, kern, same, first, last, cols,
    twice, turned, step_s, enter_s, exit_s, inner_s, xs_s, ge_s, loc, es, rs_, er, rr,
    kg, bx, cx, ends, skp, ct, ctf, ctc, sgc, far, near, own_out, oth_out, red_own, red_oth, gat, hgp,
    in_sems, c_sems, meta_sems, g_send, g_recv, e_send, e_recv, r_send, r_recv, far_sems,
    own_send, own_recv, oth_send, oth_recv, gat_send, gat_recv, hg_send, hg_recv,
):
    me, hd = lax.axis_index("seq"), lax.axis_index("head")
    par, z = lax.rem(me, 2), lax.div(me, 2)
    zs = nseq // 2
    oth = 1 - par
    partner = me + 1 - 2 * par
    tok = x_ref.shape[0]
    heads = dt_ref.shape[0]
    npair = heads // 2
    step_at = heads + 8

    fetches = [
        pltpu.make_async_copy(src, dst, in_sems.at[i])
        for i, (src, dst) in enumerate((
            (c_hbm, c_ref), (dt_hbm, dt_ref), (g_hbm, g_ref), (sc_hbm, sc_ref), (b_hbm, b_ref), (x_hbm, x_ref),
        ))
    ]
    for fetch in fetches:
        fetch.start()
    barrier = pltpu.get_barrier_semaphore()
    for j in range(1, nseq):
        pl.semaphore_signal(barrier, inc=1, device_id=(lax.rem(me + j, nseq), hd), device_id_type=MESH)
    for j in range(1, nhead):
        there = lax.rem(hd + j, nhead)
        pl.semaphore_signal(barrier, inc=1, device_id=(me, there), device_id_type=MESH)
        pl.semaphore_signal(barrier, inc=1, device_id=(partner, there), device_id_type=MESH)

    def remote(src, dst, send, recv, device):
        return pltpu.make_async_remote_copy(
            src_ref=src, dst_ref=dst, send_sem=send, recv_sem=recv,
            device_id=device, device_id_type=MESH,
        )

    across = (partner, hd)

    def c_copy(slab):
        return remote(cf.at[slab], cf.at[slab], c_sems.at[0], c_sems.at[1], across)

    def meta_copy(slab):
        return remote(meta.at[slab], meta.at[slab], meta_sems.at[0], meta_sems.at[1], across)

    def g_copy(slab, k):
        return remote(gg.at[slab, k], gg.at[slab, k], g_send.at[k], g_recv.at[k], across)

    def e_copy(k):
        return remote(es.at[k], er.at[k], e_send.at[k], e_recv.at[k], (lax.rem(me + 2, nseq), hd))

    def r_copy(k):
        return remote(rs_.at[k], rr.at[k], r_send.at[k], r_recv.at[k], (lax.rem(me + nseq - 2, nseq), hd))

    sub = lax.broadcasted_iota(jnp.int32, (heads, heads), 0)
    lane = lax.broadcasted_iota(jnp.int32, (heads, heads), 1)

    def column(ref):
        return jnp.sum(jnp.where(sub == lane, ref[...], 0.0), axis=1, keepdims=True)

    t_sub = lax.broadcasted_iota(jnp.int32, (tok, tok), 0)
    t_lane = lax.broadcasted_iota(jnp.int32, (tok, tok), 1)
    lane_a = t_lane < HEAD_DIM
    rate = jnp.exp(column(alog_ref))
    rates[...] = jnp.broadcast_to(rate, (heads, tok))
    skips[...] = jnp.broadcast_to(column(skip_ref), (heads, tok))
    row_id = lax.broadcasted_iota(jnp.int32, (8, tok), 1)
    count = jnp.zeros((8, tok), F32)
    for j in range(doc_ref.shape[1]):
        count = count + (row_id >= doc_ref[0, j]).astype(F32)
    bias = column(bias_ref)
    fetches[0].wait()
    cf[par] = c_ref[...].astype(F32)
    fetches[1].wait()
    pre = dt_ref[...].astype(F32) + bias
    step_all = jnp.maximum(pre, 0.0) + jnp.log1p(jnp.exp(-jnp.abs(pre)))
    steps[...] = step_all
    upper = (t_sub <= t_lane).astype(F32)
    meta[par, 0:heads] = lax.dot_general(
        -rate * step_all, upper, (PLAIN, ((), ())), precision=HIGHEST, preferred_element_type=F32
    )
    meta[par, heads:heads + 8] = count
    fetches[2].wait()

    pl.semaphore_wait(barrier, nseq - 1 + 2 * (nhead - 1))
    meta_copy(par).start()
    c_copy(par).start()

    def lanes_at(k):
        return pl.ds(pl.multiple_of(k * tok, tok), tok)

    def send_pair(k, carry):
        gg[par, k] = g_ref[:, lanes_at(k)].astype(F32)
        g_copy(par, k).start()
        return carry

    lax.fori_loop(0, npair, send_pair, 0)
    for fetch in fetches[3:]:
        fetch.wait()
    fac[...] = jnp.left_shift(jnp.int32(1), sc_ref[...] + 8).astype(F32) / 256.0
    kg[...] = jnp.zeros_like(kg)
    bx[...] = jnp.zeros_like(bx)
    cx[...] = jnp.zeros_like(cx)
    ctc[...] = jnp.zeros_like(ctc)
    ctf[...] = jnp.zeros_like(ctf)
    sgc[...] = jnp.zeros_like(sgc)

    @pl.when(z == 0)
    def _():
        er[...] = jnp.zeros_like(er)

    @pl.when(z == zs - 1)
    def _():
        rr[...] = jnp.zeros_like(rr)

    def row_of(q, row):
        return meta[q, pl.ds(row, 1), :]

    def prepare(q, rest):
        rows = jnp.concatenate([meta[q], rest], axis=0)
        flat = rows.T
        cols[q] = flat
        seg_col = jnp.broadcast_to(flat[:, heads:heads + 1], (tok, tok))
        first[q] = (seg_col == 0.0).astype(F32)
        whole = cf[q].astype(BF16)
        c_flat = cf[q].T.astype(BF16)
        twice[q] = jnp.concatenate([whole, whole], axis=1)
        turned[q] = jnp.concatenate([c_flat, c_flat], axis=1)
        return seg_col

    def enter_of(q, k):
        rolled = pltpu.roll(cols[q], lax.rem(tok - 2 * k, tok), 1)
        cum_cols = [jnp.broadcast_to(rolled[:, i:i + 1], (tok, tok)) for i in range(2)]
        cum = jnp.where(lane_a, cum_cols[0], cum_cols[1])
        enter_s[q, k] = jnp.exp(cum) * first[q]
        return rolled, cum_cols, cum

    seg_own = prepare(par, jnp.concatenate([steps[...], jnp.zeros((tok - 2 * heads - 8, tok), F32)], axis=0))
    seg_row = jnp.broadcast_to(meta[par, heads:heads + 1, :], (tok, tok))
    same[...] = ((t_sub <= t_lane) & (seg_row == seg_own)).astype(F32)
    last[...] = (seg_own == meta[par, heads:heads + 1, tok - 1:tok]).astype(F32)
    b_own = b_ref[...]
    b_flat = b_own.astype(F32).T.astype(BF16)
    twice[2] = jnp.concatenate([b_own, b_own], axis=1)
    turned[2] = jnp.concatenate([b_flat, b_flat], axis=1)
    kern[...] = mm(b_own, c_ref[...], ROWS)

    def decay_of(q, k):
        return enter_s[q, k, tok - 1:tok, :]

    def own_part(k):
        factor = jnp.broadcast_to(fac[pl.ds(k, 1), :], (tok, tok)).T
        x_val = x_ref[:, lanes_at(k)].astype(F32) * factor
        xv[k] = x_val
        rolled, cum_cols, cum = enter_of(par, k)
        step_cols = [jnp.broadcast_to(rolled[:, step_at + i:step_at + i + 1], (tok, tok)) for i in range(2)]
        step = jnp.where(lane_a, step_cols[0], step_cols[1])
        exit_w = jnp.exp(cum[tok - 1:tok, :] - cum) * last[...]
        step_s[k] = step
        exit_s[k] = exit_w
        xs_two = jnp.concatenate(split(exit_w * (step * x_val)), axis=0)
        xs_s[k] = xs_two
        own_state = mm(turned[2], xs_two, PLAIN)
        loc[k, 2] = own_state
        g_val = gg[par, k]
        ge_s[par, k] = jnp.concatenate(split(enter_s[par, k] * g_val), axis=0)
        g_two = jnp.concatenate(
            [jnp.where(lane_a, g_val, 0.0), jnp.where(lane_a, 0.0, g_val)], axis=0
        ).astype(BF16)
        scores = mm(x_val.astype(BF16), g_two, ROWS)
        mask = same[...] > 0.5
        kern_own = kern[...]
        total, highs, lows, flows = None, [], [], []
        for i in range(2):
            gap = row_of(par, 2 * k + i) - cum_cols[i]
            decay = jnp.exp(jnp.where(mask, gap, -1e30))
            part = scores[:, i * tok:(i + 1) * tok] * (decay * step_cols[i])
            high, low = split(decay * kern_own)
            highs.append(high)
            lows.append(low)
            flow = part * kern_own
            flows.append(flow)
            total = part if total is None else total + part
            ct[pl.ds(2 * k + i, 1), :] = jnp.sum(flow, axis=0, keepdims=True)
        kg[...] += total
        kept = ctf[...]
        for i in range(2):
            kept = jnp.where(t_lane == 2 * k + i, jnp.sum(flows[i], axis=1, keepdims=True), kept)
        ctf[...] = kept
        inner_s[k] = mm(
            jnp.concatenate(highs + lows, axis=1), jnp.concatenate([g_two, g_two], axis=0), PLAIN
        )
        skp[pl.ds(k, 1), :] = jnp.sum(g_val * x_val, axis=0, keepdims=True)

    def local_part(k):
        enter_of(oth, k)
        loc[k, 0] = jnp.where(par == 0, decay_of(1, k), 1.0) * loc[k, 2]
        ge_s[oth, k] = jnp.concatenate(split(enter_s[oth, k] * gg[oth, k]), axis=0)
        grads = [mm(turned[q], ge_s[q, k], PLAIN) for q in range(2)]
        loc[k, 1] = decay_of(0, k) * grads[1] + grads[0]
        loc[k, 3] = grads[1]

    def forward_part(k):
        @pl.when(z > 0)
        def _():
            e_copy(k).wait_recv()

        @pl.when(z < zs - 1)
        def _():
            es[k] = (decay_of(0, k) * decay_of(1, k)) * er[k] + loc[k, 0]
            e_copy(k).start()

    def backward_part(k):
        @pl.when(z < zs - 1)
        def _():
            r_copy(k).wait_recv()

        @pl.when(z > 0)
        def _():
            rs_[k] = (decay_of(0, k) * decay_of(1, k)) * rr[k] + loc[k, 1]
            r_copy(k).start()

    def wide(a):
        return jnp.concatenate([a[0:tok], a[tok:2 * tok]], axis=1)

    def corner(high, low):
        return jnp.concatenate(
            [jnp.concatenate([high, high], axis=1), jnp.concatenate([low, low], axis=1)], axis=0
        )

    def final_part(k):
        entry0, exit1 = er[k], rr[k]
        entry1 = decay_of(0, k) * entry0 + jnp.where(par == 0, loc[k, 2], 0.0)
        exit0 = decay_of(1, k) * exit1 + loc[k, 3]
        early = par == 0
        entry_own, entry_oth = jnp.where(early, entry0, entry1), jnp.where(early, entry1, entry0)
        leave_own, leave_oth = jnp.where(early, exit0, exit1), jnp.where(early, exit1, exit0)

        def entering(q, entry):
            high, low = split(entry)
            read = mm(twice[q], jnp.concatenate([high, low], axis=0), PLAIN)
            cx[q] += mm(wide(ge_s[q, k]), corner(high, low), ROWS)
            return (enter_s[q, k] * gg[q, k]) * read

        def place(cols_ref, q, full):
            kept = cols_ref[q]
            for i in range(2):
                part = jnp.where(lane_a if i == 0 else ~lane_a, full, 0.0)
                part_sum = jnp.sum(part, axis=1, keepdims=True)
                kept = kept + jnp.where(t_lane == 2 * k + i, part_sum, 0.0)
            cols_ref[q] = kept

        through = entering(oth, entry_oth)
        place(ctc, oth, through)
        ends[oth, pl.ds(k, 1), :] = jnp.sum(leave_oth * entry_oth, axis=0, keepdims=True) * decay_of(oth, k)

        x_val, g_val = xv[k], gg[par, k]
        exit_w, step = exit_s[k], step_s[k]
        l_high, l_low = split(leave_own)
        back = mm(twice[2], jnp.concatenate([l_high, l_low], axis=0), PLAIN)
        bx[...] += mm(wide(xs_s[k]), corner(l_high, l_low), ROWS)
        back_w = exit_w * back
        input_total = inner_s[k] + back_w
        exit_terms = (step * x_val) * back_w
        place(ctc, par, entering(par, entry_own) - exit_terms)
        place(sgc, 0, input_total * x_val)
        ends[par, pl.ds(k, 1), :] = (
            jnp.sum(exit_terms, axis=0, keepdims=True)
            + jnp.sum(leave_own * entry_own, axis=0, keepdims=True) * decay_of(par, k)
        )
        skip_rows = [skips[pl.ds(2 * k + i, 1), :] for i in range(2)]
        skip_lanes = jnp.where(lane_a[0:1], skip_rows[0], skip_rows[1])
        gx_out[:, lanes_at(k)] = (input_total * step + skip_lanes * g_val).astype(BF16)

    own_part(0)
    meta_copy(oth).wait_recv()
    c_copy(oth).wait_recv()
    prepare(oth, jnp.zeros((tok - heads - 8, tok), F32))
    delay = 1 + LAG * (zs - 1)

    def lap(i, carry):
        @pl.when(i < npair)
        def _():
            g_copy(oth, i).wait_recv()

        ahead = i - 1 - LAG * z

        @pl.when((ahead >= 0) & (ahead < npair))
        def _():
            forward_part(ahead)

        behind = i - 1 - LAG * (zs - 1 - z)

        @pl.when((behind >= 0) & (behind < npair))
        def _():
            backward_part(behind)

        @pl.when((i < npair - 1) & (i >= delay))
        def _():
            final_part(i - delay)
            local_part(i)
            own_part(i + 1)

        @pl.when((i < npair - 1) & (i < delay))
        def _():
            local_part(i)
            own_part(i + 1)

        @pl.when(i == npair - 1)
        def _():
            local_part(i)

        @pl.when((i >= npair - 1) & (i >= delay))
        def _():
            final_part(i - delay)

        return carry

    lax.fori_loop(0, npair + delay, lap, 0)

    def folded(a):
        return a[:, 0:tok] + a[:, tok:]

    piece = tok // nhead
    state = b_ref.shape[1]
    oth_out[...] = folded(cx[oth]).reshape(nhead, piece, state)

    def oth_copy(to, slot):
        return remote(oth_out.at[to], red_oth.at[slot], oth_send.at[to], oth_recv.at[slot], (partner, to))

    def own_copy(to, slot):
        return remote(own_out.at[to], red_own.at[slot], own_send.at[to], own_recv.at[slot], (me, to))

    for j in range(nhead):
        oth_copy(lax.rem(hd + j, nhead), hd).start()

    h_sub = lax.broadcasted_iota(jnp.int32, (heads, tok), 0)
    h_lane = lax.broadcasted_iota(jnp.int32, (heads, tok), 1)
    pick = lax.div(h_lane, HEAD_DIM) == lax.rem(h_sub, 2)

    def cumul_of(q):
        per_head = jnp.broadcast_to(ends[q][:, None, :], (npair, 2, tok)).reshape(heads, tok)
        ending = jnp.sum(jnp.where(pick, per_head, 0.0), axis=1, keepdims=True)
        return ctc[q].T[0:heads] + jnp.where(h_lane == tok - 1, ending, 0.0)

    far[...] = cumul_of(oth)
    far_copy = remote(far, near, far_sems.at[0], far_sems.at[1], across)
    far_copy.start()

    own_out[:, 0] = (mm2(kg[...], c_ref[...], PLAIN) + folded(bx[...])).reshape(nhead, piece, state)
    own_out[:, 1] = (mm2(kg[...], b_ref[...], COLS) + folded(cx[par])).reshape(nhead, piece, state)
    for j in range(1, nhead):
        own_copy(lax.rem(hd + j, nhead), hd).start()

    mine = ct[...] - ctf[...].T[0:heads] + cumul_of(par)
    lower = (t_sub >= t_lane).astype(F32)
    far_copy.wait_recv()
    decay_grad = lax.dot_general(
        mine + near[...], lower, (PLAIN, ((), ())), precision=HIGHEST, preferred_element_type=F32
    )
    step_all = steps[...]
    alog_sum = -jnp.sum(decay_grad * step_all * rates[...], axis=1, keepdims=True)
    alog_row = jnp.sum(jnp.where(h_sub == h_lane, alog_sum, 0.0), axis=0, keepdims=True)
    skip_all = skp[...]
    skip_a = jnp.sum(skip_all[:, 0:HEAD_DIM], axis=1, keepdims=True)
    skip_b = jnp.sum(skip_all[:, HEAD_DIM:], axis=1, keepdims=True)
    k_sub, k_lane = 2 * h_sub[0:npair], h_lane[0:npair]
    skip_row = jnp.sum(
        jnp.where(k_sub == k_lane, skip_a, 0.0) + jnp.where(k_sub + 1 == k_lane, skip_b, 0.0),
        axis=0, keepdims=True,
    )
    r_sub = lax.broadcasted_iota(jnp.int32, (8, tok), 0)
    hgp[me] = jnp.where(r_sub == 0, alog_row, jnp.where(r_sub == 1, skip_row, 0.0))

    def hg_copy(to, slot):
        return remote(hgp.at[slot], hgp.at[slot], hg_send.at[to], hg_recv.at[slot], (to, hd))

    for j in range(1, nseq):
        hg_copy(lax.rem(me + j, nseq), me).start()

    red_own[hd] = own_out[hd]
    for j in range(nhead):
        other = lax.rem(hd + j, nhead)
        oth_copy(other, other).wait_recv()
    for j in range(1, nhead):
        other = lax.rem(hd + j, nhead)
        own_copy(other, other).wait_recv()
    b_c = jnp.sum(red_own[...], axis=0)
    gat[hd, 0] = b_c[0]
    gat[hd, 1] = b_c[1] + jnp.sum(red_oth[...], axis=0)

    def gat_copy(to, slot):
        return remote(gat.at[slot], gat.at[slot], gat_send.at[to], gat_recv.at[slot], (me, to))

    for j in range(1, nhead):
        gat_copy(lax.rem(hd + j, nhead), hd).start()

    sigmoid = 1.0 / (1.0 + jnp.exp(-(dt_ref[...].astype(F32) + bias)))
    dt_out[...] = (sgc[0].T[0:heads] - rates[...] * decay_grad) * sigmoid
    for j in range(1, nseq):
        other = lax.rem(me + j, nseq)
        hg_copy(other, other).wait_recv()
    hg_out[...] = jnp.sum(hgp[...], axis=0)[0:2, 0:heads] * norm
    for j in range(1, nhead):
        other = lax.rem(hd + j, nhead)
        gat_copy(other, other).wait_recv()
    for i in range(2):
        bc_out[i] = gat[:, i].reshape(tok, state)

    meta_copy(par).wait_send()
    c_copy(par).wait_send()
    far_copy.wait_send()

    def drain(k, carry):
        g_copy(par, k).wait_send()

        @pl.when(z < zs - 1)
        def _():
            e_copy(k).wait_send()

        @pl.when(z > 0)
        def _():
            r_copy(k).wait_send()

        return carry

    lax.fori_loop(0, npair, drain, 0)
    for j in range(nhead):
        oth_copy(lax.rem(hd + j, nhead), hd).wait_send()
    for j in range(1, nhead):
        own_copy(lax.rem(hd + j, nhead), hd).wait_send()
        gat_copy(lax.rem(hd + j, nhead), hd).wait_send()
    for j in range(1, nseq):
        hg_copy(lax.rem(me + j, nseq), me).wait_send()


def publish(g_src, d_src, b_src, h_src, g_dst, d_dst, b_dst, h_dst, sems):
    copies = [
        pltpu.make_async_copy(src, dst, sems.at[i])
        for i, (src, dst) in enumerate(((g_src, g_dst), (b_src, b_dst), (d_src, d_dst), (h_src, h_dst)))
    ]
    for copy in copies:
        copy.start()
    for copy in copies:
        copy.wait()


def local(
    x_quant, scale_exp, dt_raw, dt_bias, a_log, skip_weight, b_proj, c_proj, doc_starts, grad_out
):
    nseq, nhead = lax.axis_size("seq"), lax.axis_size("head")
    tok, channels = x_quant.shape
    heads = dt_raw.shape[0]
    state = b_proj.shape[1]
    npair, piece = heads // 2, tok // nhead
    norm = 1.0 / math.sqrt(tok * nseq * HEAD_DIM)
    vmem = lambda *shape: pltpu.VMEM(shape, F32)
    half16 = lambda *shape: pltpu.VMEM(shape, BF16)
    dma = lambda n: pltpu.SemaphoreType.DMA((n,))
    sq = (tok, state)
    scratch = [
        half16(tok, channels), pltpu.VMEM(scale_exp.shape, jnp.int32), half16(heads, tok),
        half16(*sq), half16(*sq), half16(tok, channels),
        vmem(scale_exp.shape[0], tok),
        vmem(heads, tok), vmem(heads, tok), vmem(heads, tok),
        vmem(2, heads + 8, tok), vmem(2, *sq),
        vmem(2, npair, *sq), vmem(npair, *sq),
        vmem(*sq), vmem(*sq), vmem(2, *sq), vmem(*sq), vmem(2, *sq),
        half16(3, tok, 2 * state), half16(3, state, 2 * tok),
        vmem(npair, *sq), vmem(2, npair, *sq), vmem(npair, *sq),
        vmem(npair, *sq),
        half16(npair, 2 * tok, state), half16(2, npair, 2 * tok, state),
        vmem(npair, 4, *sq),
        vmem(npair, *sq), vmem(npair, *sq), vmem(npair, *sq), vmem(npair, *sq),
        vmem(*sq), vmem(tok, 2 * state), vmem(2, tok, 2 * state),
        vmem(2, npair, tok), vmem(npair, tok), vmem(heads, tok), vmem(*sq),
        vmem(2, *sq), vmem(1, *sq), vmem(heads, tok), vmem(heads, tok),
        vmem(nhead, 2, piece, state), vmem(nhead, piece, state),
        vmem(nhead, 2, piece, state), vmem(nhead, piece, state),
        vmem(nhead, 2, piece, state), vmem(nseq, 8, tok),
        dma(6), dma(2), dma(2), dma(npair), dma(npair), dma(npair), dma(npair), dma(npair), dma(npair),
        dma(2), dma(nhead), dma(nhead), dma(nhead), dma(nhead), dma(nhead), dma(nhead),
        dma(nseq), dma(nseq),
    ]
    whole = pl.BlockSpec(memory_space=pltpu.VMEM)
    shapes = (
        jax.ShapeDtypeStruct((tok, channels), BF16),
        jax.ShapeDtypeStruct((heads, tok), F32),
        jax.ShapeDtypeStruct((2, tok, state), F32),
        jax.ShapeDtypeStruct((2, heads), F32),
    )
    outs = pl.pallas_call(
        functools.partial(kernel, nseq, nhead, norm),
        out_shape=shapes,
        in_specs=[pl.BlockSpec(memory_space=pl.ANY)] * 6 + [whole] * 3 + [pl.BlockSpec(memory_space=pltpu.SMEM)],
        out_specs=(whole,) * 4,
        scratch_shapes=scratch,
        compiler_params=pltpu.CompilerParams(
            collective_id=0, has_side_effects=True, vmem_limit_bytes=60 << 20
        ),
    )(
        x_quant, scale_exp, dt_raw, b_proj, c_proj, grad_out, dt_bias.reshape(1, heads),
        a_log.reshape(1, heads), skip_weight.reshape(1, heads), doc_starts,
    )
    anywhere = pl.BlockSpec(memory_space=pl.ANY)
    return tuple(pl.pallas_call(
        publish,
        out_shape=shapes,
        in_specs=[anywhere] * 4,
        out_specs=(anywhere,) * 4,
        scratch_shapes=[dma(4)],
        compiler_params=pltpu.CompilerParams(vmem_limit_bytes=60 << 20),
    )(*outs))


def solution(mesh):
    in_specs = (
        P("seq", "head"),
        P("head", "seq"),
        P("head", "seq"),
        P("head"),
        P("head"),
        P("head"),
        P("seq", None),
        P("seq", None),
        P("seq", None),
        P("seq", "head"),
    )
    out_specs = (P("seq", "head"), P("head", "seq"), P(None, "seq", None), P(None, "head"))
    return jax.shard_map(local, mesh=mesh, in_specs=in_specs, out_specs=out_specs, check_vma=False)
```

```python
import functools
import math

import jax
import jax.numpy as jnp
from jax import lax
from jax.experimental import pallas as pl
from jax.experimental.pallas import tpu as pltpu
from jax.sharding import PartitionSpec as P

HEAD_DIM = 64
LAG = 4
MESH = pl.DeviceIdType.MESH
F32 = jnp.float32
BF16 = jnp.bfloat16
HIGHEST = lax.Precision.HIGHEST

ROWS = ((1,), (1,))
COLS = ((0,), (0,))
PLAIN = ((1,), (0,))


def mm(a, b, dims):
    return lax.dot_general(a, b, (dims, ((), ())), preferred_element_type=F32)


def split(a):
    high = a.astype(BF16)
    return high, (a - high.astype(F32)).astype(BF16)


def mm2(a, b, dims):
    high, low = split(a)
    return mm(high, b, dims) + mm(low, b, dims)


def mm2r(a, b, dims):
    high, low = split(b)
    return mm(a, high, dims) + mm(a, low, dims)


def kernel(
    nseq, nhead, norm,
    x_hbm, sc_hbm, dt_hbm, b_hbm, c_hbm, g_hbm, bias_ref, alog_ref, skip_ref, doc_ref,
    gx_out, dt_out, bc_out, hg_out,
    x_ref, sc_ref, dt_ref, b_ref, c_ref, g_ref,
    fac, steps, rates, skips, meta, cf, gg, xv, kern, same, first, last, cols,
    twice, turned, step_s, enter_s, exit_s, inner_s, xs_s, ge_s, loc, es, rs_, er, rr,
    kg, bx, cx, ends, skp, ct, ctc, sgc, kg_b, kg_c, far, near, own_out, oth_out, red_own, red_oth, gat, hgp,
    in_sems, c_sems, meta_sems, g_send, g_recv, e_send, e_recv, r_send, r_recv, far_sems,
    own_send, own_recv, oth_send, oth_recv, gat_send, gat_recv, hg_send, hg_recv,
):
    me, hd = lax.axis_index("seq"), lax.axis_index("head")
    par, z = lax.rem(me, 2), lax.div(me, 2)
    zs = nseq // 2
    oth = 1 - par
    partner = me + 1 - 2 * par
    tok = x_ref.shape[0]
    heads = dt_ref.shape[0]
    npair = heads // 2
    step_at = heads + 8

    fetches = [
        pltpu.make_async_copy(src, dst, in_sems.at[i])
        for i, (src, dst) in enumerate((
            (c_hbm, c_ref), (dt_hbm, dt_ref), (g_hbm, g_ref), (sc_hbm, sc_ref), (b_hbm, b_ref), (x_hbm, x_ref),
        ))
    ]
    for fetch in fetches:
        fetch.start()
    barrier = pltpu.get_barrier_semaphore()
    for j in range(1, nseq):
        pl.semaphore_signal(barrier, inc=1, device_id=(lax.rem(me + j, nseq), hd), device_id_type=MESH)
    for j in range(1, nhead):
        there = lax.rem(hd + j, nhead)
        pl.semaphore_signal(barrier, inc=1, device_id=(me, there), device_id_type=MESH)
        pl.semaphore_signal(barrier, inc=1, device_id=(partner, there), device_id_type=MESH)

    def remote(src, dst, send, recv, device):
        return pltpu.make_async_remote_copy(
            src_ref=src, dst_ref=dst, send_sem=send, recv_sem=recv,
            device_id=device, device_id_type=MESH,
        )

    across = (partner, hd)

    def c_copy(slab):
        return remote(cf.at[slab], cf.at[slab], c_sems.at[0], c_sems.at[1], across)

    def meta_copy(slab):
        return remote(meta.at[slab], meta.at[slab], meta_sems.at[0], meta_sems.at[1], across)

    def g_copy(slab, k):
        return remote(gg.at[slab, k], gg.at[slab, k], g_send.at[k], g_recv.at[k], across)

    def e_copy(k):
        return remote(es.at[k], er.at[k], e_send.at[k], e_recv.at[k], (lax.rem(me + 2, nseq), hd))

    def r_copy(k):
        return remote(rs_.at[k], rr.at[k], r_send.at[k], r_recv.at[k], (lax.rem(me + nseq - 2, nseq), hd))

    sub = lax.broadcasted_iota(jnp.int32, (heads, heads), 0)
    lane = lax.broadcasted_iota(jnp.int32, (heads, heads), 1)

    def column(ref):
        return jnp.sum(jnp.where(sub == lane, ref[...], 0.0), axis=1, keepdims=True)

    t_sub = lax.broadcasted_iota(jnp.int32, (tok, tok), 0)
    t_lane = lax.broadcasted_iota(jnp.int32, (tok, tok), 1)
    lane_a = t_lane < HEAD_DIM
    rate = jnp.exp(column(alog_ref))
    rates[...] = jnp.broadcast_to(rate, (heads, tok))
    skips[...] = jnp.broadcast_to(column(skip_ref), (heads, tok))
    row_id = lax.broadcasted_iota(jnp.int32, (8, tok), 1)
    count = jnp.zeros((8, tok), F32)
    for j in range(doc_ref.shape[1]):
        count = count + (row_id >= doc_ref[0, j]).astype(F32)
    bias = column(bias_ref)
    fetches[0].wait()
    cf[par] = c_ref[...].astype(F32)
    fetches[1].wait()
    pre = dt_ref[...].astype(F32) + bias
    step_all = jnp.maximum(pre, 0.0) + jnp.log1p(jnp.exp(-jnp.abs(pre)))
    steps[...] = step_all
    upper = (t_sub <= t_lane).astype(F32)
    meta[par, 0:heads] = lax.dot_general(
        -rate * step_all, upper, (PLAIN, ((), ())), precision=HIGHEST, preferred_element_type=F32
    )
    meta[par, heads:heads + 8] = count
    fetches[2].wait()

    pl.semaphore_wait(barrier, nseq - 1 + 2 * (nhead - 1))
    meta_copy(par).start()
    c_copy(par).start()

    def lanes_at(k):
        return pl.ds(pl.multiple_of(k * tok, tok), tok)

    def send_pair(k, carry):
        gg[par, k] = g_ref[:, lanes_at(k)].astype(F32)
        g_copy(par, k).start()
        return carry

    lax.fori_loop(0, npair, send_pair, 0)
    for fetch in fetches[3:]:
        fetch.wait()
    fac[...] = jnp.left_shift(jnp.int32(1), sc_ref[...] + 8).astype(F32) / 256.0
    kg[...] = jnp.zeros_like(kg)
    bx[...] = jnp.zeros_like(bx)
    cx[...] = jnp.zeros_like(cx)

    @pl.when(z == 0)
    def _():
        er[...] = jnp.zeros_like(er)

    @pl.when(z == zs - 1)
    def _():
        rr[...] = jnp.zeros_like(rr)

    def row_of(q, row):
        return meta[q, pl.ds(row, 1), :]

    def prepare(q, rest):
        rows = jnp.concatenate([meta[q], rest], axis=0)
        flat = rows.T
        cols[q] = flat
        seg_col = jnp.broadcast_to(flat[:, heads:heads + 1], (tok, tok))
        first[q] = (seg_col == 0.0).astype(F32)
        whole = cf[q].astype(BF16)
        c_flat = cf[q].T.astype(BF16)
        twice[q] = jnp.concatenate([whole, whole], axis=1)
        turned[q] = jnp.concatenate([c_flat, c_flat], axis=1)
        return seg_col

    def enter_of(q, k):
        rolled = pltpu.roll(cols[q], lax.rem(tok - 2 * k, tok), 1)
        cum_cols = [jnp.broadcast_to(rolled[:, i:i + 1], (tok, tok)) for i in range(2)]
        cum = jnp.where(lane_a, cum_cols[0], cum_cols[1])
        enter_s[q, k] = jnp.exp(cum) * first[q]
        return rolled, cum_cols, cum

    seg_own = prepare(par, jnp.concatenate([steps[...], jnp.zeros((tok - 2 * heads - 8, tok), F32)], axis=0))
    seg_row = jnp.broadcast_to(meta[par, heads:heads + 1, :], (tok, tok))
    same[...] = ((t_sub <= t_lane) & (seg_row == seg_own)).astype(F32)
    last[...] = (seg_own == meta[par, heads:heads + 1, tok - 1:tok]).astype(F32)
    b_own = b_ref[...]
    b_flat = b_own.astype(F32).T.astype(BF16)
    twice[2] = jnp.concatenate([b_own, b_own], axis=1)
    turned[2] = jnp.concatenate([b_flat, b_flat], axis=1)
    kern[...] = mm(b_own, c_ref[...], ROWS)

    def decay_of(q, k):
        return enter_s[q, k, tok - 1:tok, :]

    w_sub = lax.broadcasted_iota(jnp.int32, (8, 2 * tok), 0)
    w_half = lax.div(lax.rem(lax.broadcasted_iota(jnp.int32, (8, 2 * tok), 1), tok), HEAD_DIM)
    ones_half = (w_sub == w_half).astype(F32).astype(BF16)
    ones_all = jnp.ones((8, 2 * tok), BF16)

    def lane_sums(pattern, parts):
        rows = jnp.concatenate([jnp.concatenate(split(part), axis=1) for part in parts], axis=0)
        return mm(pattern, rows, ROWS)

    def own_part(k):
        factor = jnp.broadcast_to(fac[pl.ds(k, 1), :], (tok, tok)).T
        x_val = x_ref[:, lanes_at(k)].astype(F32) * factor
        xv[k] = x_val
        rolled, cum_cols, cum = enter_of(par, k)
        step_cols = [jnp.broadcast_to(rolled[:, step_at + i:step_at + i + 1], (tok, tok)) for i in range(2)]
        step = jnp.where(lane_a, step_cols[0], step_cols[1])
        exit_w = jnp.exp(cum[tok - 1:tok, :] - cum) * last[...]
        step_s[k] = step
        exit_s[k] = exit_w
        xs_two = jnp.concatenate(split(exit_w * (step * x_val)), axis=0)
        xs_s[k] = xs_two
        own_state = mm(turned[2], xs_two, PLAIN)
        loc[k, 2] = own_state
        g_val = gg[par, k]
        ge_s[par, k] = jnp.concatenate(split(enter_s[par, k] * g_val), axis=0)
        g_two = jnp.concatenate(
            [jnp.where(lane_a, g_val, 0.0), jnp.where(lane_a, 0.0, g_val)], axis=0
        ).astype(BF16)
        scores = mm(x_val.astype(BF16), g_two, ROWS)
        mask = same[...] > 0.5
        kern_own = kern[...]
        total, highs, lows, flows = None, [], [], []
        for i in range(2):
            gap = row_of(par, 2 * k + i) - cum_cols[i]
            decay = jnp.exp(jnp.where(mask, gap, -1e30))
            part = scores[:, i * tok:(i + 1) * tok] * (decay * step_cols[i])
            high, low = split(decay * kern_own)
            highs.append(high)
            lows.append(low)
            flow = part * kern_own
            flows.append(flow)
            total = part if total is None else total + part
        kg[...] += total
        across_t = lane_sums(ones_all, flows)
        for i in range(2):
            ct[pl.ds(2 * k + i, 1), :] = (
                jnp.sum(flows[i], axis=0, keepdims=True) - across_t[0:1, i * tok:(i + 1) * tok]
            )
        inner_s[k] = mm(
            jnp.concatenate(highs + lows, axis=1), jnp.concatenate([g_two, g_two], axis=0), PLAIN
        )
        skp[pl.ds(k, 1), :] = jnp.sum(g_val * x_val, axis=0, keepdims=True)

    def local_part(k):
        enter_of(oth, k)
        loc[k, 0] = jnp.where(par == 0, decay_of(1, k), 1.0) * loc[k, 2]
        ge_s[oth, k] = jnp.concatenate(split(enter_s[oth, k] * gg[oth, k]), axis=0)
        grads = [mm(turned[q], ge_s[q, k], PLAIN) for q in range(2)]
        loc[k, 1] = decay_of(0, k) * grads[1] + grads[0]
        loc[k, 3] = grads[1]

    def forward_part(k):
        @pl.when(z > 0)
        def _():
            e_copy(k).wait_recv()

        @pl.when(z < zs - 1)
        def _():
            es[k] = (decay_of(0, k) * decay_of(1, k)) * er[k] + loc[k, 0]
            e_copy(k).start()

    def backward_part(k):
        @pl.when(z < zs - 1)
        def _():
            r_copy(k).wait_recv()

        @pl.when(z > 0)
        def _():
            rs_[k] = (decay_of(0, k) * decay_of(1, k)) * rr[k] + loc[k, 1]
            r_copy(k).start()

    def wide(a):
        return jnp.concatenate([a[0:tok], a[tok:2 * tok]], axis=1)

    def corner(high, low):
        return jnp.concatenate(
            [jnp.concatenate([high, high], axis=1), jnp.concatenate([low, low], axis=1)], axis=0
        )

    def final_part(k):
        entry0, exit1 = er[k], rr[k]
        entry1 = decay_of(0, k) * entry0 + jnp.where(par == 0, loc[k, 2], 0.0)
        exit0 = decay_of(1, k) * exit1 + loc[k, 3]
        early = par == 0
        entry_own, entry_oth = jnp.where(early, entry0, entry1), jnp.where(early, entry1, entry0)
        leave_own, leave_oth = jnp.where(early, exit0, exit1), jnp.where(early, exit1, exit0)

        def entering(q, entry):
            high, low = split(entry)
            read = mm(twice[q], jnp.concatenate([high, low], axis=0), PLAIN)
            cx[q] += mm(wide(ge_s[q, k]), corner(high, low), ROWS)
            return (enter_s[q, k] * gg[q, k]) * read

        through = entering(oth, entry_oth)
        ends[oth, pl.ds(k, 1), :] = jnp.sum(leave_oth * entry_oth, axis=0, keepdims=True) * decay_of(oth, k)

        x_val, g_val = xv[k], gg[par, k]
        exit_w, step = exit_s[k], step_s[k]
        l_high, l_low = split(leave_own)
        back = mm(twice[2], jnp.concatenate([l_high, l_low], axis=0), PLAIN)
        bx[...] += mm(wide(xs_s[k]), corner(l_high, l_low), ROWS)
        back_w = exit_w * back
        input_total = inner_s[k] + back_w
        exit_terms = (step * x_val) * back_w
        sums = lane_sums(ones_half, [
            through, entering(par, entry_own) - exit_terms, input_total * x_val
        ])
        for i in range(2):
            ctc[oth, pl.ds(2 * k + i, 1), :] = sums[i:i + 1, 0:tok]
            ctc[par, pl.ds(2 * k + i, 1), :] = sums[i:i + 1, tok:2 * tok]
            sgc[pl.ds(2 * k + i, 1), :] = sums[i:i + 1, 2 * tok:3 * tok]
        ends[par, pl.ds(k, 1), :] = (
            jnp.sum(exit_terms, axis=0, keepdims=True)
            + jnp.sum(leave_own * entry_own, axis=0, keepdims=True) * decay_of(par, k)
        )
        skip_rows = [skips[pl.ds(2 * k + i, 1), :] for i in range(2)]
        skip_lanes = jnp.where(lane_a[0:1], skip_rows[0], skip_rows[1])
        gx_out[:, lanes_at(k)] = (input_total * step + skip_lanes * g_val).astype(BF16)

    own_part(0)
    meta_copy(oth).wait_recv()
    c_copy(oth).wait_recv()
    prepare(oth, jnp.zeros((tok - heads - 8, tok), F32))
    delay = 1 + LAG * (zs - 1)

    def lap(i, carry):
        @pl.when(i < npair)
        def _():
            g_copy(oth, i).wait_recv()

        ahead = i - 1 - LAG * z

        @pl.when((ahead >= 0) & (ahead < npair))
        def _():
            forward_part(ahead)

        behind = i - 1 - LAG * (zs - 1 - z)

        @pl.when((behind >= 0) & (behind < npair))
        def _():
            backward_part(behind)

        @pl.when((i < npair - 1) & (i >= delay))
        def _():
            final_part(i - delay)
            local_part(i)
            own_part(i + 1)

        @pl.when((i < npair - 1) & (i < delay))
        def _():
            local_part(i)
            own_part(i + 1)

        @pl.when(i == npair - 1)
        def _():
            local_part(i)
            kg_b[...] = mm2(kg[...], c_ref[...], PLAIN)
            kg_c[...] = mm2(kg[...], b_ref[...], COLS)

        @pl.when((i >= npair - 1) & (i >= delay))
        def _():
            final_part(i - delay)

        return carry

    lax.fori_loop(0, npair + delay, lap, 0)

    def folded(a):
        return a[:, 0:tok] + a[:, tok:]

    piece = tok // nhead
    state = b_ref.shape[1]
    oth_out[...] = folded(cx[oth]).reshape(nhead, piece, state)

    def oth_copy(to, slot):
        return remote(oth_out.at[to], red_oth.at[slot], oth_send.at[to], oth_recv.at[slot], (partner, to))

    def own_copy(to, slot):
        return remote(own_out.at[to], red_own.at[slot], own_send.at[to], own_recv.at[slot], (me, to))

    for j in range(nhead):
        oth_copy(lax.rem(hd + j, nhead), hd).start()

    h_sub = lax.broadcasted_iota(jnp.int32, (heads, tok), 0)
    h_lane = lax.broadcasted_iota(jnp.int32, (heads, tok), 1)
    pick = lax.div(h_lane, HEAD_DIM) == lax.rem(h_sub, 2)

    def cumul_of(q):
        per_head = jnp.broadcast_to(ends[q][:, None, :], (npair, 2, tok)).reshape(heads, tok)
        ending = jnp.sum(jnp.where(pick, per_head, 0.0), axis=1, keepdims=True)
        return ctc[q] + jnp.where(h_lane == tok - 1, ending, 0.0)

    far[...] = cumul_of(oth)
    far_copy = remote(far, near, far_sems.at[0], far_sems.at[1], across)
    far_copy.start()

    own_out[:, 0] = (kg_b[...] + folded(bx[...])).reshape(nhead, piece, state)
    own_out[:, 1] = (kg_c[...] + folded(cx[par])).reshape(nhead, piece, state)
    for j in range(1, nhead):
        own_copy(lax.rem(hd + j, nhead), hd).start()

    mine = ct[...] + cumul_of(par)
    lower = (t_sub >= t_lane).astype(F32)
    far_copy.wait_recv()
    decay_grad = lax.dot_general(
        mine + near[...], lower, (PLAIN, ((), ())), precision=HIGHEST, preferred_element_type=F32
    )
    step_all = steps[...]
    alog_sum = -jnp.sum(decay_grad * step_all * rates[...], axis=1, keepdims=True)
    alog_row = jnp.sum(jnp.where(h_sub == h_lane, alog_sum, 0.0), axis=0, keepdims=True)
    skip_all = skp[...]
    skip_a = jnp.sum(skip_all[:, 0:HEAD_DIM], axis=1, keepdims=True)
    skip_b = jnp.sum(skip_all[:, HEAD_DIM:], axis=1, keepdims=True)
    k_sub, k_lane = 2 * h_sub[0:npair], h_lane[0:npair]
    skip_row = jnp.sum(
        jnp.where(k_sub == k_lane, skip_a, 0.0) + jnp.where(k_sub + 1 == k_lane, skip_b, 0.0),
        axis=0, keepdims=True,
    )
    r_sub = lax.broadcasted_iota(jnp.int32, (8, tok), 0)
    hgp[me] = jnp.where(r_sub == 0, alog_row, jnp.where(r_sub == 1, skip_row, 0.0))

    def hg_copy(to, slot):
        return remote(hgp.at[slot], hgp.at[slot], hg_send.at[to], hg_recv.at[slot], (to, hd))

    for j in range(1, nseq):
        hg_copy(lax.rem(me + j, nseq), me).start()

    red_own[hd] = own_out[hd]
    for j in range(nhead):
        other = lax.rem(hd + j, nhead)
        oth_copy(other, other).wait_recv()
    for j in range(1, nhead):
        other = lax.rem(hd + j, nhead)
        own_copy(other, other).wait_recv()
    b_c = jnp.sum(red_own[...], axis=0)
    gat[hd, 0] = b_c[0]
    gat[hd, 1] = b_c[1] + jnp.sum(red_oth[...], axis=0)

    def gat_copy(to, slot):
        return remote(gat.at[slot], gat.at[slot], gat_send.at[to], gat_recv.at[slot], (me, to))

    for j in range(1, nhead):
        gat_copy(lax.rem(hd + j, nhead), hd).start()

    sigmoid = 1.0 / (1.0 + jnp.exp(-(dt_ref[...].astype(F32) + bias)))
    dt_out[...] = (sgc[...] - rates[...] * decay_grad) * sigmoid
    for j in range(1, nseq):
        other = lax.rem(me + j, nseq)
        hg_copy(other, other).wait_recv()
    hg_out[...] = jnp.sum(hgp[...], axis=0)[0:2, 0:heads] * norm
    for j in range(1, nhead):
        other = lax.rem(hd + j, nhead)
        gat_copy(other, other).wait_recv()
    for i in range(2):
        bc_out[i] = gat[:, i].reshape(tok, state)

    meta_copy(par).wait_send()
    c_copy(par).wait_send()
    far_copy.wait_send()

    def drain(k, carry):
        g_copy(par, k).wait_send()

        @pl.when(z < zs - 1)
        def _():
            e_copy(k).wait_send()

        @pl.when(z > 0)
        def _():
            r_copy(k).wait_send()

        return carry

    lax.fori_loop(0, npair, drain, 0)
    for j in range(nhead):
        oth_copy(lax.rem(hd + j, nhead), hd).wait_send()
    for j in range(1, nhead):
        own_copy(lax.rem(hd + j, nhead), hd).wait_send()
        gat_copy(lax.rem(hd + j, nhead), hd).wait_send()
    for j in range(1, nseq):
        hg_copy(lax.rem(me + j, nseq), me).wait_send()


def publish(g_src, b_src, d_src, h_src, g_dst, b_dst, d_dst, h_dst, g_mid, b_mid, d_mid, h_mid, arrive, leave):
    rows = g_src.shape[0] // 2
    triples = [(g_src.at[pl.ds(i * rows, rows)], g_mid.at[pl.ds(i * rows, rows)], g_dst.at[pl.ds(i * rows, rows)])
               for i in range(2)]
    triples += [(b_src, b_mid, b_dst), (d_src, d_mid, d_dst), (h_src, h_mid, h_dst)]
    first = [pltpu.make_async_copy(a, b, arrive.at[i]) for i, (a, b, c) in enumerate(triples)]
    second = [pltpu.make_async_copy(b, c, leave.at[i]) for i, (a, b, c) in enumerate(triples)]
    for copy in first:
        copy.start()
    for one, two in zip(first, second):
        one.wait()
        two.start()
    for copy in second:
        copy.wait()


def local(
    x_quant, scale_exp, dt_raw, dt_bias, a_log, skip_weight, b_proj, c_proj, doc_starts, grad_out
):
    nseq, nhead = lax.axis_size("seq"), lax.axis_size("head")
    tok, channels = x_quant.shape
    heads = dt_raw.shape[0]
    state = b_proj.shape[1]
    npair, piece = heads // 2, tok // nhead
    norm = 1.0 / math.sqrt(tok * nseq * HEAD_DIM)
    vmem = lambda *shape: pltpu.VMEM(shape, F32)
    half16 = lambda *shape: pltpu.VMEM(shape, BF16)
    dma = lambda n: pltpu.SemaphoreType.DMA((n,))
    sq = (tok, state)
    scratch = [
        half16(tok, channels), pltpu.VMEM(scale_exp.shape, jnp.int32), half16(heads, tok),
        half16(*sq), half16(*sq), half16(tok, channels),
        vmem(scale_exp.shape[0], tok),
        vmem(heads, tok), vmem(heads, tok), vmem(heads, tok),
        vmem(2, heads + 8, tok), vmem(2, *sq),
        vmem(2, npair, *sq), vmem(npair, *sq),
        vmem(*sq), vmem(*sq), vmem(2, *sq), vmem(*sq), vmem(2, *sq),
        half16(3, tok, 2 * state), half16(3, state, 2 * tok),
        vmem(npair, *sq), vmem(2, npair, *sq), vmem(npair, *sq),
        vmem(npair, *sq),
        half16(npair, 2 * tok, state), half16(2, npair, 2 * tok, state),
        vmem(npair, 4, *sq),
        vmem(npair, *sq), vmem(npair, *sq), vmem(npair, *sq), vmem(npair, *sq),
        vmem(*sq), vmem(tok, 2 * state), vmem(2, tok, 2 * state),
        vmem(2, npair, tok), vmem(npair, tok), vmem(heads, tok),
        vmem(2, heads, tok), vmem(heads, tok), vmem(*sq), vmem(*sq),
        vmem(heads, tok), vmem(heads, tok),
        vmem(nhead, 2, piece, state), vmem(nhead, piece, state),
        vmem(nhead, 2, piece, state), vmem(nhead, piece, state),
        vmem(nhead, 2, piece, state), vmem(nseq, 8, tok),
        dma(6), dma(2), dma(2), dma(npair), dma(npair), dma(npair), dma(npair), dma(npair), dma(npair),
        dma(2), dma(nhead), dma(nhead), dma(nhead), dma(nhead), dma(nhead), dma(nhead),
        dma(nseq), dma(nseq),
    ]
    whole = pl.BlockSpec(memory_space=pltpu.VMEM)
    shapes = (
        jax.ShapeDtypeStruct((tok, channels), BF16),
        jax.ShapeDtypeStruct((heads, tok), F32),
        jax.ShapeDtypeStruct((2, tok, state), F32),
        jax.ShapeDtypeStruct((2, heads), F32),
    )
    outs = pl.pallas_call(
        functools.partial(kernel, nseq, nhead, norm),
        out_shape=shapes,
        in_specs=[pl.BlockSpec(memory_space=pl.ANY)] * 6 + [whole] * 3 + [pl.BlockSpec(memory_space=pltpu.SMEM)],
        out_specs=(whole,) * 4,
        scratch_shapes=scratch,
        compiler_params=pltpu.CompilerParams(
            collective_id=0, has_side_effects=True, vmem_limit_bytes=60 << 20
        ),
    )(
        x_quant, scale_exp, dt_raw, b_proj, c_proj, grad_out, dt_bias.reshape(1, heads),
        a_log.reshape(1, heads), skip_weight.reshape(1, heads), doc_starts,
    )
    anywhere = pl.BlockSpec(memory_space=pl.ANY)
    order = (0, 2, 1, 3)
    given = pl.pallas_call(
        publish,
        out_shape=tuple(shapes[i] for i in order),
        in_specs=[anywhere] * 4,
        out_specs=(anywhere,) * 4,
        scratch_shapes=[pltpu.VMEM(shapes[i].shape, shapes[i].dtype) for i in order] + [dma(5), dma(5)],
        compiler_params=pltpu.CompilerParams(vmem_limit_bytes=60 << 20),
    )(*(outs[i] for i in order))
    return tuple(given[i] for i in order)


def solution(mesh):
    in_specs = (
        P("seq", "head"),
        P("head", "seq"),
        P("head", "seq"),
        P("head"),
        P("head"),
        P("head"),
        P("seq", None),
        P("seq", None),
        P("seq", None),
        P("seq", "head"),
    )
    out_specs = (P("seq", "head"), P("head", "seq"), P(None, "seq", None), P(None, "head"))
    return jax.shard_map(local, mesh=mesh, in_specs=in_specs, out_specs=out_specs, check_vma=False)
```

```python
import functools
import math

import jax
import jax.numpy as jnp
from jax import lax
from jax.experimental import pallas as pl
from jax.experimental.pallas import tpu as pltpu
from jax.sharding import PartitionSpec as P

HEAD_DIM = 64
LAG = 3
MESH = pl.DeviceIdType.MESH
F32 = jnp.float32
BF16 = jnp.bfloat16
HIGHEST = lax.Precision.HIGHEST

ROWS = ((1,), (1,))
COLS = ((0,), (0,))
PLAIN = ((1,), (0,))


def mm(a, b, dims):
    return lax.dot_general(a, b, (dims, ((), ())), preferred_element_type=F32)


def split(a):
    high = a.astype(BF16)
    return high, (a - high.astype(F32)).astype(BF16)


def mm2(a, b, dims):
    high, low = split(a)
    return mm(high, b, dims) + mm(low, b, dims)


def mm2r(a, b, dims):
    high, low = split(b)
    return mm(a, high, dims) + mm(a, low, dims)


def kernel(
    nseq, nhead, norm,
    x_hbm, sc_hbm, dt_hbm, b_hbm, c_hbm, g_hbm, bias_ref, alog_ref, skip_ref, doc_ref,
    gx_out, dt_out, bc_out, hg_out,
    x_ref, sc_ref, dt_ref, b_ref, c_ref, g_ref,
    fac, steps, rates, skips, meta, cf, gg, xv, kern, same, first, last, cols,
    twice, turned, step_s, enter_s, exit_s, inner_s, xs_s, ge_s, loc, es, rs_, er, rr,
    kg, bx, cx, ends, skp, ct, ctf, ctc, sgc, kg_b, kg_c, far, near, own_out, oth_out, red_own, red_oth, gat, hgp,
    in_sems, c_sems, meta_sems, g_send, g_recv, e_send, e_recv, r_send, r_recv, far_sems,
    own_send, own_recv, oth_send, oth_recv, gat_send, gat_recv, hg_send, hg_recv,
):
    me, hd = lax.axis_index("seq"), lax.axis_index("head")
    par, z = lax.rem(me, 2), lax.div(me, 2)
    zs = nseq // 2
    oth = 1 - par
    partner = me + 1 - 2 * par
    tok = x_ref.shape[0]
    heads = dt_ref.shape[0]
    npair = heads // 2
    step_at = heads + 8

    fetches = [
        pltpu.make_async_copy(src, dst, in_sems.at[i])
        for i, (src, dst) in enumerate((
            (c_hbm, c_ref), (dt_hbm, dt_ref), (g_hbm, g_ref), (sc_hbm, sc_ref), (b_hbm, b_ref), (x_hbm, x_ref),
        ))
    ]
    for fetch in fetches:
        fetch.start()
    barrier = pltpu.get_barrier_semaphore()
    for j in range(1, nseq):
        pl.semaphore_signal(barrier, inc=1, device_id=(lax.rem(me + j, nseq), hd), device_id_type=MESH)
    for j in range(1, nhead):
        there = lax.rem(hd + j, nhead)
        pl.semaphore_signal(barrier, inc=1, device_id=(me, there), device_id_type=MESH)
        pl.semaphore_signal(barrier, inc=1, device_id=(partner, there), device_id_type=MESH)

    def remote(src, dst, send, recv, device):
        return pltpu.make_async_remote_copy(
            src_ref=src, dst_ref=dst, send_sem=send, recv_sem=recv,
            device_id=device, device_id_type=MESH,
        )

    across = (partner, hd)

    def c_copy(slab):
        return remote(cf.at[slab], cf.at[slab], c_sems.at[0], c_sems.at[1], across)

    def meta_copy(slab):
        return remote(meta.at[slab], meta.at[slab], meta_sems.at[0], meta_sems.at[1], across)

    def g_copy(slab, k):
        return remote(gg.at[slab, k], gg.at[slab, k], g_send.at[k], g_recv.at[k], across)

    def e_copy(k):
        return remote(es.at[k], er.at[k], e_send.at[k], e_recv.at[k], (lax.rem(me + 2, nseq), hd))

    def r_copy(k):
        return remote(rs_.at[k], rr.at[k], r_send.at[k], r_recv.at[k], (lax.rem(me + nseq - 2, nseq), hd))

    sub = lax.broadcasted_iota(jnp.int32, (heads, heads), 0)
    lane = lax.broadcasted_iota(jnp.int32, (heads, heads), 1)

    def column(ref):
        return jnp.sum(jnp.where(sub == lane, ref[...], 0.0), axis=1, keepdims=True)

    t_sub = lax.broadcasted_iota(jnp.int32, (tok, tok), 0)
    t_lane = lax.broadcasted_iota(jnp.int32, (tok, tok), 1)
    lane_a = t_lane < HEAD_DIM
    rate = jnp.exp(column(alog_ref))
    rates[...] = jnp.broadcast_to(rate, (heads, tok))
    skips[...] = jnp.broadcast_to(column(skip_ref), (heads, tok))
    row_id = lax.broadcasted_iota(jnp.int32, (8, tok), 1)
    count = jnp.zeros((8, tok), F32)
    for j in range(doc_ref.shape[1]):
        count = count + (row_id >= doc_ref[0, j]).astype(F32)
    bias = column(bias_ref)
    fetches[0].wait()
    cf[par] = c_ref[...].astype(F32)
    fetches[1].wait()
    pre = dt_ref[...].astype(F32) + bias
    step_all = jnp.maximum(pre, 0.0) + jnp.log1p(jnp.exp(-jnp.abs(pre)))
    steps[...] = step_all
    upper = (t_sub <= t_lane).astype(F32)
    meta[par, 0:heads] = lax.dot_general(
        -rate * step_all, upper, (PLAIN, ((), ())), precision=HIGHEST, preferred_element_type=F32
    )
    meta[par, heads:heads + 8] = count
    fetches[2].wait()

    pl.semaphore_wait(barrier, nseq - 1 + 2 * (nhead - 1))
    meta_copy(par).start()
    c_copy(par).start()

    def lanes_at(k):
        return pl.ds(pl.multiple_of(k * tok, tok), tok)

    def send_pair(k, carry):
        gg[par, k] = g_ref[:, lanes_at(k)].astype(F32)
        g_copy(par, k).start()
        return carry

    lax.fori_loop(0, npair, send_pair, 0)
    for fetch in fetches[3:]:
        fetch.wait()
    fac[...] = jnp.left_shift(jnp.int32(1), sc_ref[...] + 8).astype(F32) / 256.0
    kg[...] = jnp.zeros_like(kg)
    bx[...] = jnp.zeros_like(bx)
    cx[...] = jnp.zeros_like(cx)
    ctc[...] = jnp.zeros_like(ctc)
    ctf[...] = jnp.zeros_like(ctf)
    sgc[...] = jnp.zeros_like(sgc)

    @pl.when(z == 0)
    def _():
        er[...] = jnp.zeros_like(er)

    @pl.when(z == zs - 1)
    def _():
        rr[...] = jnp.zeros_like(rr)

    def row_of(q, row):
        return meta[q, pl.ds(row, 1), :]

    def prepare(q, rest):
        rows = jnp.concatenate([meta[q], rest], axis=0)
        flat = rows.T
        cols[q] = flat
        seg_col = jnp.broadcast_to(flat[:, heads:heads + 1], (tok, tok))
        first[q] = (seg_col == 0.0).astype(F32)
        whole = cf[q].astype(BF16)
        c_flat = cf[q].T.astype(BF16)
        twice[q] = jnp.concatenate([whole, whole], axis=1)
        turned[q] = jnp.concatenate([c_flat, c_flat], axis=1)
        return seg_col

    def enter_of(q, k):
        rolled = pltpu.roll(cols[q], lax.rem(tok - 2 * k, tok), 1)
        cum_cols = [jnp.broadcast_to(rolled[:, i:i + 1], (tok, tok)) for i in range(2)]
        cum = jnp.where(lane_a, cum_cols[0], cum_cols[1])
        enter_s[q, k] = jnp.exp(cum) * first[q]
        return rolled, cum_cols, cum

    seg_own = prepare(par, jnp.concatenate([steps[...], jnp.zeros((tok - 2 * heads - 8, tok), F32)], axis=0))
    seg_row = jnp.broadcast_to(meta[par, heads:heads + 1, :], (tok, tok))
    same[...] = ((t_sub <= t_lane) & (seg_row == seg_own)).astype(F32)
    last[...] = (seg_own == meta[par, heads:heads + 1, tok - 1:tok]).astype(F32)
    b_own = b_ref[...]
    b_flat = b_own.astype(F32).T.astype(BF16)
    twice[2] = jnp.concatenate([b_own, b_own], axis=1)
    turned[2] = jnp.concatenate([b_flat, b_flat], axis=1)
    kern[...] = mm(b_own, c_ref[...], ROWS)

    def decay_of(q, k):
        return enter_s[q, k, tok - 1:tok, :]

    def own_part(k):
        factor = jnp.broadcast_to(fac[pl.ds(k, 1), :], (tok, tok)).T
        x_val = x_ref[:, lanes_at(k)].astype(F32) * factor
        xv[k] = x_val
        rolled, cum_cols, cum = enter_of(par, k)
        step_cols = [jnp.broadcast_to(rolled[:, step_at + i:step_at + i + 1], (tok, tok)) for i in range(2)]
        step = jnp.where(lane_a, step_cols[0], step_cols[1])
        exit_w = jnp.exp(cum[tok - 1:tok, :] - cum) * last[...]
        step_s[k] = step
        exit_s[k] = exit_w
        xs_two = jnp.concatenate(split(exit_w * (step * x_val)), axis=0)
        xs_s[k] = xs_two
        own_state = mm(turned[2], xs_two, PLAIN)
        loc[k, 2] = own_state
        g_val = gg[par, k]
        ge_s[par, k] = jnp.concatenate(split(enter_s[par, k] * g_val), axis=0)
        g_two = jnp.concatenate(
            [jnp.where(lane_a, g_val, 0.0), jnp.where(lane_a, 0.0, g_val)], axis=0
        ).astype(BF16)
        scores = mm(x_val.astype(BF16), g_two, ROWS)
        mask = same[...] > 0.5
        kern_own = kern[...]
        total, highs, lows, flows = None, [], [], []
        for i in range(2):
            gap = row_of(par, 2 * k + i) - cum_cols[i]
            decay = jnp.exp(jnp.where(mask, gap, -1e30))
            part = scores[:, i * tok:(i + 1) * tok] * (decay * step_cols[i])
            high, low = split(decay * kern_own)
            highs.append(high)
            lows.append(low)
            flow = part * kern_own
            flows.append(flow)
            total = part if total is None else total + part
            ct[pl.ds(2 * k + i, 1), :] = jnp.sum(flow, axis=0, keepdims=True)
        kg[...] += total
        kept = ctf[...]
        for i in range(2):
            kept = jnp.where(t_lane == 2 * k + i, jnp.sum(flows[i], axis=1, keepdims=True), kept)
        ctf[...] = kept
        inner_s[k] = mm(
            jnp.concatenate(highs + lows, axis=1), jnp.concatenate([g_two, g_two], axis=0), PLAIN
        )
        skp[pl.ds(k, 1), :] = jnp.sum(g_val * x_val, axis=0, keepdims=True)

    def local_part(k):
        enter_of(oth, k)
        loc[k, 0] = jnp.where(par == 0, decay_of(1, k), 1.0) * loc[k, 2]
        ge_s[oth, k] = jnp.concatenate(split(enter_s[oth, k] * gg[oth, k]), axis=0)
        grads = [mm(turned[q], ge_s[q, k], PLAIN) for q in range(2)]
        loc[k, 1] = decay_of(0, k) * grads[1] + grads[0]
        loc[k, 3] = grads[1]

    def forward_part(k):
        @pl.when(z > 0)
        def _():
            e_copy(k).wait_recv()

        @pl.when(z < zs - 1)
        def _():
            es[k] = (decay_of(0, k) * decay_of(1, k)) * er[k] + loc[k, 0]
            e_copy(k).start()

    def backward_part(k):
        @pl.when(z < zs - 1)
        def _():
            r_copy(k).wait_recv()

        @pl.when(z > 0)
        def _():
            rs_[k] = (decay_of(0, k) * decay_of(1, k)) * rr[k] + loc[k, 1]
            r_copy(k).start()

    def wide(a):
        return jnp.concatenate([a[0:tok], a[tok:2 * tok]], axis=1)

    def corner(state):
        high, low = split(state.T)
        both = jnp.concatenate([high, low], axis=1)
        return jnp.concatenate([both, both], axis=0)

    def final_part(k):
        entry0, exit1 = er[k], rr[k]
        entry1 = decay_of(0, k) * entry0 + jnp.where(par == 0, loc[k, 2], 0.0)
        exit0 = decay_of(1, k) * exit1 + loc[k, 3]
        early = par == 0
        entry_own, entry_oth = jnp.where(early, entry0, entry1), jnp.where(early, entry1, entry0)
        leave_own, leave_oth = jnp.where(early, exit0, exit1), jnp.where(early, exit1, exit0)

        def entering(q, entry):
            high, low = split(entry)
            read = mm(twice[q], jnp.concatenate([high, low], axis=0), PLAIN)
            cx[q] += mm(wide(ge_s[q, k]), corner(entry), PLAIN)
            return (enter_s[q, k] * gg[q, k]) * read

        def place(cols_ref, q, full):
            kept = cols_ref[q]
            for i in range(2):
                part = jnp.where(lane_a if i == 0 else ~lane_a, full, 0.0)
                part_sum = jnp.sum(part, axis=1, keepdims=True)
                kept = kept + jnp.where(t_lane == 2 * k + i, part_sum, 0.0)
            cols_ref[q] = kept

        through = entering(oth, entry_oth)
        place(ctc, oth, through)
        ends[oth, pl.ds(k, 1), :] = jnp.sum(leave_oth * entry_oth, axis=0, keepdims=True) * decay_of(oth, k)

        x_val, g_val = xv[k], gg[par, k]
        exit_w, step = exit_s[k], step_s[k]
        l_high, l_low = split(leave_own)
        back = mm(twice[2], jnp.concatenate([l_high, l_low], axis=0), PLAIN)
        bx[...] += mm(wide(xs_s[k]), corner(leave_own), PLAIN)
        back_w = exit_w * back
        input_total = inner_s[k] + back_w
        exit_terms = (step * x_val) * back_w
        place(ctc, par, entering(par, entry_own) - exit_terms)
        place(sgc, 0, input_total * x_val)
        ends[par, pl.ds(k, 1), :] = (
            jnp.sum(exit_terms, axis=0, keepdims=True)
            + jnp.sum(leave_own * entry_own, axis=0, keepdims=True) * decay_of(par, k)
        )
        skip_rows = [skips[pl.ds(2 * k + i, 1), :] for i in range(2)]
        skip_lanes = jnp.where(lane_a[0:1], skip_rows[0], skip_rows[1])
        gx_out[:, lanes_at(k)] = (input_total * step + skip_lanes * g_val).astype(BF16)

    own_part(0)
    meta_copy(oth).wait_recv()
    c_copy(oth).wait_recv()
    prepare(oth, jnp.zeros((tok - heads - 8, tok), F32))
    delay = 1 + LAG * (zs - 1)

    def lap(i, carry):
        @pl.when(i < npair)
        def _():
            g_copy(oth, i).wait_recv()

        ahead = i - 1 - LAG * z

        @pl.when((ahead >= 0) & (ahead < npair))
        def _():
            forward_part(ahead)

        behind = i - 1 - LAG * (zs - 1 - z)

        @pl.when((behind >= 0) & (behind < npair))
        def _():
            backward_part(behind)

        @pl.when((i < npair - 1) & (i >= delay))
        def _():
            final_part(i - delay)
            local_part(i)
            own_part(i + 1)

        @pl.when((i < npair - 1) & (i < delay))
        def _():
            local_part(i)
            own_part(i + 1)

        @pl.when(i == npair - 1)
        def _():
            local_part(i)
            kg_b[...] = mm2(kg[...], c_ref[...], PLAIN)
            kg_c[...] = mm2(kg[...], b_ref[...], COLS)

        @pl.when((i >= npair - 1) & (i >= delay))
        def _():
            final_part(i - delay)

        return carry

    lax.fori_loop(0, npair + delay, lap, 0)

    def folded(a):
        return a[:, 0:tok] + a[:, tok:]

    piece = tok // nhead
    state = b_ref.shape[1]
    oth_out[...] = folded(cx[oth]).reshape(nhead, piece, state)

    def oth_copy(to, slot):
        return remote(oth_out.at[to], red_oth.at[slot], oth_send.at[to], oth_recv.at[slot], (partner, to))

    def own_copy(to, slot):
        return remote(own_out.at[to], red_own.at[slot], own_send.at[to], own_recv.at[slot], (me, to))

    for j in range(nhead):
        oth_copy(lax.rem(hd + j, nhead), hd).start()

    h_sub = lax.broadcasted_iota(jnp.int32, (heads, tok), 0)
    h_lane = lax.broadcasted_iota(jnp.int32, (heads, tok), 1)
    pick = lax.div(h_lane, HEAD_DIM) == lax.rem(h_sub, 2)

    def cumul_of(q):
        per_head = jnp.broadcast_to(ends[q][:, None, :], (npair, 2, tok)).reshape(heads, tok)
        ending = jnp.sum(jnp.where(pick, per_head, 0.0), axis=1, keepdims=True)
        return ctc[q].T[0:heads] + jnp.where(h_lane == tok - 1, ending, 0.0)

    far[...] = cumul_of(oth)
    far_copy = remote(far, near, far_sems.at[0], far_sems.at[1], across)
    far_copy.start()

    own_out[:, 0] = (kg_b[...] + folded(bx[...])).reshape(nhead, piece, state)
    own_out[:, 1] = (kg_c[...] + folded(cx[par])).reshape(nhead, piece, state)
    for j in range(1, nhead):
        own_copy(lax.rem(hd + j, nhead), hd).start()

    mine = ct[...] - ctf[...].T[0:heads] + cumul_of(par)
    lower = (t_sub >= t_lane).astype(F32)
    far_copy.wait_recv()
    decay_grad = lax.dot_general(
        mine + near[...], lower, (PLAIN, ((), ())), precision=HIGHEST, preferred_element_type=F32
    )
    step_all = steps[...]
    alog_sum = -jnp.sum(decay_grad * step_all * rates[...], axis=1, keepdims=True)
    alog_row = jnp.sum(jnp.where(h_sub == h_lane, alog_sum, 0.0), axis=0, keepdims=True)
    skip_all = skp[...]
    skip_a = jnp.sum(skip_all[:, 0:HEAD_DIM], axis=1, keepdims=True)
    skip_b = jnp.sum(skip_all[:, HEAD_DIM:], axis=1, keepdims=True)
    k_sub, k_lane = 2 * h_sub[0:npair], h_lane[0:npair]
    skip_row = jnp.sum(
        jnp.where(k_sub == k_lane, skip_a, 0.0) + jnp.where(k_sub + 1 == k_lane, skip_b, 0.0),
        axis=0, keepdims=True,
    )
    r_sub = lax.broadcasted_iota(jnp.int32, (8, tok), 0)
    hgp[me] = jnp.where(r_sub == 0, alog_row, jnp.where(r_sub == 1, skip_row, 0.0))

    def hg_copy(to, slot):
        return remote(hgp.at[slot], hgp.at[slot], hg_send.at[to], hg_recv.at[slot], (to, hd))

    for j in range(1, nseq):
        hg_copy(lax.rem(me + j, nseq), me).start()

    red_own[hd] = own_out[hd]
    for j in range(nhead):
        other = lax.rem(hd + j, nhead)
        oth_copy(other, other).wait_recv()
    for j in range(1, nhead):
        other = lax.rem(hd + j, nhead)
        own_copy(other, other).wait_recv()
    b_c = jnp.sum(red_own[...], axis=0)
    gat[hd, 0] = b_c[0]
    gat[hd, 1] = b_c[1] + jnp.sum(red_oth[...], axis=0)

    def gat_copy(to, slot):
        return remote(gat.at[slot], gat.at[slot], gat_send.at[to], gat_recv.at[slot], (me, to))

    for j in range(1, nhead):
        gat_copy(lax.rem(hd + j, nhead), hd).start()

    sigmoid = 1.0 / (1.0 + jnp.exp(-(dt_ref[...].astype(F32) + bias)))
    dt_out[...] = (sgc[0].T[0:heads] - rates[...] * decay_grad) * sigmoid
    for j in range(1, nseq):
        other = lax.rem(me + j, nseq)
        hg_copy(other, other).wait_recv()
    hg_out[...] = jnp.sum(hgp[...], axis=0)[0:2, 0:heads] * norm
    for j in range(1, nhead):
        other = lax.rem(hd + j, nhead)
        gat_copy(other, other).wait_recv()
    for i in range(2):
        bc_out[i] = gat[:, i].reshape(tok, state)

    meta_copy(par).wait_send()
    c_copy(par).wait_send()
    far_copy.wait_send()

    def drain(k, carry):
        g_copy(par, k).wait_send()

        @pl.when(z < zs - 1)
        def _():
            e_copy(k).wait_send()

        @pl.when(z > 0)
        def _():
            r_copy(k).wait_send()

        return carry

    lax.fori_loop(0, npair, drain, 0)
    for j in range(nhead):
        oth_copy(lax.rem(hd + j, nhead), hd).wait_send()
    for j in range(1, nhead):
        own_copy(lax.rem(hd + j, nhead), hd).wait_send()
        gat_copy(lax.rem(hd + j, nhead), hd).wait_send()
    for j in range(1, nseq):
        hg_copy(lax.rem(me + j, nseq), me).wait_send()


def publish(g_src, b_src, d_src, h_src, g_dst, b_dst, d_dst, h_dst, g_mid, b_mid, d_mid, h_mid, arrive, leave):
    rows = g_src.shape[0] // 2
    triples = [(g_src.at[pl.ds(i * rows, rows)], g_mid.at[pl.ds(i * rows, rows)], g_dst.at[pl.ds(i * rows, rows)])
               for i in range(2)]
    triples += [(b_src, b_mid, b_dst), (d_src, d_mid, d_dst), (h_src, h_mid, h_dst)]
    first = [pltpu.make_async_copy(a, b, arrive.at[i]) for i, (a, b, c) in enumerate(triples)]
    second = [pltpu.make_async_copy(b, c, leave.at[i]) for i, (a, b, c) in enumerate(triples)]
    for copy in first:
        copy.start()
    for one, two in zip(first, second):
        one.wait()
        two.start()
    for copy in second:
        copy.wait()


def local(
    x_quant, scale_exp, dt_raw, dt_bias, a_log, skip_weight, b_proj, c_proj, doc_starts, grad_out
):
    nseq, nhead = lax.axis_size("seq"), lax.axis_size("head")
    tok, channels = x_quant.shape
    heads = dt_raw.shape[0]
    state = b_proj.shape[1]
    npair, piece = heads // 2, tok // nhead
    norm = 1.0 / math.sqrt(tok * nseq * HEAD_DIM)
    vmem = lambda *shape: pltpu.VMEM(shape, F32)
    half16 = lambda *shape: pltpu.VMEM(shape, BF16)
    dma = lambda n: pltpu.SemaphoreType.DMA((n,))
    sq = (tok, state)
    scratch = [
        half16(tok, channels), pltpu.VMEM(scale_exp.shape, jnp.int32), half16(heads, tok),
        half16(*sq), half16(*sq), half16(tok, channels),
        vmem(scale_exp.shape[0], tok),
        vmem(heads, tok), vmem(heads, tok), vmem(heads, tok),
        vmem(2, heads + 8, tok), vmem(2, *sq),
        vmem(2, npair, *sq), vmem(npair, *sq),
        vmem(*sq), vmem(*sq), vmem(2, *sq), vmem(*sq), vmem(2, *sq),
        half16(3, tok, 2 * state), half16(3, state, 2 * tok),
        vmem(npair, *sq), vmem(2, npair, *sq), vmem(npair, *sq),
        vmem(npair, *sq),
        half16(npair, 2 * tok, state), half16(2, npair, 2 * tok, state),
        vmem(npair, 4, *sq),
        vmem(npair, *sq), vmem(npair, *sq), vmem(npair, *sq), vmem(npair, *sq),
        vmem(*sq), vmem(tok, 2 * state), vmem(2, tok, 2 * state),
        vmem(2, npair, tok), vmem(npair, tok), vmem(heads, tok), vmem(*sq),
        vmem(2, *sq), vmem(1, *sq), vmem(*sq), vmem(*sq),
        vmem(heads, tok), vmem(heads, tok),
        vmem(nhead, 2, piece, state), vmem(nhead, piece, state),
        vmem(nhead, 2, piece, state), vmem(nhead, piece, state),
        vmem(nhead, 2, piece, state), vmem(nseq, 8, tok),
        dma(6), dma(2), dma(2), dma(npair), dma(npair), dma(npair), dma(npair), dma(npair), dma(npair),
        dma(2), dma(nhead), dma(nhead), dma(nhead), dma(nhead), dma(nhead), dma(nhead),
        dma(nseq), dma(nseq),
    ]
    whole = pl.BlockSpec(memory_space=pltpu.VMEM)
    shapes = (
        jax.ShapeDtypeStruct((tok, channels), BF16),
        jax.ShapeDtypeStruct((heads, tok), F32),
        jax.ShapeDtypeStruct((2, tok, state), F32),
        jax.ShapeDtypeStruct((2, heads), F32),
    )
    outs = pl.pallas_call(
        functools.partial(kernel, nseq, nhead, norm),
        out_shape=shapes,
        in_specs=[pl.BlockSpec(memory_space=pl.ANY)] * 6 + [whole] * 3 + [pl.BlockSpec(memory_space=pltpu.SMEM)],
        out_specs=(whole,) * 4,
        scratch_shapes=scratch,
        compiler_params=pltpu.CompilerParams(
            collective_id=0, has_side_effects=True, vmem_limit_bytes=60 << 20
        ),
    )(
        x_quant, scale_exp, dt_raw, b_proj, c_proj, grad_out, dt_bias.reshape(1, heads),
        a_log.reshape(1, heads), skip_weight.reshape(1, heads), doc_starts,
    )
    anywhere = pl.BlockSpec(memory_space=pl.ANY)
    order = (0, 2, 1, 3)
    given = pl.pallas_call(
        publish,
        out_shape=tuple(shapes[i] for i in order),
        in_specs=[anywhere] * 4,
        out_specs=(anywhere,) * 4,
        scratch_shapes=[pltpu.VMEM(shapes[i].shape, shapes[i].dtype) for i in order] + [dma(5), dma(5)],
        compiler_params=pltpu.CompilerParams(vmem_limit_bytes=60 << 20),
    )(*(outs[i] for i in order))
    return tuple(given[i] for i in order)


def solution(mesh):
    in_specs = (
        P("seq", "head"),
        P("head", "seq"),
        P("head", "seq"),
        P("head"),
        P("head"),
        P("head"),
        P("seq", None),
        P("seq", None),
        P("seq", None),
        P("seq", "head"),
    )
    out_specs = (P("seq", "head"), P("head", "seq"), P(None, "seq", None), P(None, "head"))
    return jax.shard_map(local, mesh=mesh, in_specs=in_specs, out_specs=out_specs, check_vma=False)
```

```python
import functools
import math

import jax
import jax.numpy as jnp
from jax import lax
from jax.experimental import pallas as pl
from jax.experimental.pallas import tpu as pltpu
from jax.sharding import PartitionSpec as P

HEAD_DIM = 64
LAG = 2
MESH = pl.DeviceIdType.MESH
F32 = jnp.float32
BF16 = jnp.bfloat16
HIGHEST = lax.Precision.HIGHEST

ROWS = ((1,), (1,))
COLS = ((0,), (0,))
PLAIN = ((1,), (0,))


def mm(a, b, dims):
    return lax.dot_general(a, b, (dims, ((), ())), preferred_element_type=F32)


def split(a):
    high = a.astype(BF16)
    return high, (a - high.astype(F32)).astype(BF16)


def mm2(a, b, dims):
    high, low = split(a)
    return mm(high, b, dims) + mm(low, b, dims)


def mm2r(a, b, dims):
    high, low = split(b)
    return mm(a, high, dims) + mm(a, low, dims)


def kernel(
    nseq, nhead, norm,
    x_hbm, sc_hbm, dt_hbm, b_hbm, c_hbm, g_hbm, bias_ref, alog_ref, skip_ref, doc_ref,
    gx_out, dt_out, bc_out, hg_out,
    x_ref, sc_ref, dt_ref, b_ref, c_ref, g_ref,
    fac, steps, rates, skips, meta, cf, gg, xv, kern, same, first, last, cols,
    twice, turned, step_s, enter_s, exit_s, inner_s, xs_s, ge_s, loc, es, rs_, er, rr,
    kg, bx, cx, ends, skp, ct, ctf, ctc, sgc, kg_b, kg_c, far, near, own_out, oth_out, red_own, red_oth, gat, hgp,
    in_sems, c_sems, meta_sems, g_send, g_recv, e_send, e_recv, r_send, r_recv, far_sems,
    own_send, own_recv, oth_send, oth_recv, gat_send, gat_recv, hg_send, hg_recv,
):
    me, hd = lax.axis_index("seq"), lax.axis_index("head")
    par, z = lax.rem(me, 2), lax.div(me, 2)
    zs = nseq // 2
    oth = 1 - par
    partner = me + 1 - 2 * par
    tok = x_ref.shape[0]
    heads = dt_ref.shape[0]
    npair = heads // 2
    step_at = heads + 8

    fetches = [
        pltpu.make_async_copy(src, dst, in_sems.at[i])
        for i, (src, dst) in enumerate((
            (c_hbm, c_ref), (dt_hbm, dt_ref), (g_hbm, g_ref), (sc_hbm, sc_ref), (b_hbm, b_ref), (x_hbm, x_ref),
        ))
    ]
    for fetch in fetches:
        fetch.start()
    barrier = pltpu.get_barrier_semaphore()
    for j in range(1, nseq):
        pl.semaphore_signal(barrier, inc=1, device_id=(lax.rem(me + j, nseq), hd), device_id_type=MESH)
    for j in range(1, nhead):
        there = lax.rem(hd + j, nhead)
        pl.semaphore_signal(barrier, inc=1, device_id=(me, there), device_id_type=MESH)
        pl.semaphore_signal(barrier, inc=1, device_id=(partner, there), device_id_type=MESH)

    def remote(src, dst, send, recv, device):
        return pltpu.make_async_remote_copy(
            src_ref=src, dst_ref=dst, send_sem=send, recv_sem=recv,
            device_id=device, device_id_type=MESH,
        )

    across = (partner, hd)

    def c_copy(slab):
        return remote(cf.at[slab], cf.at[slab], c_sems.at[0], c_sems.at[1], across)

    def meta_copy(slab):
        return remote(meta.at[slab], meta.at[slab], meta_sems.at[0], meta_sems.at[1], across)

    def g_copy(slab, k):
        return remote(gg.at[slab, k], gg.at[slab, k], g_send.at[k], g_recv.at[k], across)

    def e_copy(k):
        return remote(es.at[k], er.at[k], e_send.at[k], e_recv.at[k], (lax.rem(me + 2, nseq), hd))

    def r_copy(k):
        return remote(rs_.at[k], rr.at[k], r_send.at[k], r_recv.at[k], (lax.rem(me + nseq - 2, nseq), hd))

    sub = lax.broadcasted_iota(jnp.int32, (heads, heads), 0)
    lane = lax.broadcasted_iota(jnp.int32, (heads, heads), 1)

    def column(ref):
        return jnp.sum(jnp.where(sub == lane, ref[...], 0.0), axis=1, keepdims=True)

    t_sub = lax.broadcasted_iota(jnp.int32, (tok, tok), 0)
    t_lane = lax.broadcasted_iota(jnp.int32, (tok, tok), 1)
    lane_a = t_lane < HEAD_DIM
    rate = jnp.exp(column(alog_ref))
    rates[...] = jnp.broadcast_to(rate, (heads, tok))
    skips[...] = jnp.broadcast_to(column(skip_ref), (heads, tok))
    row_id = lax.broadcasted_iota(jnp.int32, (8, tok), 1)
    count = jnp.zeros((8, tok), F32)
    for j in range(doc_ref.shape[1]):
        count = count + (row_id >= doc_ref[0, j]).astype(F32)
    bias = column(bias_ref)
    fetches[0].wait()
    cf[par] = c_ref[...].astype(F32)
    fetches[1].wait()
    pre = dt_ref[...].astype(F32) + bias
    step_all = jnp.maximum(pre, 0.0) + jnp.log1p(jnp.exp(-jnp.abs(pre)))
    steps[...] = step_all
    upper = (t_sub <= t_lane).astype(F32)
    meta[par, 0:heads] = lax.dot_general(
        -rate * step_all, upper, (PLAIN, ((), ())), precision=HIGHEST, preferred_element_type=F32
    )
    meta[par, heads:heads + 8] = count
    fetches[2].wait()

    pl.semaphore_wait(barrier, nseq - 1 + 2 * (nhead - 1))
    meta_copy(par).start()
    c_copy(par).start()

    def lanes_at(k):
        return pl.ds(pl.multiple_of(k * tok, tok), tok)

    def send_pair(k, carry):
        gg[par, k] = g_ref[:, lanes_at(k)].astype(F32)
        g_copy(par, k).start()
        return carry

    lax.fori_loop(0, npair, send_pair, 0)
    for fetch in fetches[3:]:
        fetch.wait()
    fac[...] = jnp.left_shift(jnp.int32(1), sc_ref[...] + 8).astype(F32) / 256.0
    kg[...] = jnp.zeros_like(kg)
    bx[...] = jnp.zeros_like(bx)
    cx[...] = jnp.zeros_like(cx)
    ctc[...] = jnp.zeros_like(ctc)
    ctf[...] = jnp.zeros_like(ctf)
    sgc[...] = jnp.zeros_like(sgc)

    @pl.when(z == 0)
    def _():
        er[...] = jnp.zeros_like(er)

    @pl.when(z == zs - 1)
    def _():
        rr[...] = jnp.zeros_like(rr)

    def row_of(q, row):
        return meta[q, pl.ds(row, 1), :]

    def prepare(q, rest):
        rows = jnp.concatenate([meta[q], rest], axis=0)
        flat = rows.T
        cols[q] = flat
        seg_col = jnp.broadcast_to(flat[:, heads:heads + 1], (tok, tok))
        first[q] = (seg_col == 0.0).astype(F32)
        whole = cf[q].astype(BF16)
        c_flat = cf[q].T.astype(BF16)
        twice[q] = jnp.concatenate([whole, whole], axis=1)
        turned[q] = jnp.concatenate([c_flat, c_flat], axis=1)
        return seg_col

    def enter_of(q, k):
        rolled = pltpu.roll(cols[q], lax.rem(tok - 2 * k, tok), 1)
        cum_cols = [jnp.broadcast_to(rolled[:, i:i + 1], (tok, tok)) for i in range(2)]
        cum = jnp.where(lane_a, cum_cols[0], cum_cols[1])
        enter_s[q, k] = jnp.exp(cum) * first[q]
        return rolled, cum_cols, cum

    seg_own = prepare(par, jnp.concatenate([steps[...], jnp.zeros((tok - 2 * heads - 8, tok), F32)], axis=0))
    seg_row = jnp.broadcast_to(meta[par, heads:heads + 1, :], (tok, tok))
    same[...] = ((t_sub <= t_lane) & (seg_row == seg_own)).astype(F32)
    last[...] = (seg_own == meta[par, heads:heads + 1, tok - 1:tok]).astype(F32)
    b_own = b_ref[...]
    b_flat = b_own.astype(F32).T.astype(BF16)
    twice[2] = jnp.concatenate([b_own, b_own], axis=1)
    turned[2] = jnp.concatenate([b_flat, b_flat], axis=1)
    kern[...] = mm(b_own, c_ref[...], ROWS)

    def decay_of(q, k):
        return enter_s[q, k, tok - 1:tok, :]

    def own_part(k):
        factor = jnp.broadcast_to(fac[pl.ds(k, 1), :], (tok, tok)).T
        x_val = x_ref[:, lanes_at(k)].astype(F32) * factor
        xv[k] = x_val
        rolled, cum_cols, cum = enter_of(par, k)
        step_cols = [jnp.broadcast_to(rolled[:, step_at + i:step_at + i + 1], (tok, tok)) for i in range(2)]
        step = jnp.where(lane_a, step_cols[0], step_cols[1])
        exit_w = jnp.exp(cum[tok - 1:tok, :] - cum) * last[...]
        step_s[k] = step
        exit_s[k] = exit_w
        xs_two = jnp.concatenate(split(exit_w * (step * x_val)), axis=0)
        xs_s[k] = xs_two
        own_state = mm(turned[2], xs_two, PLAIN)
        loc[k, 2] = own_state
        g_val = gg[par, k]
        ge_s[par, k] = jnp.concatenate(split(enter_s[par, k] * g_val), axis=0)
        g_two = jnp.concatenate(
            [jnp.where(lane_a, g_val, 0.0), jnp.where(lane_a, 0.0, g_val)], axis=0
        ).astype(BF16)
        scores = mm(x_val.astype(BF16), g_two, ROWS)
        mask = same[...] > 0.5
        kern_own = kern[...]
        total, highs, lows, flows = None, [], [], []
        for i in range(2):
            gap = row_of(par, 2 * k + i) - cum_cols[i]
            decay = jnp.exp(jnp.where(mask, gap, -1e30))
            part = scores[:, i * tok:(i + 1) * tok] * (decay * step_cols[i])
            high, low = split(decay * kern_own)
            highs.append(high)
            lows.append(low)
            flow = part * kern_own
            flows.append(flow)
            total = part if total is None else total + part
            ct[pl.ds(2 * k + i, 1), :] = jnp.sum(flow, axis=0, keepdims=True)
        kg[...] += total
        kept = ctf[...]
        for i in range(2):
            kept = jnp.where(t_lane == 2 * k + i, jnp.sum(flows[i], axis=1, keepdims=True), kept)
        ctf[...] = kept
        inner_s[k] = mm(
            jnp.concatenate(highs + lows, axis=1), jnp.concatenate([g_two, g_two], axis=0), PLAIN
        )
        skp[pl.ds(k, 1), :] = jnp.sum(g_val * x_val, axis=0, keepdims=True)

    def local_part(k):
        enter_of(oth, k)
        loc[k, 0] = jnp.where(par == 0, decay_of(1, k), 1.0) * loc[k, 2]
        ge_s[oth, k] = jnp.concatenate(split(enter_s[oth, k] * gg[oth, k]), axis=0)
        grads = [mm(turned[q], ge_s[q, k], PLAIN) for q in range(2)]
        loc[k, 1] = decay_of(0, k) * grads[1] + grads[0]
        loc[k, 3] = grads[1]

    def forward_part(k):
        @pl.when(z > 0)
        def _():
            e_copy(k).wait_recv()

        @pl.when(z < zs - 1)
        def _():
            es[k] = (decay_of(0, k) * decay_of(1, k)) * er[k] + loc[k, 0]
            e_copy(k).start()

    def backward_part(k):
        @pl.when(z < zs - 1)
        def _():
            r_copy(k).wait_recv()

        @pl.when(z > 0)
        def _():
            rs_[k] = (decay_of(0, k) * decay_of(1, k)) * rr[k] + loc[k, 1]
            r_copy(k).start()

    def wide(a):
        return jnp.concatenate([a[0:tok], a[tok:2 * tok]], axis=1)

    def corner(state):
        high, low = split(state.T)
        both = jnp.concatenate([high, low], axis=1)
        return jnp.concatenate([both, both], axis=0)

    def final_part(k):
        entry0, exit1 = er[k], rr[k]
        entry1 = decay_of(0, k) * entry0 + jnp.where(par == 0, loc[k, 2], 0.0)
        exit0 = decay_of(1, k) * exit1 + loc[k, 3]
        early = par == 0
        entry_own, entry_oth = jnp.where(early, entry0, entry1), jnp.where(early, entry1, entry0)
        leave_own, leave_oth = jnp.where(early, exit0, exit1), jnp.where(early, exit1, exit0)

        def entering(q, entry):
            high, low = split(entry)
            read = mm(twice[q], jnp.concatenate([high, low], axis=0), PLAIN)
            cx[q] += mm(wide(ge_s[q, k]), corner(entry), PLAIN)
            return (enter_s[q, k] * gg[q, k]) * read

        def place(cols_ref, q, full):
            kept = cols_ref[q]
            for i in range(2):
                part = jnp.where(lane_a if i == 0 else ~lane_a, full, 0.0)
                part_sum = jnp.sum(part, axis=1, keepdims=True)
                kept = kept + jnp.where(t_lane == 2 * k + i, part_sum, 0.0)
            cols_ref[q] = kept

        through = entering(oth, entry_oth)
        place(ctc, oth, through)
        ends[oth, pl.ds(k, 1), :] = jnp.sum(leave_oth * entry_oth, axis=0, keepdims=True) * decay_of(oth, k)

        x_val, g_val = xv[k], gg[par, k]
        exit_w, step = exit_s[k], step_s[k]
        l_high, l_low = split(leave_own)
        back = mm(twice[2], jnp.concatenate([l_high, l_low], axis=0), PLAIN)
        bx[...] += mm(wide(xs_s[k]), corner(leave_own), PLAIN)
        back_w = exit_w * back
        input_total = inner_s[k] + back_w
        exit_terms = (step * x_val) * back_w
        place(ctc, par, entering(par, entry_own) - exit_terms)
        place(sgc, 0, input_total * x_val)
        ends[par, pl.ds(k, 1), :] = (
            jnp.sum(exit_terms, axis=0, keepdims=True)
            + jnp.sum(leave_own * entry_own, axis=0, keepdims=True) * decay_of(par, k)
        )
        skip_rows = [skips[pl.ds(2 * k + i, 1), :] for i in range(2)]
        skip_lanes = jnp.where(lane_a[0:1], skip_rows[0], skip_rows[1])
        gx_out[:, lanes_at(k)] = (input_total * step + skip_lanes * g_val).astype(BF16)

    own_part(0)
    meta_copy(oth).wait_recv()
    c_copy(oth).wait_recv()
    prepare(oth, jnp.zeros((tok - heads - 8, tok), F32))
    delay = 1 + LAG * (zs - 1)

    def lap(i, carry):
        @pl.when(i < npair)
        def _():
            g_copy(oth, i).wait_recv()

        ahead = i - 1 - LAG * z

        @pl.when((ahead >= 0) & (ahead < npair))
        def _():
            forward_part(ahead)

        behind = i - 1 - LAG * (zs - 1 - z)

        @pl.when((behind >= 0) & (behind < npair))
        def _():
            backward_part(behind)

        @pl.when((i < npair - 1) & (i >= delay))
        def _():
            final_part(i - delay)
            local_part(i)
            own_part(i + 1)

        @pl.when((i < npair - 1) & (i < delay))
        def _():
            local_part(i)
            own_part(i + 1)

        @pl.when(i == npair - 1)
        def _():
            local_part(i)
            kg_b[...] = mm2(kg[...], c_ref[...], PLAIN)
            kg_c[...] = mm2(kg[...], b_ref[...], COLS)

        @pl.when((i >= npair - 1) & (i >= delay))
        def _():
            final_part(i - delay)

        return carry

    lax.fori_loop(0, npair + delay, lap, 0)

    def folded(a):
        return a[:, 0:tok] + a[:, tok:]

    piece = tok // nhead
    state = b_ref.shape[1]
    oth_out[...] = folded(cx[oth]).reshape(nhead, piece, state)

    def oth_copy(to, slot):
        return remote(oth_out.at[to], red_oth.at[slot], oth_send.at[to], oth_recv.at[slot], (partner, to))

    def own_copy(to, slot):
        return remote(own_out.at[to], red_own.at[slot], own_send.at[to], own_recv.at[slot], (me, to))

    for j in range(nhead):
        oth_copy(lax.rem(hd + j, nhead), hd).start()

    h_sub = lax.broadcasted_iota(jnp.int32, (heads, tok), 0)
    h_lane = lax.broadcasted_iota(jnp.int32, (heads, tok), 1)
    pick = lax.div(h_lane, HEAD_DIM) == lax.rem(h_sub, 2)

    def cumul_of(q):
        per_head = jnp.broadcast_to(ends[q][:, None, :], (npair, 2, tok)).reshape(heads, tok)
        ending = jnp.sum(jnp.where(pick, per_head, 0.0), axis=1, keepdims=True)
        return ctc[q].T[0:heads] + jnp.where(h_lane == tok - 1, ending, 0.0)

    far[...] = cumul_of(oth)
    far_copy = remote(far, near, far_sems.at[0], far_sems.at[1], across)
    far_copy.start()

    own_out[:, 0] = (kg_b[...] + folded(bx[...])).reshape(nhead, piece, state)
    own_out[:, 1] = (kg_c[...] + folded(cx[par])).reshape(nhead, piece, state)
    for j in range(1, nhead):
        own_copy(lax.rem(hd + j, nhead), hd).start()

    mine = ct[...] - ctf[...].T[0:heads] + cumul_of(par)
    lower = (t_sub >= t_lane).astype(F32)
    far_copy.wait_recv()
    decay_grad = lax.dot_general(
        mine + near[...], lower, (PLAIN, ((), ())), precision=HIGHEST, preferred_element_type=F32
    )
    step_all = steps[...]
    alog_sum = -jnp.sum(decay_grad * step_all * rates[...], axis=1, keepdims=True)
    alog_row = jnp.sum(jnp.where(h_sub == h_lane, alog_sum, 0.0), axis=0, keepdims=True)
    skip_all = skp[...]
    skip_a = jnp.sum(skip_all[:, 0:HEAD_DIM], axis=1, keepdims=True)
    skip_b = jnp.sum(skip_all[:, HEAD_DIM:], axis=1, keepdims=True)
    k_sub, k_lane = 2 * h_sub[0:npair], h_lane[0:npair]
    skip_row = jnp.sum(
        jnp.where(k_sub == k_lane, skip_a, 0.0) + jnp.where(k_sub + 1 == k_lane, skip_b, 0.0),
        axis=0, keepdims=True,
    )
    r_sub = lax.broadcasted_iota(jnp.int32, (8, tok), 0)
    hgp[me] = jnp.where(r_sub == 0, alog_row, jnp.where(r_sub == 1, skip_row, 0.0))

    def hg_copy(to, slot):
        return remote(hgp.at[slot], hgp.at[slot], hg_send.at[to], hg_recv.at[slot], (to, hd))

    for j in range(1, nseq):
        hg_copy(lax.rem(me + j, nseq), me).start()

    red_own[hd] = own_out[hd]
    for j in range(nhead):
        other = lax.rem(hd + j, nhead)
        oth_copy(other, other).wait_recv()
    for j in range(1, nhead):
        other = lax.rem(hd + j, nhead)
        own_copy(other, other).wait_recv()
    b_c = jnp.sum(red_own[...], axis=0)
    gat[hd, 0] = b_c[0]
    gat[hd, 1] = b_c[1] + jnp.sum(red_oth[...], axis=0)

    def gat_copy(to, slot):
        return remote(gat.at[slot], gat.at[slot], gat_send.at[to], gat_recv.at[slot], (me, to))

    for j in range(1, nhead):
        gat_copy(lax.rem(hd + j, nhead), hd).start()

    sigmoid = 1.0 / (1.0 + jnp.exp(-(dt_ref[...].astype(F32) + bias)))
    dt_out[...] = (sgc[0].T[0:heads] - rates[...] * decay_grad) * sigmoid
    for j in range(1, nseq):
        other = lax.rem(me + j, nseq)
        hg_copy(other, other).wait_recv()
    hg_out[...] = jnp.sum(hgp[...], axis=0)[0:2, 0:heads] * norm
    for j in range(1, nhead):
        other = lax.rem(hd + j, nhead)
        gat_copy(other, other).wait_recv()
    for i in range(2):
        bc_out[i] = gat[:, i].reshape(tok, state)

    meta_copy(par).wait_send()
    c_copy(par).wait_send()
    far_copy.wait_send()

    def drain(k, carry):
        g_copy(par, k).wait_send()

        @pl.when(z < zs - 1)
        def _():
            e_copy(k).wait_send()

        @pl.when(z > 0)
        def _():
            r_copy(k).wait_send()

        return carry

    lax.fori_loop(0, npair, drain, 0)
    for j in range(nhead):
        oth_copy(lax.rem(hd + j, nhead), hd).wait_send()
    for j in range(1, nhead):
        own_copy(lax.rem(hd + j, nhead), hd).wait_send()
        gat_copy(lax.rem(hd + j, nhead), hd).wait_send()
    for j in range(1, nseq):
        hg_copy(lax.rem(me + j, nseq), me).wait_send()


def publish(g_src, b_src, d_src, h_src, g_dst, b_dst, d_dst, h_dst, g_mid, b_mid, d_mid, h_mid, arrive, leave):
    rows = g_src.shape[0] // 2
    triples = [(g_src.at[pl.ds(i * rows, rows)], g_mid.at[pl.ds(i * rows, rows)], g_dst.at[pl.ds(i * rows, rows)])
               for i in range(2)]
    triples += [(b_src, b_mid, b_dst), (d_src, d_mid, d_dst), (h_src, h_mid, h_dst)]
    first = [pltpu.make_async_copy(a, b, arrive.at[i]) for i, (a, b, c) in enumerate(triples)]
    second = [pltpu.make_async_copy(b, c, leave.at[i]) for i, (a, b, c) in enumerate(triples)]
    for copy in first:
        copy.start()
    for one, two in zip(first, second):
        one.wait()
        two.start()
    for copy in second:
        copy.wait()


def local(
    x_quant, scale_exp, dt_raw, dt_bias, a_log, skip_weight, b_proj, c_proj, doc_starts, grad_out
):
    nseq, nhead = lax.axis_size("seq"), lax.axis_size("head")
    tok, channels = x_quant.shape
    heads = dt_raw.shape[0]
    state = b_proj.shape[1]
    npair, piece = heads // 2, tok // nhead
    norm = 1.0 / math.sqrt(tok * nseq * HEAD_DIM)
    vmem = lambda *shape: pltpu.VMEM(shape, F32)
    half16 = lambda *shape: pltpu.VMEM(shape, BF16)
    dma = lambda n: pltpu.SemaphoreType.DMA((n,))
    sq = (tok, state)
    scratch = [
        half16(tok, channels), pltpu.VMEM(scale_exp.shape, jnp.int32), half16(heads, tok),
        half16(*sq), half16(*sq), half16(tok, channels),
        vmem(scale_exp.shape[0], tok),
        vmem(heads, tok), vmem(heads, tok), vmem(heads, tok),
        vmem(2, heads + 8, tok), vmem(2, *sq),
        vmem(2, npair, *sq), vmem(npair, *sq),
        vmem(*sq), vmem(*sq), vmem(2, *sq), vmem(*sq), vmem(2, *sq),
        half16(3, tok, 2 * state), half16(3, state, 2 * tok),
        vmem(npair, *sq), vmem(2, npair, *sq), vmem(npair, *sq),
        vmem(npair, *sq),
        half16(npair, 2 * tok, state), half16(2, npair, 2 * tok, state),
        vmem(npair, 4, *sq),
        vmem(npair, *sq), vmem(npair, *sq), vmem(npair, *sq), vmem(npair, *sq),
        vmem(*sq), vmem(tok, 2 * state), vmem(2, tok, 2 * state),
        vmem(2, npair, tok), vmem(npair, tok), vmem(heads, tok), vmem(*sq),
        vmem(2, *sq), vmem(1, *sq), vmem(*sq), vmem(*sq),
        vmem(heads, tok), vmem(heads, tok),
        vmem(nhead, 2, piece, state), vmem(nhead, piece, state),
        vmem(nhead, 2, piece, state), vmem(nhead, piece, state),
        vmem(nhead, 2, piece, state), vmem(nseq, 8, tok),
        dma(6), dma(2), dma(2), dma(npair), dma(npair), dma(npair), dma(npair), dma(npair), dma(npair),
        dma(2), dma(nhead), dma(nhead), dma(nhead), dma(nhead), dma(nhead), dma(nhead),
        dma(nseq), dma(nseq),
    ]
    whole = pl.BlockSpec(memory_space=pltpu.VMEM)
    shapes = (
        jax.ShapeDtypeStruct((tok, channels), BF16),
        jax.ShapeDtypeStruct((heads, tok), F32),
        jax.ShapeDtypeStruct((2, tok, state), F32),
        jax.ShapeDtypeStruct((2, heads), F32),
    )
    outs = pl.pallas_call(
        functools.partial(kernel, nseq, nhead, norm),
        out_shape=shapes,
        in_specs=[pl.BlockSpec(memory_space=pl.ANY)] * 6 + [whole] * 3 + [pl.BlockSpec(memory_space=pltpu.SMEM)],
        out_specs=(whole,) * 4,
        scratch_shapes=scratch,
        compiler_params=pltpu.CompilerParams(
            collective_id=0, has_side_effects=True, vmem_limit_bytes=60 << 20
        ),
    )(
        x_quant, scale_exp, dt_raw, b_proj, c_proj, grad_out, dt_bias.reshape(1, heads),
        a_log.reshape(1, heads), skip_weight.reshape(1, heads), doc_starts,
    )
    anywhere = pl.BlockSpec(memory_space=pl.ANY)
    order = (0, 2, 1, 3)
    given = pl.pallas_call(
        publish,
        out_shape=tuple(shapes[i] for i in order),
        in_specs=[anywhere] * 4,
        out_specs=(anywhere,) * 4,
        scratch_shapes=[pltpu.VMEM(shapes[i].shape, shapes[i].dtype) for i in order] + [dma(5), dma(5)],
        compiler_params=pltpu.CompilerParams(vmem_limit_bytes=60 << 20),
    )(*(outs[i] for i in order))
    return tuple(given[i] for i in order)


def solution(mesh):
    in_specs = (
        P("seq", "head"),
        P("head", "seq"),
        P("head", "seq"),
        P("head"),
        P("head"),
        P("head"),
        P("seq", None),
        P("seq", None),
        P("seq", None),
        P("seq", "head"),
    )
    out_specs = (P("seq", "head"), P("head", "seq"), P(None, "seq", None), P(None, "head"))
    return jax.shard_map(local, mesh=mesh, in_specs=in_specs, out_specs=out_specs, check_vma=False)
```
